256 devices in a mesh: dp: 4 (over x), seq: 64 (over y, z, core).
Axes of the slice: x: 4, y: 4, z: 8, core: 2. Of those that a mesh axis runs over, the one named last changes fastest.
Arguments:
- tokens: bfloat16 [4, 8192, 1152], P('dp', 'seq'), may hold values from -40 to 40
- d_out: bfloat16 [4, 8192, 1152], P('dp', 'seq'), may hold values from -16 to 16
- frames: int32 [4], P('dp'), may hold values from 16 to 32, as said below
- frame_order: int32 [4, 32], P('dp'), may hold values from 0 to 31, each once within a row
- w_qkv: bfloat16 [1152, 3456], replicated, may hold values from -4 to 4
- w_out: bfloat16 [1152, 1152], replicated, may hold values from -0.1875 to 0.1875
Outputs:
- d_tokens: bfloat16 [4, 8192, 1152], P('dp', 'seq')
- d_w_out: float32 [1152, 1152], P('seq', 'dp')
The draws below stay inside these ranges and needn't reach their ends.
Inputs may be any that keep to these rules, and one draw needn't show every extreme that they name: Some clip has 32 frames. `frame_order`: each row holds every number of 0 to 31 once.
All inputs are finite; a program needn't handle non-finite values.
Results may differ from the reference program's by a relative error of at most 0.012.
The reference program's roundings to bfloat16 on the way count: a program that leaves them out, or rounds other values in their place, can miss the bound.
Values may be sent and summed in bfloat16 or wider, within the bound.
No kernel may reach another device: no remote copies, remote signals or barrier semaphores. Data moves between devices by JAX's collectives and lax.ppermute only.
A program may use at most 64 MiB of HBM per device.

```python
import math
import jax
import jax.numpy as jnp
from jax import lax

D = 1152
H = 16
P_SIZE = 256
F_MAX = 32
CLIPS = 1
CLIP_TOTAL = 4
ROWS = 8192
N_DP = 4


def draw_frames(key, part):
    clip_total = N_DP * CLIPS
    counts = jax.random.randint(jax.random.fold_in(key, 11), (clip_total,), F_MAX // 2, F_MAX + 1)
    largest_at = jax.random.randint(jax.random.fold_in(key, 12), (), 0, clip_total)
    return jnp.where(jnp.arange(clip_total) == largest_at, F_MAX, counts).astype(jnp.int32)


def draw_tokens(key, part):
    full_shape = (N_DP * CLIPS, F_MAX, P_SIZE, D)
    row_scales = jnp.exp(jax.random.uniform(jax.random.fold_in(key, 21), (N_DP * CLIPS, F_MAX, P_SIZE, 1), jnp.float32) * jnp.log(10.0))
    gaussian = jnp.clip(jax.random.normal(jax.random.fold_in(key, 23), full_shape, jnp.float32), -4.0, 4.0)
    result = gaussian * row_scales
    return result.reshape(N_DP * CLIPS, F_MAX * P_SIZE, D).astype(jnp.bfloat16)


def draw_w_qkv(key, part):
    matrix = jnp.clip(jax.random.normal(jax.random.fold_in(key, 31), (D, 3 * D), jnp.float32), -4.0, 4.0) * D ** (-0.5)
    return jnp.clip(matrix, -4.0, 4.0).astype(jnp.bfloat16)


def with_spikes(drawn, key, source, target, blocks, factor):
    owner, partner = [(jnp.arange(drawn.shape[dim]) // (drawn.shape[dim] // blocks)).reshape([-1 if axis == dim else 1 for axis in range(drawn.ndim)]) for dim in (source, target)]
    chosen = jax.random.permutation(key, blocks)[partner]
    strong = (owner == chosen) | (owner == (partner + blocks // 2) % blocks)
    return jnp.where(strong, factor * drawn, drawn)


def block_scale(stream_key, extent, shards, least, top_value):
    loudness = 1.0
    for axis_at, shards_of in shards:
        draws = jax.random.uniform(jax.random.fold_in(jax.random.fold_in(stream_key, 6), axis_at), (shards_of,), jnp.float32, least / len(shards), top_value / len(shards))
        loudness = loudness * jnp.repeat(jnp.exp(draws), extent[axis_at] // shards_of).reshape((-1,) + (1,) * (len(extent) - 1 - axis_at))
    return loudness


def bell_draw(own_key, dims, width, bound, split=(), held_as=jnp.bfloat16):
    entries = jax.random.normal(own_key, dims, jnp.float32) * width
    if len(split) > 0:
        entries = block_scale(own_key, dims, split, -0.22, 0.18) * entries
    return jnp.clip(entries, min=-bound, max=bound).astype(held_as)


def heavy_noise(key, dims, scale, reach, cuts, heavy, dtype=jnp.bfloat16):
    entries = scale * jax.random.normal(key, dims, jnp.float32)
    if cuts:
        entries = entries * block_scale(key, dims, cuts, -0.22, 0.18)
    return jnp.clip(with_spikes(entries, jax.random.fold_in(key, 3), *heavy), -reach, reach).astype(dtype)


def setup_inputs(seed: int = 0) -> dict:
    key_of = jax.random.split(jax.random.key(seed), 7)
    tokens = draw_tokens(jax.random.fold_in(key_of[6], 71), 0)
    d_out = heavy_noise(key_of[1], (CLIP_TOTAL, ROWS, D), 1.0, 16.0, ((0, 4), (1, 64)), (1, 2, 64, 4.0))
    frames = draw_frames(jax.random.fold_in(key_of[6], 71), 0)
    frame_order = jax.vmap(lambda own: jax.random.permutation(own, F_MAX))(jax.random.split(key_of[3], CLIP_TOTAL)).reshape((CLIP_TOTAL, F_MAX)).astype(jnp.int32)
    w_qkv = draw_w_qkv(jax.random.fold_in(key_of[6], 71), 0)
    w_out = bell_draw(key_of[5], (D, D), D ** -0.5, 0.1875)
    return dict(tokens=tokens, d_out=d_out, frames=frames, frame_order=frame_order, w_qkv=w_qkv, w_out=w_out)


def layer_stats(tokens):
    values = tokens.astype(jnp.float32)
    center = values - lax.optimization_barrier(jnp.mean(values, axis=-1, keepdims=True))
    spread = lax.optimization_barrier(jnp.mean(center * center, axis=-1, keepdims=True))
    inverse = lax.rsqrt(spread + 1e-06)
    return (center * inverse, inverse)

def attend_forward(queries, keys_in, values, live_slots, score_scale):
    scores = jnp.einsum('ciqhe,cjqhe->cqhij', queries.astype(jnp.float32), keys_in.astype(jnp.float32)) * score_scale
    scores = jnp.where(live_slots[:, None, None, None, :] > 0.5, scores, -1e+30)
    row_max = lax.optimization_barrier(jnp.max(scores, axis=-1, keepdims=True))
    exponent = jnp.exp(scores - row_max)
    softmax_out = exponent / lax.optimization_barrier(jnp.sum(exponent, axis=-1, keepdims=True))
    rounded = softmax_out.astype(jnp.bfloat16)
    attended = jnp.einsum('cqhij,cjqhe->ciqhe', rounded.astype(jnp.float32), values.astype(jnp.float32)).astype(jnp.bfloat16)
    return (softmax_out, rounded, attended)

def attend_backward(queries, keys_in, values, softmax_out, rounded, head_grad, score_scale):
    grad_float = head_grad.astype(jnp.float32)
    d_values = jnp.einsum('cqhij,ciqhe->cjqhe', rounded.astype(jnp.float32), grad_float).astype(jnp.bfloat16)
    prob_grad = jnp.einsum('ciqhe,cjqhe->cqhij', grad_float, values.astype(jnp.float32))
    inner_sum = lax.optimization_barrier(jnp.sum(softmax_out * prob_grad, axis=-1, keepdims=True))
    score_grad = (softmax_out * (prob_grad - inner_sum) * score_scale).astype(jnp.bfloat16)
    score_float = score_grad.astype(jnp.float32)
    d_queries = jnp.einsum('cqhij,cjqhe->ciqhe', score_float, keys_in.astype(jnp.float32)).astype(jnp.bfloat16)
    d_keys = jnp.einsum('cqhij,ciqhe->cjqhe', score_float, queries.astype(jnp.float32)).astype(jnp.bfloat16)
    return (d_queries, d_keys, d_values)

def reference(tokens, d_out, frames, frame_order, w_qkv, w_out):
    head_dim = D // H
    score_scale = 1.0 / math.sqrt(head_dim)
    grad_out = jnp.zeros((D, D), jnp.float32)
    results = []
    for clip_index in range(N_DP * CLIPS):
        live_slots = (frame_order[clip_index] < frames[clip_index]).astype(jnp.float32)
        row_live = jnp.repeat(live_slots, P_SIZE)
        normalized, inverse = layer_stats(tokens[clip_index])
        normed = normalized.astype(jnp.bfloat16)
        joined = jnp.dot(normed, w_qkv, preferred_element_type=jnp.float32).astype(jnp.bfloat16)
        head_grid = joined.reshape(1, F_MAX, P_SIZE, 3, H, head_dim)
        queries = head_grid[:, :, :, 0]
        keys_in = head_grid[:, :, :, 1]
        values = head_grid[:, :, :, 2]
        softmax_out, rounded, attended = attend_forward(queries, keys_in, values, live_slots[None, :], score_scale)
        masked = (d_out[clip_index].astype(jnp.float32) * row_live[:, None]).astype(jnp.bfloat16)
        head_rows = jnp.dot(masked, w_out.T, preferred_element_type=jnp.float32).astype(jnp.bfloat16)
        attended_rows = attended.reshape(F_MAX * P_SIZE, D)
        grad_out = grad_out + jnp.dot(attended_rows.T, masked, preferred_element_type=jnp.float32)
        head_grad = head_rows.reshape(1, F_MAX, P_SIZE, H, head_dim)
        d_queries, d_keys, d_values = attend_backward(queries, keys_in, values, softmax_out, rounded, head_grad, score_scale)
        qkv_grad = jnp.stack((d_queries, d_keys, d_values), axis=3).reshape(F_MAX * P_SIZE, 3 * D)
        normed_grad = jnp.dot(qkv_grad, w_qkv.T, preferred_element_type=jnp.float32)
        mean_grad = lax.optimization_barrier(jnp.mean(normed_grad, axis=-1, keepdims=True))
        mean_cross = lax.optimization_barrier(jnp.mean(normed_grad * normalized, axis=-1, keepdims=True))
        d_rows = masked.astype(jnp.float32) + inverse * (normed_grad - mean_grad - normalized * mean_cross)
        results.append(d_rows.astype(jnp.bfloat16))
    return (jnp.stack(results, axis=0), grad_out)
```

```python
import math

import jax
import jax.numpy as jnp
from jax import lax
from jax.experimental import pallas as pl
from jax.experimental.pallas import tpu as pltpu
from jax.sharding import Mesh, PartitionSpec as P

H = 16
D = 1152
E = D // H
SLOTS = 32
PATCHES = 4
ROWS = SLOTS * PATCHES
SCALE = 1.0 / math.sqrt(E)
BF = jnp.bfloat16
F32 = jnp.float32
MIB = 1024 * 1024
COLS = 288
WIDE = 384
OUT_ROWS = 18
PAD_ROWS = 24

NN = (((1,), (0,)), ((), ()))
NT = (((1,), (1,)), ((), ()))
TN = (((0,), (0,)), ((), ()))


def dot(a, b, dims=NN):
    return lax.dot_general(a, b, dims, preferred_element_type=F32)


def whole():
    return pl.BlockSpec(memory_space=pltpu.VMEM)


def call(kernel, out_shape, inputs, scratch=(), limit=32, flops=0, data=0, smem=()):
    specs = [
        pl.BlockSpec(memory_space=pltpu.SMEM) if i in smem else whole() for i in range(len(inputs))
    ]
    return pl.pallas_call(
        kernel,
        out_shape=out_shape,
        in_specs=specs,
        out_specs=jax.tree.map(lambda _: whole(), out_shape),
        scratch_shapes=list(scratch),
        compiler_params=pltpu.CompilerParams(vmem_limit_bytes=limit * MIB),
        cost_estimate=pl.CostEstimate(flops=flops, bytes_accessed=data, transcendentals=0),
    )(*inputs)


def interleave(rows_first):
    packed = lax.broadcasted_iota(jnp.int32, (256, 256), 0 if rows_first else 1)
    plain = lax.broadcasted_iota(jnp.int32, (256, 256), 1 if rows_first else 0)
    inner = packed % 8
    target = (packed // 8) * 4 + inner % 4 + jnp.where(inner >= 4, 128, 0)
    return (plain == target).astype(F32).astype(BF)


def pack_kernel(tokens_ref, d_out_ref, packed_ref):
    both = jnp.concatenate([tokens_ref[...], d_out_ref[...]], axis=0)
    packed_ref[...] = dot(interleave(True), both).astype(BF)


def row_stats(tokens):
    values = tokens.astype(F32)
    center = values - jnp.mean(values, axis=-1, keepdims=True)
    spread = jnp.mean(center * center, axis=-1, keepdims=True)
    inverse = lax.rsqrt(spread + 1e-06)
    return center * inverse, inverse


def window(head):
    low = head * E
    base = low // 128 * 128
    width = 128 if low + E <= base + 128 else 256
    lane = lax.broadcasted_iota(jnp.int32, (ROWS, width), 1)
    inside = (lane >= low - base) & (lane < low - base + E)
    return base, width, inside


def only(inside, array):
    return jnp.where(inside, array, jnp.zeros_like(array))


def forward_kernel(
    place_ref, packed_ref, live_row_ref, live_col_ref, w_qkv_ref,
    tokens_ref, masked_ref, joined_ref, probs_ref, own_ref, one_ref, two_ref, three_ref,
    slice_ref,
):
    plain = dot(interleave(False), packed_ref[...])
    tokens = plain[:ROWS].astype(BF)
    tokens_ref[...] = tokens
    masked = (plain[ROWS:] * live_row_ref[...]).astype(BF)
    masked_ref[...] = masked
    normalized, _ = row_stats(tokens)
    normed = normalized.astype(BF)
    for chunk in range(9):
        columns = slice(chunk * 384, (chunk + 1) * 384)
        joined_ref[:, columns] = dot(normed, w_qkv_ref[:, columns]).astype(BF)
    for part in range(4):
        slice_ref[part, :, :COLS] = masked[:, part * COLS : (part + 1) * COLS]
        slice_ref[part, :, COLS:] = jnp.zeros((ROWS, WIDE - COLS), BF)
    me = place_ref[0]
    sends = (own_ref, one_ref, two_ref, three_ref)
    for step, out_ref in enumerate(sends):
        out_ref[:, D:] = slice_ref[(me + step) % 4]
    row = lax.broadcasted_iota(jnp.int32, (ROWS, ROWS), 0)
    col = lax.broadcasted_iota(jnp.int32, (ROWS, ROWS), 1)
    allowed = (row % PATCHES == col % PATCHES) & (live_col_ref[...] > 0.5)
    for head in range(H):
        base, width, inside = window(head)
        queries = only(inside, joined_ref[:, base : base + width])
        keys_in = joined_ref[:, D + base : D + base + width]
        values = joined_ref[:, 2 * D + base : 2 * D + base + width]
        scores = jnp.where(allowed, dot(queries, keys_in, NT) * SCALE, -1e30)
        exponent = jnp.exp(scores - jnp.max(scores, axis=-1, keepdims=True))
        probs = exponent / jnp.sum(exponent, axis=-1, keepdims=True)
        probs_ref[head] = probs
        attended = dot(probs.astype(BF), values).astype(BF)
        if head == 0:
            own_ref[:, base : base + width] = attended
        else:
            before = own_ref[:, base : base + width]
            own_ref[:, base : base + width] = jnp.where(inside, attended, before)
    attended = own_ref[:, :D]
    one_ref[:, :D] = attended
    two_ref[:, :D] = attended
    three_ref[:, :D] = attended


def backward_kernel(
    tokens_ref, masked_ref, joined_ref, probs_ref, w_qkv_ref, w_out_ref, d_tokens_ref, grad_ref, head_ref
):
    masked = masked_ref[...]
    for chunk in range(3):
        columns = slice(chunk * 384, (chunk + 1) * 384)
        head_ref[:, columns] = dot(masked, w_out_ref[columns, :], NT).astype(BF)
    for head in range(H):
        base, width, inside = window(head)
        queries = only(inside, joined_ref[:, base : base + width])
        keys_in = joined_ref[:, D + base : D + base + width]
        values = joined_ref[:, 2 * D + base : 2 * D + base + width]
        head_grad = only(inside, head_ref[:, base : base + width])
        probs = probs_ref[head]
        prob_grad = dot(head_grad, values, NT)
        inner = jnp.sum(probs * prob_grad, axis=-1, keepdims=True)
        score_grad = (probs * (prob_grad - inner) * SCALE).astype(BF)
        parts = (
            dot(score_grad, keys_in).astype(BF),
            dot(score_grad, queries, TN).astype(BF),
            dot(probs.astype(BF), head_grad, TN).astype(BF),
        )
        for index, part in enumerate(parts):
            at = index * D + base
            if head == 0:
                grad_ref[:, at : at + width] = part
            else:
                grad_ref[:, at : at + width] = jnp.where(inside, part, grad_ref[:, at : at + width])
    normed_grad = jnp.concatenate(
        [dot(grad_ref[...], w_qkv_ref[c * 384 : (c + 1) * 384, :], NT) for c in range(3)], axis=1
    )
    normalized, inverse = row_stats(tokens_ref[...])
    mean_grad = jnp.mean(normed_grad, axis=-1, keepdims=True)
    mean_cross = jnp.mean(normed_grad * normalized, axis=-1, keepdims=True)
    d_tokens_ref[...] = (
        masked.astype(F32) + inverse * (normed_grad - mean_grad - normalized * mean_cross)
    ).astype(BF)


def weight_kernel(own_ref, one_ref, two_ref, three_ref, mine_ref, theirs_ref, keep_ref, send_ref):
    refs = (own_ref, one_ref, two_ref, three_ref)
    attended = jnp.concatenate([ref[:, :D] for ref in refs], axis=0)
    masked = jnp.concatenate([ref[:, D:] for ref in refs], axis=0)
    theirs = dot(attended, theirs_ref[...]).astype(BF)
    send_ref[...] = dot(theirs, masked, TN).astype(BF)
    mine = dot(attended, mine_ref[...]).astype(BF)
    keep_ref[...] = dot(mine, masked, TN)


def chosen_columns(core):
    lane = jnp.arange(SLOTS * PAD_ROWS, dtype=jnp.int32)
    inner = lane % PAD_ROWS
    target = lane // PAD_ROWS * (2 * OUT_ROWS) + core * OUT_ROWS + inner
    target = jnp.where(inner < OUT_ROWS, target, -1)
    return (jnp.arange(D, dtype=jnp.int32)[:, None] == target[None, :]).astype(BF)


def body(tokens, d_out, frames, frame_order, w_qkv, w_out):
    place = lax.axis_index("dp")
    core = lax.axis_index("core")
    shape = jax.ShapeDtypeStruct
    live = (frame_order[0] < frames[0]).astype(F32)
    live_rows = jnp.repeat(live, PATCHES)
    packed = call(pack_kernel, shape((256, D), BF), (tokens[0], d_out[0]), limit=16)
    arrived = lax.all_to_all(
        packed.reshape(SLOTS, 8, D), ("y", "z"), split_axis=0, concat_axis=0, tiled=True
    ).reshape(256, D)
    kept, masked, joined, probs, own, one, two, three = call(
        forward_kernel,
        (
            shape((ROWS, D), BF),
            shape((ROWS, D), BF),
            shape((ROWS, 3 * D), BF),
            shape((H, ROWS, ROWS), F32),
        )
        + (shape((ROWS, D + WIDE), BF),) * 4,
        (place.reshape(1), arrived, live_rows[:, None], live_rows[None, :], w_qkv),
        scratch=(pltpu.VMEM((4, ROWS, WIDE), BF),),
        smem=(0,),
        flops=int(2e9),
        data=int(14e6),
    )
    ring = lambda step: [(i, (i + step) % 4) for i in range(4)]
    from_one = lax.ppermute(one, "dp", ring(1))
    from_two = lax.ppermute(two, "dp", ring(2))
    from_three = lax.ppermute(three, "dp", ring(3))
    d_rows = call(
        backward_kernel,
        shape((ROWS, D), BF),
        (kept, masked, joined, probs, w_qkv, w_out),
        scratch=(pltpu.VMEM((ROWS, 3 * D), BF), pltpu.VMEM((ROWS, D), BF)),
        flops=int(3e9),
        data=int(16e6),
    )
    returned = lax.all_to_all(
        d_rows.reshape(SLOTS, PATCHES, D), ("y", "z"), split_axis=0, concat_axis=0, tiled=True
    )
    d_tokens = returned.reshape(1, ROWS, D)
    keep, send = call(
        weight_kernel,
        (shape((SLOTS * PAD_ROWS, WIDE), F32), shape((SLOTS * PAD_ROWS, WIDE), BF)),
        (own, from_one, from_two, from_three, chosen_columns(core), chosen_columns(1 - core)),
        flops=int(3e9),
        data=int(8e6),
    )
    got = lax.ppermute(send, "core", [(0, 1), (1, 0)])
    partial = (keep + got.astype(F32)).astype(BF).reshape(SLOTS, PAD_ROWS, WIDE)
    terms = lax.all_to_all(partial, ("y", "z"), split_axis=0, concat_axis=0, tiled=True)
    total = jnp.sum(terms.astype(F32), axis=0)
    return d_tokens, total[:OUT_ROWS, :COLS]


def solution(mesh):
    fine = Mesh(mesh.devices.reshape(4, 4, 8, 2), ("dp", "y", "z", "core"))
    seq = ("y", "z", "core")
    placed = (P("dp", seq, None), P("dp", seq, None), P("dp"), P("dp", None), P(), P())
    return jax.shard_map(
        body,
        mesh=fine,
        in_specs=placed,
        out_specs=(P("dp", seq, None), P(seq, "dp")),
        check_vma=False,
    )
```

```python
import math

import jax
import jax.numpy as jnp
from jax import lax
from jax.experimental import pallas as pl
from jax.experimental.pallas import tpu as pltpu
from jax.sharding import Mesh, PartitionSpec as P

H = 16
D = 1152
E = D // H
SLOTS = 32
PATCHES = 4
ROWS = SLOTS * PATCHES
SCALE = 1.0 / math.sqrt(E)
BF = jnp.bfloat16
F32 = jnp.float32
MIB = 1024 * 1024
COLS = 288
WIDE = 384
OUT_ROWS = 18
PAD_ROWS = 24

NN = (((1,), (0,)), ((), ()))
NT = (((1,), (1,)), ((), ()))
TN = (((0,), (0,)), ((), ()))


def dot(a, b, dims=NN):
    return lax.dot_general(a, b, dims, preferred_element_type=F32)


def whole():
    return pl.BlockSpec(memory_space=pltpu.VMEM)


def call(kernel, out_shape, inputs, scratch=(), limit=32, flops=0, data=0, smem=(), far=()):
    spaces = {i: pltpu.SMEM for i in smem} | {i: pl.ANY for i in far}
    specs = [
        pl.BlockSpec(memory_space=spaces.get(i, pltpu.VMEM)) for i in range(len(inputs))
    ]
    return pl.pallas_call(
        kernel,
        out_shape=out_shape,
        in_specs=specs,
        out_specs=jax.tree.map(lambda _: whole(), out_shape),
        scratch_shapes=list(scratch),
        compiler_params=pltpu.CompilerParams(vmem_limit_bytes=limit * MIB),
        cost_estimate=pl.CostEstimate(flops=flops, bytes_accessed=data, transcendentals=0),
    )(*inputs)


def interleave(rows_first):
    packed = lax.broadcasted_iota(jnp.int32, (256, 256), 0 if rows_first else 1)
    plain = lax.broadcasted_iota(jnp.int32, (256, 256), 1 if rows_first else 0)
    inner = packed % 8
    target = (packed // 8) * 4 + inner % 4 + jnp.where(inner >= 4, 128, 0)
    return (plain == target).astype(F32).astype(BF)


def pack_kernel(tokens_ref, d_out_ref, packed_ref, both_ref, sems):
    copies = [
        pltpu.make_async_copy(ref, both_ref.at[pl.ds(i * ROWS, ROWS)], sems.at[i])
        for i, ref in enumerate((tokens_ref, d_out_ref))
    ]
    for copy in copies:
        copy.start()
    chooser = interleave(True)
    for copy in copies:
        copy.wait()
    packed_ref[...] = dot(chooser, both_ref[...]).astype(BF)


def row_stats(tokens):
    values = tokens.astype(F32)
    center = values - jnp.mean(values, axis=-1, keepdims=True)
    spread = jnp.mean(center * center, axis=-1, keepdims=True)
    inverse = lax.rsqrt(spread + 1e-06)
    return center * inverse, inverse


def window(head):
    low = head * E
    base = low // 128 * 128
    width = 128 if low + E <= base + 128 else 256
    lane = lax.broadcasted_iota(jnp.int32, (ROWS, width), 1)
    inside = (lane >= low - base) & (lane < low - base + E)
    return base, width, inside


def only(inside, array):
    return jnp.where(inside, array, jnp.zeros_like(array))


def forward_kernel(
    place_ref, packed_ref, live_row_ref, live_col_ref, w_qkv_ref,
    tokens_ref, masked_ref, joined_ref, probs_ref, own_ref, one_ref, two_ref, three_ref,
    slice_ref, attended_ref, weight_ref, sems,
):
    copies = [
        pltpu.make_async_copy(
            w_qkv_ref.at[:, pl.ds(chunk * WIDE, WIDE)],
            weight_ref.at[:, pl.ds(chunk * WIDE, WIDE)],
            sems.at[chunk],
        )
        for chunk in range(9)
    ]
    for copy in copies:
        copy.start()
    plain = dot(interleave(False), packed_ref[...])
    tokens = plain[:ROWS].astype(BF)
    tokens_ref[...] = tokens
    normalized, _ = row_stats(tokens)
    normed = normalized.astype(BF)
    masked = (plain[ROWS:] * live_row_ref[...]).astype(BF)
    masked_ref[...] = masked
    for part in range(4):
        slice_ref[part, :, :COLS] = masked[:, part * COLS : (part + 1) * COLS]
        slice_ref[part, :, COLS:] = jnp.zeros((ROWS, WIDE - COLS), BF)
    me = place_ref[0]
    sends = (own_ref, one_ref, two_ref, three_ref)
    for step, out_ref in enumerate(sends):
        chosen = slice_ref[(me + step) % 4]
        for third in range(3):
            out_ref[D + third * ROWS : D + (third + 1) * ROWS, :] = chosen[
                :, third * 128 : (third + 1) * 128
            ]
    for chunk in range(9):
        copies[chunk].wait()
        columns = slice(chunk * WIDE, (chunk + 1) * WIDE)
        joined_ref[:, columns] = dot(normed, weight_ref[:, columns]).astype(BF)
    row = lax.broadcasted_iota(jnp.int32, (ROWS, ROWS), 0)
    col = lax.broadcasted_iota(jnp.int32, (ROWS, ROWS), 1)
    allowed = (row % PATCHES == col % PATCHES) & (live_col_ref[...] > 0.5)
    for head in range(H):
        base, width, inside = window(head)
        queries = only(inside, joined_ref[:, base : base + width])
        keys_in = joined_ref[:, D + base : D + base + width]
        values = joined_ref[:, 2 * D + base : 2 * D + base + width]
        scores = jnp.where(allowed, dot(queries, keys_in, NT) * SCALE, -1e30)
        exponent = jnp.exp(scores - jnp.max(scores, axis=-1, keepdims=True))
        probs = exponent / jnp.sum(exponent, axis=-1, keepdims=True)
        probs_ref[head] = probs
        attended = dot(probs.astype(BF), values)
        if head == 0:
            attended_ref[:, base : base + width] = attended
        else:
            before = attended_ref[:, base : base + width]
            attended_ref[:, base : base + width] = jnp.where(inside, attended, before)
    for block in range(9):
        lanes = slice(block * 128, (block + 1) * 128)
        turned = attended_ref[:, lanes].T.astype(BF)
        for out_ref in sends:
            out_ref[lanes, :] = turned


def spread_rows(to_packed):
    shape = (512, 384) if to_packed else (384, 512)
    packed = lax.broadcasted_iota(jnp.int32, shape, 0 if to_packed else 1)
    plain = lax.broadcasted_iota(jnp.int32, shape, 1 if to_packed else 0)
    row = plain % ROWS
    target = row // PATCHES * 16 + plain // ROWS * PATCHES + row % PATCHES
    return (packed == target).astype(F32).astype(BF)


def backward_kernel(
    tokens_ref, masked_ref, joined_ref, probs_ref, w_qkv_ref, w_out_ref,
    packed_ref,
    grad_ref, head_ref, weight_ref, out_weight_ref, sems,
):
    out_copies = [
        pltpu.make_async_copy(
            w_out_ref.at[pl.ds(chunk * WIDE, WIDE)],
            out_weight_ref.at[pl.ds(chunk * WIDE, WIDE)],
            sems.at[chunk],
        )
        for chunk in range(3)
    ]
    qkv_copies = [
        pltpu.make_async_copy(
            w_qkv_ref.at[pl.ds(chunk * WIDE, WIDE)],
            weight_ref.at[pl.ds(chunk * WIDE, WIDE)],
            sems.at[3 + chunk],
        )
        for chunk in range(3)
    ]
    for copy in out_copies + qkv_copies:
        copy.start()
    masked = masked_ref[...]
    for chunk in range(3):
        columns = slice(chunk * WIDE, (chunk + 1) * WIDE)
        out_copies[chunk].wait()
        head_ref[:, columns] = dot(masked, out_weight_ref[columns, :], NT).astype(BF)
    for head in range(H):
        base, width, inside = window(head)
        queries = only(inside, joined_ref[:, base : base + width])
        keys_in = joined_ref[:, D + base : D + base + width]
        values = joined_ref[:, 2 * D + base : 2 * D + base + width]
        head_grad = only(inside, head_ref[:, base : base + width])
        probs = probs_ref[head]
        prob_grad = dot(head_grad, values, NT)
        inner = jnp.sum(probs * prob_grad, axis=-1, keepdims=True)
        score_grad = (probs * (prob_grad - inner) * SCALE).astype(BF)
        parts = (
            dot(score_grad, keys_in).astype(BF),
            dot(score_grad, queries, TN).astype(BF),
            dot(probs.astype(BF), head_grad, TN).astype(BF),
        )
        for index, part in enumerate(parts):
            at = index * D + base
            if head == 0:
                grad_ref[:, at : at + width] = part
            else:
                grad_ref[:, at : at + width] = jnp.where(inside, part, grad_ref[:, at : at + width])
    pieces = []
    for chunk in range(3):
        qkv_copies[chunk].wait()
        rows = slice(chunk * WIDE, (chunk + 1) * WIDE)
        pieces.append(dot(grad_ref[...], weight_ref[rows, :], NT))
    normed_grad = jnp.concatenate(pieces, axis=1)
    normalized, inverse = row_stats(tokens_ref[...])
    mean_grad = jnp.mean(normed_grad, axis=-1, keepdims=True)
    mean_cross = jnp.mean(normed_grad * normalized, axis=-1, keepdims=True)
    d_tokens = (
        masked.astype(F32) + inverse * (normed_grad - mean_grad - normalized * mean_cross)
    ).astype(BF)
    stacked = jnp.concatenate([d_tokens[:, c * WIDE : (c + 1) * WIDE] for c in range(3)], axis=0)
    packed_ref[...] = dot(spread_rows(True), stacked).astype(BF)


def weight_kernel(own_ref, one_ref, two_ref, three_ref, chosen_ref, after_ref, terms_ref):
    refs = (own_ref, one_ref, two_ref, three_ref)
    attended = jnp.concatenate([ref[:D, :] for ref in refs], axis=1)
    masked = jnp.concatenate(
        [
            jnp.concatenate([ref[D + t * 128 : D + (t + 1) * 128, :] for t in range(3)], axis=1)
            for ref in refs
        ],
        axis=0,
    )
    chosen = dot(chosen_ref[...], attended).astype(BF)
    terms_ref[...] = dot(chosen, masked).astype(terms_ref.dtype)


def merge_kernel(rows_ref, keep_ref, got_ref, merged_ref):
    rows = rows_ref[...].astype(F32).reshape(SLOTS, 16, WIDE)
    terms = (keep_ref[...] + got_ref[...].astype(F32)).reshape(SLOTS, PAD_ROWS, WIDE)
    merged = jnp.concatenate([rows, terms], axis=1).reshape(SLOTS * 40, WIDE)
    merged_ref[...] = merged.astype(BF)


def unpack_kernel(merged_ref, d_tokens_ref, d_w_ref):
    merged = merged_ref[...].astype(F32).reshape(SLOTS, 40, WIDE)
    rows = merged[:, :16].reshape(512, WIDE).astype(BF)
    plain = dot(spread_rows(False), rows).astype(BF)
    for block in range(3):
        d_tokens_ref[:, block * WIDE : (block + 1) * WIDE] = plain[block * ROWS : (block + 1) * ROWS]
    total = jnp.sum(merged[:, 16:], axis=0)
    d_w_ref[...] = total[:OUT_ROWS, :COLS]


def chosen_rows(core):
    at = jnp.arange(SLOTS * PAD_ROWS, dtype=jnp.int32)
    inner = at % PAD_ROWS
    target = at // PAD_ROWS * (2 * OUT_ROWS) + core * OUT_ROWS + inner
    target = jnp.where(inner < OUT_ROWS, target, -1)
    return (target[:, None] == jnp.arange(D, dtype=jnp.int32)[None, :]).astype(BF)


def body(tokens, d_out, frames, frame_order, w_qkv, w_out):
    place = lax.axis_index("dp")
    core = lax.axis_index("core")
    shape = jax.ShapeDtypeStruct
    live = (frame_order[0] < frames[0]).astype(F32)
    live_rows = jnp.repeat(live, PATCHES)
    packed = call(
        pack_kernel,
        shape((256, D), BF),
        (tokens[0], d_out[0]),
        scratch=(pltpu.VMEM((256, D), BF), pltpu.SemaphoreType.DMA((2,))),
        limit=60,
        far=(0, 1),
    )
    arrived = lax.all_to_all(
        packed.reshape(SLOTS, 8, D), ("y", "z"), split_axis=0, concat_axis=0, tiled=True
    ).reshape(256, D)
    kept, masked, joined, probs, own, one, two, three = call(
        forward_kernel,
        (
            shape((ROWS, D), BF),
            shape((ROWS, D), BF),
            shape((ROWS, 3 * D), BF),
            shape((H, ROWS, ROWS), F32),
        )
        + (shape((D + WIDE, ROWS), BF),) * 4,
        (place.reshape(1), arrived, live_rows[:, None], live_rows[None, :], w_qkv),
        scratch=(
            pltpu.VMEM((4, ROWS, WIDE), BF),
            pltpu.VMEM((ROWS, D), F32),
            pltpu.VMEM((D, 3 * D), BF),
            pltpu.SemaphoreType.DMA((9,)),
        ),
        smem=(0,),
        far=(4,),
        limit=47,
        flops=int(2e9),
        data=int(14e6),
    )
    ring = lambda step: [(i, (i + step) % 4) for i in range(4)]
    from_one = lax.ppermute(one, "dp", ring(1))
    from_two = lax.ppermute(two, "dp", ring(2))
    from_three = lax.ppermute(three, "dp", ring(3))
    rows = call(
        backward_kernel,
        shape((512, WIDE), BF),
        (kept, masked, joined, probs, w_qkv, w_out),
        scratch=(
            pltpu.VMEM((ROWS, 3 * D), BF),
            pltpu.VMEM((ROWS, D), BF),
            pltpu.VMEM((D, 3 * D), BF),
            pltpu.VMEM((D, D), BF),
            pltpu.SemaphoreType.DMA((6,)),
        ),
        far=(4, 5),
        limit=47,
        flops=int(3e9),
        data=int(16e6),
    )
    payloads = (own, from_one, from_two, from_three)
    send = call(
        weight_kernel,
        shape((SLOTS * PAD_ROWS, WIDE), BF),
        payloads + (chosen_rows(1 - core), rows),
        far=(5,),
        flops=int(1e9),
        data=int(4e6),
    )
    got = lax.ppermute(send, "core", [(0, 1), (1, 0)])
    keep = call(
        weight_kernel,
        shape((SLOTS * PAD_ROWS, WIDE), F32),
        payloads + (chosen_rows(core), send),
        far=(5,),
        flops=int(1e9),
        data=int(4e6),
    )
    merged = call(merge_kernel, shape((SLOTS * 40, WIDE), BF), (rows, keep, got), limit=16)
    returned = lax.all_to_all(
        merged.reshape(SLOTS, 40, WIDE), ("y", "z"), split_axis=0, concat_axis=0, tiled=True
    ).reshape(SLOTS * 40, WIDE)
    d_tokens, d_w = call(
        unpack_kernel, (shape((ROWS, D), BF), shape((OUT_ROWS, COLS), F32)), (returned,), limit=16
    )
    return d_tokens[None], d_w


def solution(mesh):
    fine = Mesh(mesh.devices.reshape(4, 4, 8, 2), ("dp", "y", "z", "core"))
    seq = ("y", "z", "core")
    placed = (P("dp", seq, None), P("dp", seq, None), P("dp"), P("dp", None), P(), P())
    return jax.shard_map(
        body,
        mesh=fine,
        in_specs=placed,
        out_specs=(P("dp", seq, None), P(seq, "dp")),
        check_vma=False,
    )
```

```python
import math

import jax
import jax.numpy as jnp
from jax import lax
from jax.experimental import pallas as pl
from jax.experimental.pallas import tpu as pltpu
from jax.sharding import Mesh, PartitionSpec as P

H = 16
D = 1152
E = D // H
SLOTS = 32
PATCHES = 4
ROWS = SLOTS * PATCHES
SCALE = 1.0 / math.sqrt(E)
BF = jnp.bfloat16
F32 = jnp.float32
MIB = 1024 * 1024
COLS = 288
WIDE = 384
OUT_ROWS = 18
CHUNK = 80
TOKEN_ROWS = 36
PAYLOAD = D + COLS
EXP_SCALE = SCALE * math.log2(math.e)

NN = (((1,), (0,)), ((), ()))
NT = (((1,), (1,)), ((), ()))
TN = (((0,), (0,)), ((), ()))


def dot(a, b, dims=NN):
    return lax.dot_general(a, b, dims, preferred_element_type=F32)


def whole():
    return pl.BlockSpec(memory_space=pltpu.VMEM)


def call(kernel, out_shape, inputs, scratch=(), limit=32, flops=0, data=0, smem=(), far=()):
    spaces = {i: pltpu.SMEM for i in smem} | {i: pl.ANY for i in far}
    specs = [
        pl.BlockSpec(memory_space=spaces.get(i, pltpu.VMEM)) for i in range(len(inputs))
    ]
    return pl.pallas_call(
        kernel,
        out_shape=out_shape,
        in_specs=specs,
        out_specs=jax.tree.map(lambda _: whole(), out_shape),
        scratch_shapes=list(scratch),
        compiler_params=pltpu.CompilerParams(vmem_limit_bytes=limit * MIB),
        cost_estimate=pl.CostEstimate(flops=flops, bytes_accessed=data, transcendentals=0),
    )(*inputs)


def pick(shape, target, along):
    return (lax.broadcasted_iota(jnp.int32, shape, along) == target).astype(F32).astype(BF)


def row_index(rows):
    return lax.broadcasted_iota(jnp.int32, (rows, 1), 0)


def lane_index(lanes):
    return lax.broadcasted_iota(jnp.int32, (1, lanes), 1)


def source_row(packed):
    inner = packed % 8
    return packed // 8 * PATCHES + inner % PATCHES + jnp.where(inner >= PATCHES, ROWS, 0)


def patch_row(packed):
    inner = packed % 8
    return packed // 8 + inner % PATCHES * SLOTS + jnp.where(inner >= PATCHES, ROWS, 0)


def pack_kernel(tokens_ref, d_out_ref, packed_ref, both_ref, sems):
    copies = [
        pltpu.make_async_copy(ref, both_ref.at[pl.ds(i * ROWS, ROWS)], sems.at[i])
        for i, ref in enumerate((tokens_ref, d_out_ref))
    ]
    for copy in copies:
        copy.start()
    chooser = pick((256, 256), source_row(row_index(256)), 1)
    for copy in copies:
        copy.wait()
    packed_ref[...] = dot(chooser, both_ref[...]).astype(BF)


def row_stats(tokens):
    values = tokens.astype(F32)
    center = values - jnp.mean(values, axis=-1, keepdims=True)
    spread = jnp.mean(center * center, axis=-1, keepdims=True)
    inverse = lax.rsqrt(spread + 1e-06)
    return center * inverse, inverse


def window(head):
    low = head * E
    base = low // 128 * 128
    width = 128 if low + E <= base + 128 else 256
    lane = lax.broadcasted_iota(jnp.int32, (ROWS, width), 1)
    inside = (lane >= low - base) & (lane < low - base + E)
    return base, width, inside


def only(inside, array):
    return jnp.where(inside, array, jnp.zeros_like(array))


def lane_patch():
    return lax.broadcasted_iota(jnp.int32, (SLOTS, ROWS), 1) // SLOTS


def diagonal(full, patch):
    packed = full[:SLOTS]
    for p in range(1, PATCHES):
        packed = jnp.where(patch == p, full[p * SLOTS : (p + 1) * SLOTS], packed)
    return packed


def spread(packed, patch):
    blocks = [jnp.where(patch == p, packed, 0.0) for p in range(PATCHES)]
    return jnp.concatenate(blocks, axis=0).astype(BF)


def forward_kernel(
    place_ref, packed_ref, live_ref, w_qkv_ref,
    tokens_ref, masked_ref, joined_ref, probs_ref, own_ref, one_ref, two_ref, three_ref,
    turned_ref, values_ref, attended_ref, weight_ref, sems,
):
    spans = [pl.ds(kind * D + chunk * WIDE, WIDE) for chunk in range(3) for kind in range(3)]
    copies = [
        pltpu.make_async_copy(w_qkv_ref.at[:, span], weight_ref.at[:, span], sems.at[i])
        for i, span in enumerate(spans)
    ]
    for copy in copies:
        copy.start()
    plain = dot(pick((256, 256), patch_row(lane_index(256)), 0), packed_ref[...])
    tokens = plain[:ROWS].astype(BF)
    tokens_ref[...] = tokens
    normalized, _ = row_stats(tokens)
    normed = normalized.astype(BF)
    live = live_ref[...]
    masked = plain[ROWS:] * jnp.concatenate([live] * PATCHES, axis=0)
    masked_ref[...] = masked.astype(BF)
    for block in range(9):
        lanes = slice(block * 128, (block + 1) * 128)
        turned_ref[lanes, :] = masked[:, lanes].T.astype(BF)
    me = place_ref[0]
    sends = (own_ref, one_ref, two_ref, three_ref)
    for step, out_ref in enumerate(sends):
        start = pl.multiple_of((me + step) % 4 * COLS, 16)
        out_ref[D:, :] = turned_ref[pl.ds(start, COLS), :]
    patch = lane_patch()
    done = 0
    for chunk in range(3):
        for kind in range(3):
            copies[chunk * 3 + kind].wait()
            columns = slice(kind * D + chunk * WIDE, kind * D + (chunk + 1) * WIDE)
            product = dot(normed, weight_ref[:, columns])
            joined_ref[:, columns] = product.astype(BF)
            if kind == 2:
                for block in range(3):
                    at = chunk * WIDE + block * 128
                    values_ref[at : at + 128, :] = product[:, block * 128 : (block + 1) * 128].T
        while done < H and window(done)[0] + window(done)[1] <= (chunk + 1) * WIDE:
            head = done
            done += 1
            base, width, inside = window(head)
            queries = only(inside, joined_ref[:, base : base + width])
            keys_in = joined_ref[:, D + base : D + base + width]
            scores = diagonal(dot(keys_in, queries, NT), patch)
            scores = jnp.where(live > 0.5, scores, -1e30)
            top = jnp.max(scores, axis=0, keepdims=True)
            exponent = jnp.exp2((scores - top) * EXP_SCALE)
            probs = exponent / jnp.sum(exponent, axis=0, keepdims=True)
            probs_ref[head] = probs
            rows = slice(head * E, (head + 1) * E)
            attended_ref[rows, :] = dot(values_ref[rows, :].astype(BF), spread(probs, patch))
    attended = attended_ref[...].astype(BF)
    for out_ref in sends:
        out_ref[:D, :] = attended


def backward_kernel(
    tokens_ref, masked_ref, joined_ref, probs_ref, w_qkv_ref, w_out_ref,
    packed_ref, place_ref,
    grad_ref, head_ref, weight_ref, out_weight_ref, sems,
):
    out_copies = [
        pltpu.make_async_copy(
            w_out_ref.at[pl.ds(chunk * WIDE, WIDE)],
            out_weight_ref.at[pl.ds(chunk * WIDE, WIDE)],
            sems.at[chunk],
        )
        for chunk in range(3)
    ]
    qkv_copies = [
        pltpu.make_async_copy(
            w_qkv_ref.at[pl.ds(chunk * WIDE, WIDE)],
            weight_ref.at[pl.ds(chunk * WIDE, WIDE)],
            sems.at[3 + chunk],
        )
        for chunk in range(3)
    ]
    for copy in out_copies + qkv_copies:
        copy.start()
    term = lane_index(3 * 8 * OUT_ROWS)
    kind, inner = term // (8 * OUT_ROWS), term % (8 * OUT_ROWS)
    row = inner % OUT_ROWS
    at = TOKEN_ROWS + kind * OUT_ROWS + jnp.where(kind == 2, row // 4, row)
    place_ref[...] = pick((8 * CHUNK, 3 * 8 * OUT_ROWS), inner // OUT_ROWS * CHUNK + at, 0)
    masked = masked_ref[...]
    for chunk in range(3):
        columns = slice(chunk * WIDE, (chunk + 1) * WIDE)
        out_copies[chunk].wait()
        head_ref[:, columns] = dot(masked, out_weight_ref[columns, :], NT).astype(BF)
    patch = lane_patch()
    for head in range(H):
        base, width, inside = window(head)
        queries = only(inside, joined_ref[:, base : base + width])
        keys_in = joined_ref[:, D + base : D + base + width]
        values = joined_ref[:, 2 * D + base : 2 * D + base + width]
        head_grad = only(inside, head_ref[:, base : base + width])
        probs = probs_ref[head]
        prob_grad = diagonal(dot(values, head_grad, NT), patch)
        inner_sum = jnp.sum(probs * prob_grad, axis=0, keepdims=True)
        score_grad = spread(probs * (prob_grad - inner_sum) * SCALE, patch)
        parts = (
            dot(score_grad, keys_in, TN).astype(BF),
            dot(score_grad, queries).astype(BF),
            dot(spread(probs, patch), head_grad).astype(BF),
        )
        for index, part in enumerate(parts):
            at = index * D + base
            if head == 0:
                grad_ref[:, at : at + width] = part
            else:
                grad_ref[:, at : at + width] = jnp.where(inside, part, grad_ref[:, at : at + width])
    pieces = []
    for chunk in range(3):
        qkv_copies[chunk].wait()
        rows = slice(chunk * WIDE, (chunk + 1) * WIDE)
        pieces.append(dot(grad_ref[...], weight_ref[rows, :], NT))
    normed_grad = jnp.concatenate(pieces, axis=1)
    normalized, inverse = row_stats(tokens_ref[...])
    mean_grad = jnp.mean(normed_grad, axis=-1, keepdims=True)
    mean_cross = jnp.mean(normed_grad * normalized, axis=-1, keepdims=True)
    d_tokens = (
        masked.astype(F32) + inverse * (normed_grad - mean_grad - normalized * mean_cross)
    ).astype(BF)
    piece = lane_index(576)
    target = piece % 16 * CHUNK + piece // 64 * PATCHES + piece % 64 // 16
    chooser = pick((16 * CHUNK, 576), target, 0)
    for half in range(2):
        stacked = jnp.concatenate(
            [
                d_tokens[p * SLOTS + half * 16 : p * SLOTS + half * 16 + 16, c * 128 : (c + 1) * 128]
                for c in range(9)
                for p in range(PATCHES)
            ],
            axis=0,
        )
        packed_ref[half * 16 * CHUNK : (half + 1) * 16 * CHUNK, :] = dot(chooser, stacked).astype(BF)


def weight_kernel(own_ref, one_ref, two_ref, three_ref, chosen_ref, after_ref, terms_ref):
    refs = (own_ref, one_ref, two_ref, three_ref)
    attended = jnp.concatenate([ref[:D, :] for ref in refs], axis=1)
    masked = jnp.concatenate([ref[D:, :] for ref in refs], axis=1)
    masked = jnp.concatenate([masked[:256]] + [masked[256:]] * 4, axis=0)
    chosen = dot(chosen_ref[...], attended).astype(BF)
    terms_ref[...] = dot(chosen, masked, NT).astype(terms_ref.dtype)


def merge_kernel(rows_ref, keep_ref, got_ref, place_ref, merged_ref):
    terms = keep_ref[...] + got_ref[...].astype(F32)
    row = row_index(SLOTS * OUT_ROWS) % OUT_ROWS
    last = jnp.where(row % 4 == lane_index(128) // 32, terms[:, 256:], 0.0)
    blocks = [block.astype(BF) for block in (terms[:, :128], terms[:, 128:256], last)]
    for group in range(4):
        rows = slice(group * 8 * OUT_ROWS, (group + 1) * 8 * OUT_ROWS)
        stacked = jnp.concatenate([block[rows] for block in blocks], axis=0)
        out = slice(group * 8 * CHUNK, (group + 1) * 8 * CHUNK)
        merged_ref[out, :] = (
            dot(place_ref[...], stacked) + rows_ref[out, :].astype(F32)
        ).astype(BF)


def unpack_kernel(merged_ref, d_tokens_ref, d_w_ref, total_ref):
    piece = row_index(288)
    row = piece % 32
    source = row // PATCHES * CHUNK + piece // 32 * PATCHES + row % PATCHES
    chooser = pick((288, 8 * CHUNK), source, 1)
    for group in range(4):
        rows = dot(chooser, merged_ref[group * 8 * CHUNK : (group + 1) * 8 * CHUNK, :]).astype(BF)
        for block in range(9):
            d_tokens_ref[group * 32 : (group + 1) * 32, block * 128 : (block + 1) * 128] = rows[
                block * 32 : (block + 1) * 32
            ]
    merged = merged_ref[...].astype(F32).reshape(SLOTS, CHUNK, 128)
    total_ref[...] = jnp.sum(merged[:, 32:], axis=0)
    first = TOKEN_ROWS - 32
    d_w_ref[:, :128] = total_ref[first : first + OUT_ROWS, :]
    d_w_ref[:, 128:256] = total_ref[first + OUT_ROWS : first + 2 * OUT_ROWS, :]
    for row in range(OUT_ROWS):
        at = first + 2 * OUT_ROWS + row // 4
        lanes = slice(row % 4 * 32, row % 4 * 32 + 32)
        d_w_ref[row : row + 1, 256:] = total_ref[at : at + 1, lanes]


def chosen_rows(core):
    at = jnp.arange(SLOTS * OUT_ROWS, dtype=jnp.int32)
    target = at // OUT_ROWS * (2 * OUT_ROWS) + core * OUT_ROWS + at % OUT_ROWS
    return (target[:, None] == jnp.arange(D, dtype=jnp.int32)[None, :]).astype(BF)


def body(tokens, d_out, frames, frame_order, w_qkv, w_out):
    place = lax.axis_index("dp")
    core = lax.axis_index("core")
    shape = jax.ShapeDtypeStruct
    live = (frame_order[0] < frames[0]).astype(F32)
    packed = call(
        pack_kernel,
        shape((256, D), BF),
        (tokens[0], d_out[0]),
        scratch=(pltpu.VMEM((256, D), BF), pltpu.SemaphoreType.DMA((2,))),
        limit=60,
        far=(0, 1),
    )
    arrived = lax.all_to_all(
        packed.reshape(SLOTS, 8, D), ("y", "z"), split_axis=0, concat_axis=0, tiled=True
    ).reshape(256, D)
    kept, masked, joined, probs, own, one, two, three = call(
        forward_kernel,
        (
            shape((ROWS, D), BF),
            shape((ROWS, D), BF),
            shape((ROWS, 3 * D), BF),
            shape((H, SLOTS, ROWS), F32),
        )
        + (shape((PAYLOAD, ROWS), BF),) * 4,
        (place.reshape(1), arrived, live[:, None], w_qkv),
        scratch=(
            pltpu.VMEM((D, ROWS), BF),
            pltpu.VMEM((D, ROWS), F32),
            pltpu.VMEM((D, ROWS), F32),
            pltpu.VMEM((D, 3 * D), BF),
            pltpu.SemaphoreType.DMA((9,)),
        ),
        smem=(0,),
        far=(3,),
        limit=47,
        flops=int(2e9),
        data=int(14e6),
    )
    ring = lambda step: [(i, (i + step) % 4) for i in range(4)]
    from_one = lax.ppermute(one, "dp", ring(1))
    from_two = lax.ppermute(two, "dp", ring(2))
    from_three = lax.ppermute(three, "dp", ring(3))
    rows, places = call(
        backward_kernel,
        (shape((SLOTS * CHUNK, 128), BF), shape((8 * CHUNK, 3 * 8 * OUT_ROWS), BF)),
        (kept, masked, joined, probs, w_qkv, w_out),
        scratch=(
            pltpu.VMEM((ROWS, 3 * D), BF),
            pltpu.VMEM((ROWS, D), BF),
            pltpu.VMEM((D, 3 * D), BF),
            pltpu.VMEM((D, D), BF),
            pltpu.SemaphoreType.DMA((6,)),
        ),
        far=(4, 5),
        limit=47,
        flops=int(3e9),
        data=int(16e6),
    )
    payloads = (own, from_one, from_two, from_three)
    send = call(
        weight_kernel,
        shape((SLOTS * OUT_ROWS, WIDE), BF),
        payloads + (chosen_rows(1 - core), rows),
        far=(5,),
        flops=int(1e9),
        data=int(4e6),
    )
    got = lax.ppermute(send, "core", [(0, 1), (1, 0)])
    keep = call(
        weight_kernel,
        shape((SLOTS * OUT_ROWS, WIDE), F32),
        payloads + (chosen_rows(core), send),
        far=(5,),
        flops=int(1e9),
        data=int(4e6),
    )
    merged = call(
        merge_kernel, shape((SLOTS * CHUNK, 128), BF), (rows, keep, got, places), limit=16
    )
    returned = lax.all_to_all(
        merged.reshape(SLOTS, CHUNK, 128), ("y", "z"), split_axis=0, concat_axis=0, tiled=True
    ).reshape(SLOTS * CHUNK, 128)
    d_tokens, d_w = call(
        unpack_kernel,
        (shape((ROWS, D), BF), shape((OUT_ROWS, COLS), F32)),
        (returned,),
        scratch=(pltpu.VMEM((CHUNK - 32, 128), F32),),
        limit=16,
    )
    return d_tokens[None], d_w


def solution(mesh):
    fine = Mesh(mesh.devices.reshape(4, 4, 8, 2), ("dp", "y", "z", "core"))
    seq = ("y", "z", "core")
    placed = (P("dp", seq, None), P("dp", seq, None), P("dp"), P("dp", None), P(), P())
    return jax.shard_map(
        body,
        mesh=fine,
        in_specs=placed,
        out_specs=(P("dp", seq, None), P(seq, "dp")),
        check_vma=False,
    )
```

```python
import math

import jax
import jax.numpy as jnp
from jax import lax
from jax.experimental import pallas as pl
from jax.experimental.pallas import tpu as pltpu
from jax.sharding import Mesh, PartitionSpec as P

H = 16
D = 1152
E = D // H
SLOTS = 32
PATCHES = 4
ROWS = SLOTS * PATCHES
SCALE = 1.0 / math.sqrt(E)
BF = jnp.bfloat16
F32 = jnp.float32
MIB = 1024 * 1024
COLS = 288
WIDE = 384
OUT_ROWS = 18
CHUNK = 80
TOKEN_ROWS = 36
PAYLOAD = D + COLS
EXP_SCALE = SCALE * math.log2(math.e)

NN = (((1,), (0,)), ((), ()))
NT = (((1,), (1,)), ((), ()))
TN = (((0,), (0,)), ((), ()))


def dot(a, b, dims=NN):
    return lax.dot_general(a, b, dims, preferred_element_type=F32)


def whole():
    return pl.BlockSpec(memory_space=pltpu.VMEM)


def call(
    kernel, out_shape, inputs, scratch=(), limit=32, flops=0, data=0, smem=(), far=(), smem_out=()
):
    spaces = {i: pltpu.SMEM for i in smem} | {i: pl.ANY for i in far}
    specs = [
        pl.BlockSpec(memory_space=spaces.get(i, pltpu.VMEM)) for i in range(len(inputs))
    ]
    return pl.pallas_call(
        kernel,
        out_shape=out_shape,
        in_specs=specs,
        out_specs=[
            pl.BlockSpec(memory_space=pltpu.SMEM) if i in smem_out else whole()
            for i in range(len(out_shape))
        ],
        scratch_shapes=list(scratch),
        compiler_params=pltpu.CompilerParams(vmem_limit_bytes=limit * MIB),
        cost_estimate=pl.CostEstimate(flops=flops, bytes_accessed=data, transcendentals=0),
    )(*inputs)


def pick(shape, target, along):
    return (lax.broadcasted_iota(jnp.int32, shape, along) == target).astype(F32).astype(BF)


def row_index(rows):
    return lax.broadcasted_iota(jnp.int32, (rows, 1), 0)


def lane_index(lanes):
    return lax.broadcasted_iota(jnp.int32, (1, lanes), 1)


def source_row(packed):
    inner = packed % 8
    return packed // 8 * PATCHES + inner % PATCHES + jnp.where(inner >= PATCHES, ROWS, 0)


def patch_row(packed):
    inner = packed % 8
    return packed // 8 + inner % PATCHES * SLOTS + jnp.where(inner >= PATCHES, ROWS, 0)


def pack_kernel(
    dp_ref, core_ref, frames_ref, order_ref, tokens_ref, d_out_ref,
    packed_ref, dp_out_ref, core_out_ref, live_ref,
    both_ref, sems,
):
    dp_out_ref[0] = dp_ref[0]
    core_out_ref[0] = core_ref[0]
    copies = [
        pltpu.make_async_copy(ref, both_ref.at[pl.ds(i * ROWS, ROWS)], sems.at[i])
        for i, ref in enumerate((tokens_ref, d_out_ref))
    ]
    for copy in copies:
        copy.start()
    chooser = pick((256, 256), source_row(row_index(256)), 1)
    live = (order_ref[...] < frames_ref[0]).astype(F32)
    live = jnp.where(row_index(SLOTS) == lane_index(SLOTS), live, 0.0)
    live_ref[...] = jnp.sum(live, axis=1, keepdims=True)
    for copy in copies:
        copy.wait()
    packed_ref[...] = dot(chooser, both_ref[...]).astype(BF)


def row_stats(tokens):
    values = tokens.astype(F32)
    center = values - jnp.mean(values, axis=-1, keepdims=True)
    spread = jnp.mean(center * center, axis=-1, keepdims=True)
    inverse = lax.rsqrt(spread + 1e-06)
    return center * inverse, inverse


def window(head):
    low = head * E
    base = low // 128 * 128
    width = 128 if low + E <= base + 128 else 256
    lane = lax.broadcasted_iota(jnp.int32, (ROWS, width), 1)
    inside = (lane >= low - base) & (lane < low - base + E)
    return base, width, inside


def only(inside, array):
    return jnp.where(inside, array, jnp.zeros_like(array))


def lane_patch():
    return lax.broadcasted_iota(jnp.int32, (SLOTS, ROWS), 1) // SLOTS


def diagonal(full, patch):
    packed = full[:SLOTS]
    for p in range(1, PATCHES):
        packed = jnp.where(patch == p, full[p * SLOTS : (p + 1) * SLOTS], packed)
    return packed


def spread(packed, patch):
    blocks = [jnp.where(patch == p, packed, 0.0) for p in range(PATCHES)]
    return jnp.concatenate(blocks, axis=0).astype(BF)


def forward_kernel(
    place_ref, packed_ref, live_ref, w_qkv_ref,
    tokens_ref, masked_ref, joined_ref, probs_ref, own_ref, one_ref, two_ref, three_ref,
    turned_ref, values_ref, attended_ref, weight_ref, sems,
):
    spans = [pl.ds(kind * D + chunk * WIDE, WIDE) for chunk in range(3) for kind in range(3)]
    copies = [
        pltpu.make_async_copy(w_qkv_ref.at[:, span], weight_ref.at[:, span], sems.at[i])
        for i, span in enumerate(spans)
    ]
    for copy in copies:
        copy.start()
    plain = dot(pick((256, 256), patch_row(lane_index(256)), 0), packed_ref[...])
    tokens = plain[:ROWS].astype(BF)
    tokens_ref[...] = tokens
    normalized, _ = row_stats(tokens)
    normed = normalized.astype(BF)
    live = live_ref[...]
    masked = plain[ROWS:] * jnp.concatenate([live] * PATCHES, axis=0)
    masked_ref[...] = masked.astype(BF)
    for block in range(9):
        lanes = slice(block * 128, (block + 1) * 128)
        turned_ref[lanes, :] = masked[:, lanes].T.astype(BF)
    me = place_ref[0]
    sends = (own_ref, one_ref, two_ref, three_ref)
    for step, out_ref in enumerate(sends):
        start = pl.multiple_of((me + step) % 4 * COLS, 16)
        out_ref[D:, :] = turned_ref[pl.ds(start, COLS), :]
    patch = lane_patch()
    done = 0
    for chunk in range(3):
        for kind in range(3):
            copies[chunk * 3 + kind].wait()
            columns = slice(kind * D + chunk * WIDE, kind * D + (chunk + 1) * WIDE)
            product = dot(normed, weight_ref[:, columns])
            joined_ref[:, columns] = product.astype(BF)
            if kind == 2:
                for block in range(3):
                    at = chunk * WIDE + block * 128
                    values_ref[at : at + 128, :] = product[:, block * 128 : (block + 1) * 128].T
        while done < H and window(done)[0] + window(done)[1] <= (chunk + 1) * WIDE:
            head = done
            done += 1
            base, width, inside = window(head)
            queries = only(inside, joined_ref[:, base : base + width])
            keys_in = joined_ref[:, D + base : D + base + width]
            scores = diagonal(dot(keys_in, queries, NT), patch)
            scores = jnp.where(live > 0.5, scores, -1e30)
            top = jnp.max(scores, axis=0, keepdims=True)
            exponent = jnp.exp2((scores - top) * EXP_SCALE)
            probs = exponent / jnp.sum(exponent, axis=0, keepdims=True)
            probs_ref[head] = probs
            rows = slice(head * E, (head + 1) * E)
            attended_ref[rows, :] = dot(values_ref[rows, :].astype(BF), spread(probs, patch))
    attended = attended_ref[...].astype(BF)
    for out_ref in sends:
        out_ref[:D, :] = attended


def backward_kernel(
    core_ref, tokens_ref, masked_ref, joined_ref, probs_ref, w_qkv_ref, w_out_ref,
    packed_ref, place_ref, mine_ref, theirs_ref,
    grad_ref, head_ref, weight_ref, out_weight_ref, sems,
):
    out_copies = [
        pltpu.make_async_copy(
            w_out_ref.at[pl.ds(chunk * WIDE, WIDE)],
            out_weight_ref.at[pl.ds(chunk * WIDE, WIDE)],
            sems.at[chunk],
        )
        for chunk in range(3)
    ]
    qkv_copies = [
        pltpu.make_async_copy(
            w_qkv_ref.at[pl.ds(chunk * WIDE, WIDE)],
            weight_ref.at[pl.ds(chunk * WIDE, WIDE)],
            sems.at[3 + chunk],
        )
        for chunk in range(3)
    ]
    for copy in out_copies + qkv_copies:
        copy.start()
    term = lane_index(3 * 8 * OUT_ROWS)
    kind, inner = term // (8 * OUT_ROWS), term % (8 * OUT_ROWS)
    row = inner % OUT_ROWS
    at = TOKEN_ROWS + kind * OUT_ROWS + jnp.where(kind == 2, row // 4, row)
    place_ref[...] = pick((8 * CHUNK, 3 * 8 * OUT_ROWS), inner // OUT_ROWS * CHUNK + at, 0)
    row = row_index(SLOTS * OUT_ROWS)
    start = row // OUT_ROWS * (2 * OUT_ROWS) + row % OUT_ROWS
    core = core_ref[0]
    mine_ref[...] = pick((SLOTS * OUT_ROWS, D), start + core * OUT_ROWS, 1)
    theirs_ref[...] = pick((SLOTS * OUT_ROWS, D), start + (1 - core) * OUT_ROWS, 1)
    masked = masked_ref[...]
    for chunk in range(3):
        columns = slice(chunk * WIDE, (chunk + 1) * WIDE)
        out_copies[chunk].wait()
        head_ref[:, columns] = dot(masked, out_weight_ref[columns, :], NT).astype(BF)
    patch = lane_patch()
    for head in range(H):
        base, width, inside = window(head)
        queries = only(inside, joined_ref[:, base : base + width])
        keys_in = joined_ref[:, D + base : D + base + width]
        values = joined_ref[:, 2 * D + base : 2 * D + base + width]
        head_grad = only(inside, head_ref[:, base : base + width])
        probs = probs_ref[head]
        prob_grad = diagonal(dot(values, head_grad, NT), patch)
        inner_sum = jnp.sum(probs * prob_grad, axis=0, keepdims=True)
        score_grad = spread(probs * (prob_grad - inner_sum) * SCALE, patch)
        parts = (
            dot(score_grad, keys_in, TN).astype(BF),
            dot(score_grad, queries).astype(BF),
            dot(spread(probs, patch), head_grad).astype(BF),
        )
        for index, part in enumerate(parts):
            at = index * D + base
            if head == 0:
                grad_ref[:, at : at + width] = part
            else:
                grad_ref[:, at : at + width] = jnp.where(inside, part, grad_ref[:, at : at + width])
    pieces = []
    for chunk in range(3):
        qkv_copies[chunk].wait()
        rows = slice(chunk * WIDE, (chunk + 1) * WIDE)
        pieces.append(dot(grad_ref[...], weight_ref[rows, :], NT))
    normed_grad = jnp.concatenate(pieces, axis=1)
    normalized, inverse = row_stats(tokens_ref[...])
    mean_grad = jnp.mean(normed_grad, axis=-1, keepdims=True)
    mean_cross = jnp.mean(normed_grad * normalized, axis=-1, keepdims=True)
    d_tokens = (
        masked.astype(F32) + inverse * (normed_grad - mean_grad - normalized * mean_cross)
    ).astype(BF)
    piece = lane_index(576)
    target = piece % 16 * CHUNK + piece // 64 * PATCHES + piece % 64 // 16
    chooser = pick((16 * CHUNK, 576), target, 0)
    for half in range(2):
        stacked = jnp.concatenate(
            [
                d_tokens[p * SLOTS + half * 16 : p * SLOTS + half * 16 + 16, c * 128 : (c + 1) * 128]
                for c in range(9)
                for p in range(PATCHES)
            ],
            axis=0,
        )
        packed_ref[half * 16 * CHUNK : (half + 1) * 16 * CHUNK, :] = dot(chooser, stacked).astype(BF)


def weight_kernel(own_ref, one_ref, two_ref, three_ref, chosen_ref, *after_and_out):
    terms_ref = after_and_out[-1]
    refs = (own_ref, one_ref, two_ref, three_ref)
    attended = jnp.concatenate([ref[:D, :] for ref in refs], axis=1)
    masked = jnp.concatenate([ref[D:, :] for ref in refs], axis=1)
    masked = jnp.concatenate([masked[:256]] + [masked[256:]] * 4, axis=0)
    chosen = dot(chosen_ref[...], attended).astype(BF)
    terms_ref[...] = dot(chosen, masked, NT).astype(terms_ref.dtype)


def merge_kernel(rows_ref, keep_ref, got_ref, place_ref, merged_ref):
    terms = keep_ref[...] + got_ref[...].astype(F32)
    row = row_index(SLOTS * OUT_ROWS) % OUT_ROWS
    last = jnp.where(row % 4 == lane_index(128) // 32, terms[:, 256:], 0.0)
    blocks = [block.astype(BF) for block in (terms[:, :128], terms[:, 128:256], last)]
    for group in range(4):
        rows = slice(group * 8 * OUT_ROWS, (group + 1) * 8 * OUT_ROWS)
        stacked = jnp.concatenate([block[rows] for block in blocks], axis=0)
        out = slice(group * 8 * CHUNK, (group + 1) * 8 * CHUNK)
        merged_ref[out, :] = (
            dot(place_ref[...], stacked) + rows_ref[out, :].astype(F32)
        ).astype(BF)


def unpack_kernel(merged_ref, d_tokens_ref, d_w_ref, total_ref):
    piece = row_index(288)
    row = piece % 32
    source = row // PATCHES * CHUNK + piece // 32 * PATCHES + row % PATCHES
    chooser = pick((288, 8 * CHUNK), source, 1)
    for group in range(4):
        rows = dot(chooser, merged_ref[group * 8 * CHUNK : (group + 1) * 8 * CHUNK, :]).astype(BF)
        for block in range(9):
            d_tokens_ref[group * 32 : (group + 1) * 32, block * 128 : (block + 1) * 128] = rows[
                block * 32 : (block + 1) * 32
            ]
    merged = merged_ref[...].astype(F32).reshape(SLOTS, CHUNK, 128)
    total_ref[...] = jnp.sum(merged[:, 32:], axis=0)
    first = TOKEN_ROWS - 32
    d_w_ref[:, :128] = total_ref[first : first + OUT_ROWS, :]
    d_w_ref[:, 128:256] = total_ref[first + OUT_ROWS : first + 2 * OUT_ROWS, :]
    for row in range(OUT_ROWS):
        at = first + 2 * OUT_ROWS + row // 4
        lanes = slice(row % 4 * 32, row % 4 * 32 + 32)
        d_w_ref[row : row + 1, 256:] = total_ref[at : at + 1, lanes]


def body(tokens, d_out, frames, frame_order, w_qkv, w_out):
    shape = jax.ShapeDtypeStruct
    one_int = shape((1,), jnp.int32)
    packed, place, core, live = call(
        pack_kernel,
        (shape((256, D), BF), one_int, one_int, shape((SLOTS, 1), F32)),
        (
            lax.axis_index("dp").reshape(1),
            lax.axis_index("core").reshape(1),
            frames,
            frame_order,
            tokens[0],
            d_out[0],
        ),
        scratch=(pltpu.VMEM((256, D), BF), pltpu.SemaphoreType.DMA((2,))),
        limit=60,
        smem=(0, 1, 2),
        far=(4, 5),
        smem_out=(1, 2),
    )
    arrived = lax.all_to_all(
        packed.reshape(SLOTS, 8, D), ("y", "z"), split_axis=0, concat_axis=0, tiled=True
    ).reshape(256, D)
    kept, masked, joined, probs, own, one, two, three = call(
        forward_kernel,
        (
            shape((ROWS, D), BF),
            shape((ROWS, D), BF),
            shape((ROWS, 3 * D), BF),
            shape((H, SLOTS, ROWS), F32),
        )
        + (shape((PAYLOAD, ROWS), BF),) * 4,
        (place, arrived, live, w_qkv),
        scratch=(
            pltpu.VMEM((D, ROWS), BF),
            pltpu.VMEM((D, ROWS), F32),
            pltpu.VMEM((D, ROWS), F32),
            pltpu.VMEM((D, 3 * D), BF),
            pltpu.SemaphoreType.DMA((9,)),
        ),
        smem=(0,),
        far=(3,),
        limit=47,
        flops=int(2e9),
        data=int(14e6),
    )
    ring = lambda step: [(i, (i + step) % 4) for i in range(4)]
    from_one = lax.ppermute(one, "dp", ring(1))
    from_two = lax.ppermute(two, "dp", ring(2))
    from_three = lax.ppermute(three, "dp", ring(3))
    chosen = shape((SLOTS * OUT_ROWS, D), BF)
    rows, places, mine, theirs = call(
        backward_kernel,
        (shape((SLOTS * CHUNK, 128), BF), shape((8 * CHUNK, 3 * 8 * OUT_ROWS), BF), chosen, chosen),
        (core, kept, masked, joined, probs, w_qkv, w_out),
        scratch=(
            pltpu.VMEM((ROWS, 3 * D), BF),
            pltpu.VMEM((ROWS, D), BF),
            pltpu.VMEM((D, 3 * D), BF),
            pltpu.VMEM((D, D), BF),
            pltpu.SemaphoreType.DMA((6,)),
        ),
        smem=(0,),
        far=(5, 6),
        limit=47,
        flops=int(3e9),
        data=int(16e6),
    )
    payloads = (own, from_one, from_two, from_three)
    (send,) = call(
        weight_kernel,
        (shape((SLOTS * OUT_ROWS, WIDE), BF),),
        payloads + (theirs,),
        flops=int(1e9),
        data=int(4e6),
    )
    got = lax.ppermute(send, "core", [(0, 1), (1, 0)])
    (keep,) = call(
        weight_kernel,
        (shape((SLOTS * OUT_ROWS, WIDE), F32),),
        payloads + (mine, send),
        far=(5,),
        flops=int(1e9),
        data=int(4e6),
    )
    (merged,) = call(
        merge_kernel, (shape((SLOTS * CHUNK, 128), BF),), (rows, keep, got, places), limit=16
    )
    returned = lax.all_to_all(
        merged.reshape(SLOTS, CHUNK, 128), ("y", "z"), split_axis=0, concat_axis=0, tiled=True
    ).reshape(SLOTS * CHUNK, 128)
    d_tokens, d_w = call(
        unpack_kernel,
        (shape((ROWS, D), BF), shape((OUT_ROWS, COLS), F32)),
        (returned,),
        scratch=(pltpu.VMEM((CHUNK - 32, 128), F32),),
        limit=16,
    )
    return d_tokens[None], d_w


def solution(mesh):
    fine = Mesh(mesh.devices.reshape(4, 4, 8, 2), ("dp", "y", "z", "core"))
    seq = ("y", "z", "core")
    placed = (P("dp", seq, None), P("dp", seq, None), P("dp"), P("dp", None), P(), P())
    return jax.shard_map(
        body,
        mesh=fine,
        in_specs=placed,
        out_specs=(P("dp", seq, None), P(seq, "dp")),
        check_vma=False,
    )
```

```python
import functools
import math

import jax
import jax.numpy as jnp
from jax import lax
from jax.experimental import pallas as pl
from jax.experimental.pallas import tpu as pltpu
from jax.sharding import Mesh, PartitionSpec as P

H = 16
D = 1152
E = D // H
SLOTS = 32
PATCHES = 4
ROWS = SLOTS * PATCHES
SCALE = 1.0 / math.sqrt(E)
BF = jnp.bfloat16
F32 = jnp.float32
MIB = 1024 * 1024
COLS = 288
WIDE = 384
OUT_ROWS = 18
CHUNK = 80
TOKEN_ROWS = 36
PAYLOAD = D + COLS
HALF = D // 2
EXP_SCALE = SCALE * math.log2(math.e)

NN = (((1,), (0,)), ((), ()))
NT = (((1,), (1,)), ((), ()))
TN = (((0,), (0,)), ((), ()))


def dot(a, b, dims=NN):
    return lax.dot_general(a, b, dims, preferred_element_type=F32)


def whole():
    return pl.BlockSpec(memory_space=pltpu.VMEM)


def call(kernel, out_shape, inputs, scratch=(), limit=32, flops=0, data=0, smem=(), far=()):
    spaces = {i: pltpu.SMEM for i in smem} | {i: pl.ANY for i in far}
    specs = [
        pl.BlockSpec(memory_space=spaces.get(i, pltpu.VMEM)) for i in range(len(inputs))
    ]
    return pl.pallas_call(
        kernel,
        out_shape=out_shape,
        in_specs=specs,
        out_specs=jax.tree.map(lambda _: whole(), out_shape),
        scratch_shapes=list(scratch),
        compiler_params=pltpu.CompilerParams(vmem_limit_bytes=limit * MIB),
        cost_estimate=pl.CostEstimate(flops=flops, bytes_accessed=data, transcendentals=0),
    )(*inputs)


def pick(shape, target, along):
    return (lax.broadcasted_iota(jnp.int32, shape, along) == target).astype(F32).astype(BF)


def row_index(rows):
    return lax.broadcasted_iota(jnp.int32, (rows, 1), 0)


def lane_index(lanes):
    return lax.broadcasted_iota(jnp.int32, (1, lanes), 1)


def source_row(packed):
    inner = packed % 8
    return packed // 8 * PATCHES + inner % PATCHES + jnp.where(inner >= PATCHES, ROWS, 0)


def patch_row(packed):
    inner = packed % 8
    return packed // 8 + inner % PATCHES * SLOTS + jnp.where(inner >= PATCHES, ROWS, 0)


def pack_kernel(tokens_ref, d_out_ref, packed_ref, both_ref, sems):
    copies = [
        pltpu.make_async_copy(ref, both_ref.at[pl.ds(i * ROWS, ROWS)], sems.at[i])
        for i, ref in enumerate((tokens_ref, d_out_ref))
    ]
    for copy in copies:
        copy.start()
    chooser = pick((256, 256), source_row(row_index(256)), 1)
    for copy in copies:
        copy.wait()
    packed_ref[...] = dot(chooser, both_ref[...]).astype(BF)


def row_stats(tokens):
    values = tokens.astype(F32)
    center = values - jnp.mean(values, axis=-1, keepdims=True)
    spread = jnp.mean(center * center, axis=-1, keepdims=True)
    inverse = lax.rsqrt(spread + 1e-06)
    return center * inverse, inverse


def window(head):
    low = head * E
    base = low // 128 * 128
    width = 128 if low + E <= base + 128 else 256
    lane = lax.broadcasted_iota(jnp.int32, (ROWS, width), 1)
    inside = (lane >= low - base) & (lane < low - base + E)
    return base, width, inside


def only(inside, array):
    return jnp.where(inside, array, jnp.zeros_like(array))


def lane_patch():
    return lax.broadcasted_iota(jnp.int32, (SLOTS, ROWS), 1) // SLOTS


def diagonal(full, patch):
    packed = full[:SLOTS]
    for p in range(1, PATCHES):
        packed = jnp.where(patch == p, full[p * SLOTS : (p + 1) * SLOTS], packed)
    return packed


def spread(packed, patch):
    blocks = [jnp.where(patch == p, packed, 0.0) for p in range(PATCHES)]
    return jnp.concatenate(blocks, axis=0).astype(BF)


def forward_kernel(
    place_ref, core_ref, packed_ref, live_ref, first_q_ref, first_k_ref, first_v_ref, w_qkv_ref,
    tokens_ref, masked_ref, joined_ref, probs_ref, own_ref, one_ref, two_ref, three_ref,
    turned_ref, values_ref, attended_ref, weight_ref, sems,
):
    spans = [pl.ds(kind * D + chunk * WIDE, WIDE) for chunk in (1, 2) for kind in range(3)]
    copies = [
        pltpu.make_async_copy(w_qkv_ref.at[:, span], weight_ref.at[:, span], sems.at[i])
        for i, span in enumerate(spans)
    ]
    for copy in copies:
        copy.start()
    plain = dot(pick((256, 256), patch_row(lane_index(256)), 0), packed_ref[...])
    tokens = plain[:ROWS].astype(BF)
    tokens_ref[...] = tokens
    normalized, _ = row_stats(tokens)
    normed = normalized.astype(BF)
    live = live_ref[...]
    masked = plain[ROWS:] * jnp.concatenate([live] * PATCHES, axis=0)
    masked_ref[...] = masked.astype(BF)
    for block in range(9):
        lanes = slice(block * 128, (block + 1) * 128)
        turned_ref[lanes, :] = masked[:, lanes].T.astype(BF)
    me = place_ref[0]
    sends = (own_ref, one_ref, two_ref, three_ref)
    for step, out_ref in enumerate(sends):
        start = pl.multiple_of((me + step) % 4 * COLS, 16)
        out_ref[D:, :] = turned_ref[pl.ds(start, COLS), :]
    patch = lane_patch()
    done = 0
    for chunk in range(3):
        if chunk > 0:
            for copy in copies[chunk * 3 - 3 : chunk * 3]:
                copy.wait()
        for kind in range(3):
            columns = slice(kind * D + chunk * WIDE, kind * D + (chunk + 1) * WIDE)
            if chunk == 0:
                weight = (first_q_ref, first_k_ref, first_v_ref)[kind][...]
            else:
                weight = weight_ref[:, columns]
            product = dot(normed, weight)
            joined_ref[:, columns] = product.astype(BF)
            if kind == 2:
                for block in range(3):
                    at = chunk * WIDE + block * 128
                    values_ref[at : at + 128, :] = product[:, block * 128 : (block + 1) * 128].T
        while done < H and window(done)[0] + window(done)[1] <= (chunk + 1) * WIDE:
            head = done
            done += 1
            base, width, inside = window(head)
            queries = only(inside, joined_ref[:, base : base + width])
            keys_in = joined_ref[:, D + base : D + base + width]
            scores = diagonal(dot(keys_in, queries, NT), patch)
            scores = jnp.where(live > 0.5, scores, -1e30)
            top = jnp.max(scores, axis=0, keepdims=True)
            exponent = jnp.exp2((scores - top) * EXP_SCALE)
            probs = exponent / jnp.sum(exponent, axis=0, keepdims=True)
            probs_ref[head] = probs
            rows = slice(head * E, (head + 1) * E)
            attended = dot(values_ref[rows, :].astype(BF), spread(probs, patch))
            for group in range(4):
                at = group % 2 * HALF + head * 2 * OUT_ROWS + group // 2 * OUT_ROWS
                attended_ref[at : at + OUT_ROWS, :] = attended[group * OUT_ROWS : (group + 1) * OUT_ROWS]
    attended = attended_ref[...].astype(BF)
    for out_ref in sends:
        out_ref[:D, :] = attended


def backward_kernel(
    tokens_ref, masked_ref, joined_ref, probs_ref, w_qkv_ref, w_out_ref,
    packed_ref, place_ref,
    grad_ref, head_ref, weight_ref, out_weight_ref, sems,
):
    out_copies = [
        pltpu.make_async_copy(
            w_out_ref.at[pl.ds(chunk * WIDE, WIDE)],
            out_weight_ref.at[pl.ds(chunk * WIDE, WIDE)],
            sems.at[chunk],
        )
        for chunk in range(3)
    ]
    qkv_copies = [
        pltpu.make_async_copy(
            w_qkv_ref.at[pl.ds(chunk * WIDE, WIDE)],
            weight_ref.at[pl.ds(chunk * WIDE, WIDE)],
            sems.at[3 + chunk],
        )
        for chunk in range(3)
    ]
    for copy in out_copies + qkv_copies:
        copy.start()
    term = lane_index(3 * 8 * OUT_ROWS)
    kind, inner = term // (8 * OUT_ROWS), term % (8 * OUT_ROWS)
    row = inner % OUT_ROWS
    at = TOKEN_ROWS + kind * OUT_ROWS + jnp.where(kind == 2, row // 4, row)
    place_ref[...] = pick((8 * CHUNK, 3 * 8 * OUT_ROWS), inner // OUT_ROWS * CHUNK + at, 0)
    masked = masked_ref[...]
    for copy in out_copies:
        copy.wait()
    for chunk in range(3):
        columns = slice(chunk * WIDE, (chunk + 1) * WIDE)
        head_ref[:, columns] = dot(masked, out_weight_ref[columns, :], NT).astype(BF)
    patch = lane_patch()
    for head in range(H):
        base, width, inside = window(head)
        queries = only(inside, joined_ref[:, base : base + width])
        keys_in = joined_ref[:, D + base : D + base + width]
        values = joined_ref[:, 2 * D + base : 2 * D + base + width]
        head_grad = only(inside, head_ref[:, base : base + width])
        probs = probs_ref[head]
        prob_grad = diagonal(dot(values, head_grad, NT), patch)
        inner_sum = jnp.sum(probs * prob_grad, axis=0, keepdims=True)
        score_grad = spread(probs * (prob_grad - inner_sum) * SCALE, patch)
        parts = (
            dot(score_grad, keys_in, TN).astype(BF),
            dot(score_grad, queries).astype(BF),
            dot(spread(probs, patch), head_grad).astype(BF),
        )
        for index, part in enumerate(parts):
            at = index * D + base
            if head == 0:
                grad_ref[:, at : at + width] = part
            else:
                grad_ref[:, at : at + width] = jnp.where(inside, part, grad_ref[:, at : at + width])
    pieces = []
    for copy in qkv_copies:
        copy.wait()
    for chunk in range(3):
        rows = slice(chunk * WIDE, (chunk + 1) * WIDE)
        pieces.append(dot(grad_ref[...], weight_ref[rows, :], NT))
    normed_grad = jnp.concatenate(pieces, axis=1)
    normalized, inverse = row_stats(tokens_ref[...])
    mean_grad = jnp.mean(normed_grad, axis=-1, keepdims=True)
    mean_cross = jnp.mean(normed_grad * normalized, axis=-1, keepdims=True)
    d_tokens = (
        masked.astype(F32) + inverse * (normed_grad - mean_grad - normalized * mean_cross)
    ).astype(BF)
    piece = lane_index(576)
    target = piece % 16 * CHUNK + piece // 64 * PATCHES + piece % 64 // 16
    chooser = pick((16 * CHUNK, 576), target, 0)
    for half in range(2):
        stacked = jnp.concatenate(
            [
                d_tokens[p * SLOTS + half * 16 : p * SLOTS + half * 16 + 16, c * 128 : (c + 1) * 128]
                for c in range(9)
                for p in range(PATCHES)
            ],
            axis=0,
        )
        packed_ref[half * 16 * CHUNK : (half + 1) * 16 * CHUNK, :] = dot(chooser, stacked).astype(BF)


def weight_kernel(other, core_ref, own_ref, one_ref, two_ref, three_ref, after_ref, terms_ref):
    refs = (own_ref, one_ref, two_ref, three_ref)
    core = 1 - core_ref[0] if other else core_ref[0]
    start = pl.multiple_of(core * HALF, HALF)
    attended = jnp.concatenate([ref[pl.ds(start, HALF), :] for ref in refs], axis=1)
    masked = jnp.concatenate([ref[D:, :] for ref in refs], axis=1)
    masked = jnp.concatenate([masked[:256]] + [masked[256:]] * 4, axis=0)
    terms_ref[...] = dot(attended, masked, NT).astype(terms_ref.dtype)


def merge_kernel(rows_ref, keep_ref, got_ref, place_ref, merged_ref):
    terms = keep_ref[...] + got_ref[...].astype(F32)
    row = row_index(SLOTS * OUT_ROWS) % OUT_ROWS
    last = jnp.where(row % 4 == lane_index(128) // 32, terms[:, 256:], 0.0)
    blocks = [block.astype(BF) for block in (terms[:, :128], terms[:, 128:256], last)]
    for group in range(4):
        rows = slice(group * 8 * OUT_ROWS, (group + 1) * 8 * OUT_ROWS)
        stacked = jnp.concatenate([block[rows] for block in blocks], axis=0)
        out = slice(group * 8 * CHUNK, (group + 1) * 8 * CHUNK)
        merged_ref[out, :] = (
            dot(place_ref[...], stacked) + rows_ref[out, :].astype(F32)
        ).astype(BF)


def unpack_kernel(merged_ref, d_tokens_ref, d_w_ref, total_ref):
    piece = row_index(288)
    row = piece % 32
    source = row // PATCHES * CHUNK + piece // 32 * PATCHES + row % PATCHES
    chooser = pick((288, 8 * CHUNK), source, 1)
    for group in range(4):
        rows = dot(chooser, merged_ref[group * 8 * CHUNK : (group + 1) * 8 * CHUNK, :]).astype(BF)
        for block in range(9):
            d_tokens_ref[group * 32 : (group + 1) * 32, block * 128 : (block + 1) * 128] = rows[
                block * 32 : (block + 1) * 32
            ]
    merged = merged_ref[...].astype(F32).reshape(SLOTS, CHUNK, 128)
    total_ref[...] = jnp.sum(merged[:, 32:], axis=0)
    first = TOKEN_ROWS - 32
    d_w_ref[:, :128] = total_ref[first : first + OUT_ROWS, :]
    d_w_ref[:, 128:256] = total_ref[first + OUT_ROWS : first + 2 * OUT_ROWS, :]
    for row in range(OUT_ROWS):
        at = first + 2 * OUT_ROWS + row // 4
        lanes = slice(row % 4 * 32, row % 4 * 32 + 32)
        d_w_ref[row : row + 1, 256:] = total_ref[at : at + 1, lanes]


def body(tokens, d_out, frames, frame_order, w_qkv, w_out):
    place = lax.axis_index("dp")
    core = lax.axis_index("core")
    shape = jax.ShapeDtypeStruct
    live = (frame_order[0] < frames[0]).astype(F32)
    packed = call(
        pack_kernel,
        shape((256, D), BF),
        (tokens[0], d_out[0]),
        scratch=(pltpu.VMEM((256, D), BF), pltpu.SemaphoreType.DMA((2,))),
        limit=60,
        far=(0, 1),
    )
    arrived = lax.all_to_all(
        packed.reshape(SLOTS, 8, D), ("y", "z"), split_axis=0, concat_axis=0, tiled=True
    ).reshape(256, D)
    firsts = tuple(w_qkv[:, kind * D : kind * D + WIDE] for kind in range(3))
    kept, masked, joined, probs, own, one, two, three = call(
        forward_kernel,
        (
            shape((ROWS, D), BF),
            shape((ROWS, D), BF),
            shape((ROWS, 3 * D), BF),
            shape((H, SLOTS, ROWS), F32),
        )
        + (shape((PAYLOAD, ROWS), BF),) * 4,
        (place.reshape(1), core.reshape(1), arrived, live[:, None]) + firsts + (w_qkv,),
        scratch=(
            pltpu.VMEM((D, ROWS), BF),
            pltpu.VMEM((D, ROWS), F32),
            pltpu.VMEM((D, ROWS), F32),
            pltpu.VMEM((D, 3 * D), BF),
            pltpu.SemaphoreType.DMA((6,)),
        ),
        smem=(0, 1),
        far=(7,),
        limit=47,
        flops=int(2e9),
        data=int(14e6),
    )
    ring = lambda step: [(i, (i + step) % 4) for i in range(4)]
    from_one = lax.ppermute(one, "dp", ring(1))
    from_two = lax.ppermute(two, "dp", ring(2))
    from_three = lax.ppermute(three, "dp", ring(3))
    rows, places = call(
        backward_kernel,
        (shape((SLOTS * CHUNK, 128), BF), shape((8 * CHUNK, 3 * 8 * OUT_ROWS), BF)),
        (kept, masked, joined, probs, w_qkv, w_out),
        scratch=(
            pltpu.VMEM((ROWS, 3 * D), BF),
            pltpu.VMEM((ROWS, D), BF),
            pltpu.VMEM((D, 3 * D), BF),
            pltpu.VMEM((D, D), BF),
            pltpu.SemaphoreType.DMA((6,)),
        ),
        far=(4, 5),
        limit=47,
        flops=int(3e9),
        data=int(16e6),
    )
    payloads = (own, from_one, from_two, from_three)
    send = call(
        functools.partial(weight_kernel, True),
        shape((SLOTS * OUT_ROWS, WIDE), BF),
        (core.reshape(1),) + payloads + (rows,),
        smem=(0,),
        far=(5,),
        flops=int(1e9),
        data=int(4e6),
    )
    got = lax.ppermute(send, "core", [(0, 1), (1, 0)])
    keep = call(
        functools.partial(weight_kernel, False),
        shape((SLOTS * OUT_ROWS, WIDE), F32),
        (core.reshape(1),) + payloads + (send,),
        smem=(0,),
        far=(5,),
        flops=int(1e9),
        data=int(4e6),
    )
    merged = call(
        merge_kernel, shape((SLOTS * CHUNK, 128), BF), (rows, keep, got, places), limit=16
    )
    returned = lax.all_to_all(
        merged.reshape(SLOTS, CHUNK, 128), ("y", "z"), split_axis=0, concat_axis=0, tiled=True
    ).reshape(SLOTS * CHUNK, 128)
    d_tokens, d_w = call(
        unpack_kernel,
        (shape((ROWS, D), BF), shape((OUT_ROWS, COLS), F32)),
        (returned,),
        scratch=(pltpu.VMEM((CHUNK - 32, 128), F32),),
        limit=16,
    )
    return d_tokens[None], d_w


def solution(mesh):
    fine = Mesh(mesh.devices.reshape(4, 4, 8, 2), ("dp", "y", "z", "core"))
    seq = ("y", "z", "core")
    placed = (P("dp", seq, None), P("dp", seq, None), P("dp"), P("dp", None), P(), P())
    return jax.shard_map(
        body,
        mesh=fine,
        in_specs=placed,
        out_specs=(P("dp", seq, None), P(seq, "dp")),
        check_vma=False,
    )
```

```python
import functools
import math

import jax
import jax.numpy as jnp
from jax import lax
from jax.experimental import pallas as pl
from jax.experimental.pallas import tpu as pltpu
from jax.sharding import Mesh, PartitionSpec as P

H = 16
D = 1152
E = D // H
SLOTS = 32
PATCHES = 4
ROWS = SLOTS * PATCHES
SCALE = 1.0 / math.sqrt(E)
BF = jnp.bfloat16
F32 = jnp.float32
MIB = 1024 * 1024
COLS = 288
WIDE = 384
OUT_ROWS = 18
CHUNK = 80
TOKEN_ROWS = 36
PAYLOAD = D + COLS
HALF = D // 2
EXP_SCALE = SCALE * math.log2(math.e)

NN = (((1,), (0,)), ((), ()))
NT = (((1,), (1,)), ((), ()))
TN = (((0,), (0,)), ((), ()))


def dot(a, b, dims=NN):
    return lax.dot_general(a, b, dims, preferred_element_type=F32)


def call(
    kernel, out_shape, inputs, scratch=(), limit=32, flops=0, data=0, smem=(), far=(), far_out=()
):
    spaces = {i: pltpu.SMEM for i in smem} | {i: pl.ANY for i in far}
    single = isinstance(out_shape, jax.ShapeDtypeStruct)
    shapes = (out_shape,) if single else tuple(out_shape)
    outs = pl.pallas_call(
        kernel,
        out_shape=shapes,
        in_specs=[
            pl.BlockSpec(memory_space=spaces.get(i, pltpu.VMEM)) for i in range(len(inputs))
        ],
        out_specs=tuple(
            pl.BlockSpec(memory_space=pl.ANY if i in far_out else pltpu.VMEM)
            for i in range(len(shapes))
        ),
        scratch_shapes=list(scratch),
        compiler_params=pltpu.CompilerParams(vmem_limit_bytes=limit * MIB),
        cost_estimate=pl.CostEstimate(flops=flops, bytes_accessed=data, transcendentals=0),
    )(*inputs)
    return outs[0] if single else outs


def pick(shape, target, along):
    return (lax.broadcasted_iota(jnp.int32, shape, along) == target).astype(F32).astype(BF)


def row_index(rows):
    return lax.broadcasted_iota(jnp.int32, (rows, 1), 0)


def lane_index(lanes):
    return lax.broadcasted_iota(jnp.int32, (1, lanes), 1)


def source_row(packed):
    inner = packed % 8
    return packed // 8 * PATCHES + inner % PATCHES + jnp.where(inner >= PATCHES, ROWS, 0)


def patch_row(packed):
    inner = packed % 8
    return packed // 8 + inner % PATCHES * SLOTS + jnp.where(inner >= PATCHES, ROWS, 0)


def pack_kernel(tokens_ref, d_out_ref, packed_ref, both_ref, sems):
    copies = [
        pltpu.make_async_copy(ref, both_ref.at[pl.ds(i * ROWS, ROWS)], sems.at[i])
        for i, ref in enumerate((tokens_ref, d_out_ref))
    ]
    for copy in copies:
        copy.start()
    chooser = pick((256, 256), source_row(row_index(256)), 1)
    for copy in copies:
        copy.wait()
    packed_ref[...] = dot(chooser, both_ref[...]).astype(BF)


def row_stats(tokens):
    values = tokens.astype(F32)
    center = values - jnp.mean(values, axis=-1, keepdims=True)
    spread = jnp.mean(center * center, axis=-1, keepdims=True)
    inverse = lax.rsqrt(spread + 1e-06)
    return center * inverse, inverse


def window(head):
    low = head * E
    base = low // 128 * 128
    width = 128 if low + E <= base + 128 else 256
    lane = lax.broadcasted_iota(jnp.int32, (ROWS, width), 1)
    inside = (lane >= low - base) & (lane < low - base + E)
    return base, width, inside


def only(inside, array):
    return jnp.where(inside, array, jnp.zeros_like(array))


def lane_patch():
    return lax.broadcasted_iota(jnp.int32, (SLOTS, ROWS), 1) // SLOTS


def diagonal(full, patch):
    packed = full[:SLOTS]
    for p in range(1, PATCHES):
        packed = jnp.where(patch == p, full[p * SLOTS : (p + 1) * SLOTS], packed)
    return packed


def spread(packed, patch):
    blocks = [jnp.where(patch == p, packed, 0.0) for p in range(PATCHES)]
    return jnp.concatenate(blocks, axis=0).astype(BF)


def forward_kernel(
    core_ref, packed_ref, live_ref, first_q_ref, first_k_ref, first_v_ref, w_qkv_ref,
    tokens_ref, masked_ref, joined_ref, probs_ref, sends_ref,
    turned_ref, values_ref, attended_ref, rounded_ref, weight_ref, sems, send_sems,
):
    spans = [pl.ds(kind * D + chunk * WIDE, WIDE) for chunk in (1, 2) for kind in range(3)]
    copies = [
        pltpu.make_async_copy(w_qkv_ref.at[:, span], weight_ref.at[:, span], sems.at[i])
        for i, span in enumerate(spans)
    ]
    for copy in copies:
        copy.start()
    plain = dot(pick((256, 256), patch_row(lane_index(256)), 0), packed_ref[...])
    tokens = plain[:ROWS].astype(BF)
    tokens_ref[...] = tokens
    normalized, _ = row_stats(tokens)
    normed = normalized.astype(BF)
    live = live_ref[...]
    masked = plain[ROWS:] * jnp.concatenate([live] * PATCHES, axis=0)
    masked_ref[...] = masked.astype(BF)
    for block in range(9):
        lanes = slice(block * 128, (block + 1) * 128)
        turned_ref[lanes, :] = masked[:, lanes].T.astype(BF)
    slices = [
        pltpu.make_async_copy(
            turned_ref.at[pl.ds(part * COLS, COLS)], sends_ref.at[part, pl.ds(D, COLS)], send_sems.at[part]
        )
        for part in range(4)
    ]
    for copy in slices:
        copy.start()
    patch = lane_patch()
    done = 0
    for chunk in range(3):
        if chunk > 0:
            for copy in copies[chunk * 3 - 3 : chunk * 3]:
                copy.wait()
        for kind in range(3):
            columns = slice(kind * D + chunk * WIDE, kind * D + (chunk + 1) * WIDE)
            if chunk == 0:
                weight = (first_q_ref, first_k_ref, first_v_ref)[kind][...]
            else:
                weight = weight_ref[:, columns]
            product = dot(normed, weight)
            joined_ref[:, columns] = product.astype(BF)
            if kind == 2:
                for block in range(3):
                    at = chunk * WIDE + block * 128
                    values_ref[at : at + 128, :] = product[:, block * 128 : (block + 1) * 128].T
        while done < H and window(done)[0] + window(done)[1] <= (chunk + 1) * WIDE:
            head = done
            done += 1
            base, width, inside = window(head)
            queries = only(inside, joined_ref[:, base : base + width])
            keys_in = joined_ref[:, D + base : D + base + width]
            scores = diagonal(dot(keys_in, queries, NT), patch)
            scores = jnp.where(live > 0.5, scores, -1e30)
            top = jnp.max(scores, axis=0, keepdims=True)
            exponent = jnp.exp2((scores - top) * EXP_SCALE)
            probs = exponent / jnp.sum(exponent, axis=0, keepdims=True)
            probs_ref[head] = probs
            rows = slice(head * E, (head + 1) * E)
            attended = dot(values_ref[rows, :].astype(BF), spread(probs, patch))
            for group in range(4):
                at = group % 2 * HALF + head * 2 * OUT_ROWS + group // 2 * OUT_ROWS
                attended_ref[at : at + OUT_ROWS, :] = attended[group * OUT_ROWS : (group + 1) * OUT_ROWS]
    rounded_ref[...] = attended_ref[...].astype(BF)
    wholes = [
        pltpu.make_async_copy(rounded_ref, sends_ref.at[part, pl.ds(0, D)], send_sems.at[4 + part])
        for part in range(4)
    ]
    for copy in wholes:
        copy.start()
    for copy in slices + wholes:
        copy.wait()


def backward_kernel(
    tokens_ref, masked_ref, joined_ref, probs_ref, w_qkv_ref, w_out_ref,
    packed_ref, place_ref,
    grad_ref, head_ref, weight_ref, out_weight_ref, sems,
):
    out_copies = [
        pltpu.make_async_copy(
            w_out_ref.at[pl.ds(chunk * WIDE, WIDE)],
            out_weight_ref.at[pl.ds(chunk * WIDE, WIDE)],
            sems.at[chunk],
        )
        for chunk in range(3)
    ]
    qkv_copies = [
        pltpu.make_async_copy(
            w_qkv_ref.at[pl.ds(chunk * WIDE, WIDE)],
            weight_ref.at[pl.ds(chunk * WIDE, WIDE)],
            sems.at[3 + chunk],
        )
        for chunk in range(3)
    ]
    for copy in out_copies + qkv_copies:
        copy.start()
    term = lane_index(3 * 8 * OUT_ROWS)
    kind, inner = term // (8 * OUT_ROWS), term % (8 * OUT_ROWS)
    row = inner % OUT_ROWS
    at = TOKEN_ROWS + kind * OUT_ROWS + jnp.where(kind == 2, row // 4, row)
    place_ref[...] = pick((8 * CHUNK, 3 * 8 * OUT_ROWS), inner // OUT_ROWS * CHUNK + at, 0)
    masked = masked_ref[...]
    for copy in out_copies:
        copy.wait()
    for chunk in range(3):
        columns = slice(chunk * WIDE, (chunk + 1) * WIDE)
        head_ref[:, columns] = dot(masked, out_weight_ref[columns, :], NT).astype(BF)
    patch = lane_patch()
    for head in range(H):
        base, width, inside = window(head)
        queries = only(inside, joined_ref[:, base : base + width])
        keys_in = joined_ref[:, D + base : D + base + width]
        values = joined_ref[:, 2 * D + base : 2 * D + base + width]
        head_grad = only(inside, head_ref[:, base : base + width])
        probs = probs_ref[head]
        prob_grad = diagonal(dot(values, head_grad, NT), patch)
        inner_sum = jnp.sum(probs * prob_grad, axis=0, keepdims=True)
        score_grad = spread(probs * (prob_grad - inner_sum) * SCALE, patch)
        parts = (
            dot(score_grad, keys_in, TN).astype(BF),
            dot(score_grad, queries).astype(BF),
            dot(spread(probs, patch), head_grad).astype(BF),
        )
        for index, part in enumerate(parts):
            at = index * D + base
            if head == 0:
                grad_ref[:, at : at + width] = part
            else:
                grad_ref[:, at : at + width] = jnp.where(inside, part, grad_ref[:, at : at + width])
    pieces = []
    for copy in qkv_copies:
        copy.wait()
    for chunk in range(3):
        rows = slice(chunk * WIDE, (chunk + 1) * WIDE)
        pieces.append(dot(grad_ref[...], weight_ref[rows, :], NT))
    normed_grad = jnp.concatenate(pieces, axis=1)
    normalized, inverse = row_stats(tokens_ref[...])
    mean_grad = jnp.mean(normed_grad, axis=-1, keepdims=True)
    mean_cross = jnp.mean(normed_grad * normalized, axis=-1, keepdims=True)
    d_tokens = (
        masked.astype(F32) + inverse * (normed_grad - mean_grad - normalized * mean_cross)
    ).astype(BF)
    piece = lane_index(576)
    target = piece % 16 * CHUNK + piece // 64 * PATCHES + piece % 64 // 16
    chooser = pick((16 * CHUNK, 576), target, 0)
    for half in range(2):
        stacked = jnp.concatenate(
            [
                d_tokens[p * SLOTS + half * 16 : p * SLOTS + half * 16 + 16, c * 128 : (c + 1) * 128]
                for c in range(9)
                for p in range(PATCHES)
            ],
            axis=0,
        )
        packed_ref[half * 16 * CHUNK : (half + 1) * 16 * CHUNK, :] = dot(chooser, stacked).astype(BF)


def weight_kernel(other, core_ref, gathered_ref, after_ref, terms_ref):
    core = 1 - core_ref[0] if other else core_ref[0]
    start = pl.multiple_of(core * HALF, HALF)
    attended = jnp.concatenate([gathered_ref[i, pl.ds(start, HALF), :] for i in range(4)], axis=1)
    masked = jnp.concatenate([gathered_ref[i, D:, :] for i in range(4)], axis=1)
    masked = jnp.concatenate([masked[:256]] + [masked[256:]] * 4, axis=0)
    terms_ref[...] = dot(attended, masked, NT).astype(terms_ref.dtype)


def merge_kernel(rows_ref, keep_ref, got_ref, place_ref, merged_ref):
    terms = keep_ref[...] + got_ref[...].astype(F32)
    row = row_index(SLOTS * OUT_ROWS) % OUT_ROWS
    last = jnp.where(row % 4 == lane_index(128) // 32, terms[:, 256:], 0.0)
    blocks = [block.astype(BF) for block in (terms[:, :128], terms[:, 128:256], last)]
    for group in range(4):
        rows = slice(group * 8 * OUT_ROWS, (group + 1) * 8 * OUT_ROWS)
        stacked = jnp.concatenate([block[rows] for block in blocks], axis=0)
        out = slice(group * 8 * CHUNK, (group + 1) * 8 * CHUNK)
        merged_ref[out, :] = (
            dot(place_ref[...], stacked) + rows_ref[out, :].astype(F32)
        ).astype(BF)


def unpack_kernel(merged_ref, d_tokens_ref, d_w_ref, total_ref):
    piece = row_index(288)
    row = piece % 32
    source = row // PATCHES * CHUNK + piece // 32 * PATCHES + row % PATCHES
    chooser = pick((288, 8 * CHUNK), source, 1)
    for group in range(4):
        rows = dot(chooser, merged_ref[group * 8 * CHUNK : (group + 1) * 8 * CHUNK, :]).astype(BF)
        for block in range(9):
            d_tokens_ref[group * 32 : (group + 1) * 32, block * 128 : (block + 1) * 128] = rows[
                block * 32 : (block + 1) * 32
            ]
    merged = merged_ref[...].astype(F32).reshape(SLOTS, CHUNK, 128)
    total_ref[...] = jnp.sum(merged[:, 32:], axis=0)
    first = TOKEN_ROWS - 32
    d_w_ref[:, :128] = total_ref[first : first + OUT_ROWS, :]
    d_w_ref[:, 128:256] = total_ref[first + OUT_ROWS : first + 2 * OUT_ROWS, :]
    for row in range(OUT_ROWS):
        at = first + 2 * OUT_ROWS + row // 4
        lanes = slice(row % 4 * 32, row % 4 * 32 + 32)
        d_w_ref[row : row + 1, 256:] = total_ref[at : at + 1, lanes]


def body(tokens, d_out, frames, frame_order, w_qkv, w_out):
    core = lax.axis_index("core")
    shape = jax.ShapeDtypeStruct
    live = (frame_order[0] < frames[0]).astype(F32)
    packed = call(
        pack_kernel,
        shape((256, D), BF),
        (tokens[0], d_out[0]),
        scratch=(pltpu.VMEM((256, D), BF), pltpu.SemaphoreType.DMA((2,))),
        limit=60,
        far=(0, 1),
    )
    arrived = lax.all_to_all(
        packed.reshape(SLOTS, 8, D), ("y", "z"), split_axis=0, concat_axis=0, tiled=True
    ).reshape(256, D)
    firsts = tuple(w_qkv[:, kind * D : kind * D + WIDE] for kind in range(3))
    kept, masked, joined, probs, sends = call(
        forward_kernel,
        (
            shape((ROWS, D), BF),
            shape((ROWS, D), BF),
            shape((ROWS, 3 * D), BF),
            shape((H, SLOTS, ROWS), F32),
            shape((4, PAYLOAD, ROWS), BF),
        ),
        (core.reshape(1), arrived, live[:, None]) + firsts + (w_qkv,),
        scratch=(
            pltpu.VMEM((D, ROWS), BF),
            pltpu.VMEM((D, ROWS), F32),
            pltpu.VMEM((D, ROWS), F32),
            pltpu.VMEM((D, ROWS), BF),
            pltpu.VMEM((D, 3 * D), BF),
            pltpu.SemaphoreType.DMA((6,)),
            pltpu.SemaphoreType.DMA((8,)),
        ),
        smem=(0,),
        far=(6,),
        far_out=(4,),
        limit=52,
        flops=int(2e9),
        data=int(14e6),
    )
    gathered = lax.all_to_all(sends, "dp", split_axis=0, concat_axis=0, tiled=True)
    rows, places = call(
        backward_kernel,
        (shape((SLOTS * CHUNK, 128), BF), shape((8 * CHUNK, 3 * 8 * OUT_ROWS), BF)),
        (kept, masked, joined, probs, w_qkv, w_out),
        scratch=(
            pltpu.VMEM((ROWS, 3 * D), BF),
            pltpu.VMEM((ROWS, D), BF),
            pltpu.VMEM((D, 3 * D), BF),
            pltpu.VMEM((D, D), BF),
            pltpu.SemaphoreType.DMA((6,)),
        ),
        far=(4, 5),
        limit=52,
        flops=int(3e9),
        data=int(16e6),
    )
    send = call(
        functools.partial(weight_kernel, True),
        shape((SLOTS * OUT_ROWS, WIDE), BF),
        (core.reshape(1), gathered, rows),
        smem=(0,),
        far=(2,),
        flops=int(1e9),
        data=int(4e6),
    )
    got = lax.ppermute(send, "core", [(0, 1), (1, 0)])
    keep = call(
        functools.partial(weight_kernel, False),
        shape((SLOTS * OUT_ROWS, WIDE), F32),
        (core.reshape(1), gathered, send),
        smem=(0,),
        far=(2,),
        flops=int(1e9),
        data=int(4e6),
    )
    merged = call(
        merge_kernel, shape((SLOTS * CHUNK, 128), BF), (rows, keep, got, places), limit=16
    )
    returned = lax.all_to_all(
        merged.reshape(SLOTS, CHUNK, 128), ("y", "z"), split_axis=0, concat_axis=0, tiled=True
    ).reshape(SLOTS * CHUNK, 128)
    d_tokens, d_w = call(
        unpack_kernel,
        (shape((ROWS, D), BF), shape((OUT_ROWS, COLS), F32)),
        (returned,),
        scratch=(pltpu.VMEM((CHUNK - 32, 128), F32),),
        limit=16,
    )
    return d_tokens[None], d_w


def solution(mesh):
    fine = Mesh(mesh.devices.reshape(4, 4, 8, 2), ("dp", "y", "z", "core"))
    seq = ("y", "z", "core")
    placed = (P("dp", seq, None), P("dp", seq, None), P("dp"), P("dp", None), P(), P())
    return jax.shard_map(
        body,
        mesh=fine,
        in_specs=placed,
        out_specs=(P("dp", seq, None), P(seq, "dp")),
        check_vma=False,
    )
```

```python
import functools
import math

import jax
import jax.numpy as jnp
from jax import lax
from jax.experimental import pallas as pl
from jax.experimental.pallas import tpu as pltpu
from jax.sharding import Mesh, PartitionSpec as P

H = 16
D = 1152
E = D // H
SLOTS = 32
PATCHES = 4
ROWS = SLOTS * PATCHES
SCALE = 1.0 / math.sqrt(E)
BF = jnp.bfloat16
F32 = jnp.float32
MIB = 1024 * 1024
COLS = 288
WIDE = 384
OUT_ROWS = 18
CHUNK = 80
TOKEN_ROWS = 36
PAYLOAD = D + COLS
HALF = D // 2
EXP_SCALE = SCALE * math.log2(math.e)

NN = (((1,), (0,)), ((), ()))
NT = (((1,), (1,)), ((), ()))
TN = (((0,), (0,)), ((), ()))


def dot(a, b, dims=NN):
    return lax.dot_general(a, b, dims, preferred_element_type=F32)


def whole():
    return pl.BlockSpec(memory_space=pltpu.VMEM)


def call(kernel, out_shape, inputs, scratch=(), limit=32, flops=0, data=0, smem=(), far=()):
    spaces = {i: pltpu.SMEM for i in smem} | {i: pl.ANY for i in far}
    specs = [
        pl.BlockSpec(memory_space=spaces.get(i, pltpu.VMEM)) for i in range(len(inputs))
    ]
    return pl.pallas_call(
        kernel,
        out_shape=out_shape,
        in_specs=specs,
        out_specs=jax.tree.map(lambda _: whole(), out_shape),
        scratch_shapes=list(scratch),
        compiler_params=pltpu.CompilerParams(vmem_limit_bytes=limit * MIB),
        cost_estimate=pl.CostEstimate(flops=flops, bytes_accessed=data, transcendentals=0),
    )(*inputs)


def pick(shape, target, along):
    return (lax.broadcasted_iota(jnp.int32, shape, along) == target).astype(F32).astype(BF)


def row_index(rows):
    return lax.broadcasted_iota(jnp.int32, (rows, 1), 0)


def lane_index(lanes):
    return lax.broadcasted_iota(jnp.int32, (1, lanes), 1)


def source_row(packed):
    inner = packed % 8
    return packed // 8 * PATCHES + inner % PATCHES + jnp.where(inner >= PATCHES, ROWS, 0)


def patch_row(packed):
    inner = packed % 8
    return packed // 8 + inner % PATCHES * SLOTS + jnp.where(inner >= PATCHES, ROWS, 0)


def pack_kernel(tokens_ref, d_out_ref, packed_ref, both_ref, sems):
    copies = [
        pltpu.make_async_copy(ref, both_ref.at[pl.ds(i * ROWS, ROWS)], sems.at[i])
        for i, ref in enumerate((tokens_ref, d_out_ref))
    ]
    for copy in copies:
        copy.start()
    chooser = pick((256, 256), source_row(row_index(256)), 1)
    for copy in copies:
        copy.wait()
    packed_ref[...] = dot(chooser, both_ref[...]).astype(BF)


def row_stats(tokens):
    values = tokens.astype(F32)
    center = values - jnp.mean(values, axis=-1, keepdims=True)
    spread = jnp.mean(center * center, axis=-1, keepdims=True)
    inverse = lax.rsqrt(spread + 1e-06)
    return center * inverse, inverse


def window(head):
    low = head * E
    base = low // 128 * 128
    width = 128 if low + E <= base + 128 else 256
    lane = lax.broadcasted_iota(jnp.int32, (ROWS, width), 1)
    inside = (lane >= low - base) & (lane < low - base + E)
    return base, width, inside


def only(inside, array):
    return jnp.where(inside, array, jnp.zeros_like(array))


def lane_patch():
    return lax.broadcasted_iota(jnp.int32, (SLOTS, ROWS), 1) // SLOTS


def diagonal(full, patch):
    packed = full[:SLOTS]
    for p in range(1, PATCHES):
        packed = jnp.where(patch == p, full[p * SLOTS : (p + 1) * SLOTS], packed)
    return packed


def spread(packed, patch):
    blocks = [jnp.where(patch == p, packed, 0.0) for p in range(PATCHES)]
    return jnp.concatenate(blocks, axis=0).astype(BF)


def forward_kernel(
    place_ref, core_ref, packed_ref, live_ref, first_q_ref, first_k_ref, first_v_ref, w_qkv_ref,
    tokens_ref, masked_ref, joined_ref, probs_ref,
    own_ref, right_far_ref, left_far_ref, right_ref, left_ref,
    turned_ref, values_ref, attended_ref, weight_ref, sems,
):
    spans = [pl.ds(kind * D + chunk * WIDE, WIDE) for chunk in (1, 2) for kind in range(3)]
    copies = [
        pltpu.make_async_copy(w_qkv_ref.at[:, span], weight_ref.at[:, span], sems.at[i])
        for i, span in enumerate(spans)
    ]
    for copy in copies:
        copy.start()
    plain = dot(pick((256, 256), patch_row(lane_index(256)), 0), packed_ref[...])
    tokens = plain[:ROWS].astype(BF)
    tokens_ref[...] = tokens
    normalized, _ = row_stats(tokens)
    normed = normalized.astype(BF)
    live = live_ref[...]
    masked = plain[ROWS:] * jnp.concatenate([live] * PATCHES, axis=0)
    masked_ref[...] = masked.astype(BF)
    for block in range(9):
        lanes = slice(block * 128, (block + 1) * 128)
        turned_ref[lanes, :] = masked[:, lanes].T.astype(BF)
    me = place_ref[0]

    def slice_for(step, first, size):
        start = pl.multiple_of((me + step) % 4 * COLS, 16) + first
        return turned_ref[pl.ds(pl.multiple_of(start, 16), size), :]

    own_ref[D:, :] = slice_for(0, 0, COLS)
    right_ref[HALF:, :] = slice_for(1, 0, COLS)
    left_ref[HALF:, :] = slice_for(3, 0, COLS)
    right_far_ref[HALF:, :] = slice_for(2, 0, COLS // 2)
    left_far_ref[HALF:, :] = slice_for(2, COLS // 2, COLS // 2)
    patch = lane_patch()
    done = 0
    for chunk in range(3):
        if chunk > 0:
            for copy in copies[chunk * 3 - 3 : chunk * 3]:
                copy.wait()
        for kind in range(3):
            columns = slice(kind * D + chunk * WIDE, kind * D + (chunk + 1) * WIDE)
            if chunk == 0:
                weight = (first_q_ref, first_k_ref, first_v_ref)[kind][...]
            else:
                weight = weight_ref[:, columns]
            product = dot(normed, weight)
            joined_ref[:, columns] = product.astype(BF)
            if kind == 2:
                for block in range(3):
                    at = chunk * WIDE + block * 128
                    values_ref[at : at + 128, :] = product[:, block * 128 : (block + 1) * 128].T
        while done < H and window(done)[0] + window(done)[1] <= (chunk + 1) * WIDE:
            head = done
            done += 1
            base, width, inside = window(head)
            queries = only(inside, joined_ref[:, base : base + width])
            keys_in = joined_ref[:, D + base : D + base + width]
            scores = diagonal(dot(keys_in, queries, NT), patch)
            scores = jnp.where(live > 0.5, scores, -1e30)
            top = jnp.max(scores, axis=0, keepdims=True)
            exponent = jnp.exp2((scores - top) * EXP_SCALE)
            probs = exponent / jnp.sum(exponent, axis=0, keepdims=True)
            probs_ref[head] = probs
            rows = slice(head * E, (head + 1) * E)
            attended = dot(values_ref[rows, :].astype(BF), spread(probs, patch))
            for group in range(4):
                at = group % 2 * HALF + head * 2 * OUT_ROWS + group // 2 * OUT_ROWS
                attended_ref[at : at + OUT_ROWS, :] = attended[group * OUT_ROWS : (group + 1) * OUT_ROWS]
    attended = attended_ref[...].astype(BF)
    own_ref[:D, :] = attended
    right_far_ref[:HALF, :] = attended[:HALF]
    left_far_ref[:HALF, :] = attended[HALF:]
    right_ref[:HALF, :] = attended[HALF:]
    left_ref[:HALF, :] = attended[:HALF]


def attention_grad_kernel(masked_ref, joined_ref, probs_ref, w_out_ref, grad_ref, head_ref):
    masked = masked_ref[...]
    for chunk in range(3):
        columns = slice(chunk * WIDE, (chunk + 1) * WIDE)
        head_ref[:, columns] = dot(masked, w_out_ref[columns, :], NT).astype(BF)
    patch = lane_patch()
    for head in range(H):
        base, width, inside = window(head)
        queries = only(inside, joined_ref[:, base : base + width])
        keys_in = joined_ref[:, D + base : D + base + width]
        values = joined_ref[:, 2 * D + base : 2 * D + base + width]
        head_grad = only(inside, head_ref[:, base : base + width])
        probs = probs_ref[head]
        prob_grad = diagonal(dot(values, head_grad, NT), patch)
        inner_sum = jnp.sum(probs * prob_grad, axis=0, keepdims=True)
        score_grad = spread(probs * (prob_grad - inner_sum) * SCALE, patch)
        parts = (
            dot(score_grad, keys_in, TN).astype(BF),
            dot(score_grad, queries).astype(BF),
            dot(spread(probs, patch), head_grad).astype(BF),
        )
        for index, part in enumerate(parts):
            at = index * D + base
            if head == 0:
                grad_ref[:, at : at + width] = part
            else:
                grad_ref[:, at : at + width] = jnp.where(inside, part, grad_ref[:, at : at + width])


def token_grad_kernel(
    tokens_ref, masked_ref, grad_ref, w_qkv_ref, after_ref, also_after_ref, packed_ref, place_ref
):
    term = lane_index(3 * 8 * OUT_ROWS)
    kind, inner = term // (8 * OUT_ROWS), term % (8 * OUT_ROWS)
    row = inner % OUT_ROWS
    at = TOKEN_ROWS + kind * OUT_ROWS + jnp.where(kind == 2, row // 4, row)
    place_ref[...] = pick((8 * CHUNK, 3 * 8 * OUT_ROWS), inner // OUT_ROWS * CHUNK + at, 0)
    masked = masked_ref[...]
    pieces = []
    for chunk in range(3):
        rows = slice(chunk * WIDE, (chunk + 1) * WIDE)
        pieces.append(dot(grad_ref[...], w_qkv_ref[rows, :], NT))
    normed_grad = jnp.concatenate(pieces, axis=1)
    normalized, inverse = row_stats(tokens_ref[...])
    mean_grad = jnp.mean(normed_grad, axis=-1, keepdims=True)
    mean_cross = jnp.mean(normed_grad * normalized, axis=-1, keepdims=True)
    d_tokens = (
        masked.astype(F32) + inverse * (normed_grad - mean_grad - normalized * mean_cross)
    ).astype(BF)
    piece = lane_index(576)
    target = piece % 16 * CHUNK + piece // 64 * PATCHES + piece % 64 // 16
    chooser = pick((16 * CHUNK, 576), target, 0)
    for half in range(2):
        stacked = jnp.concatenate(
            [
                d_tokens[p * SLOTS + half * 16 : p * SLOTS + half * 16 + 16, c * 128 : (c + 1) * 128]
                for c in range(9)
                for p in range(PATCHES)
            ],
            axis=0,
        )
        packed_ref[half * 16 * CHUNK : (half + 1) * 16 * CHUNK, :] = dot(chooser, stacked).astype(BF)


def weight_kernel(
    other, core_ref, own_ref, left_a_ref, left_b_ref, right_a_ref, right_b_ref, far_a_ref, far_b_ref,
    after_ref, terms_ref,
):
    core = 1 - core_ref[0] if other else core_ref[0]
    start = pl.multiple_of(core * HALF, HALF)
    pairs = ((left_a_ref, left_b_ref), (right_b_ref, right_a_ref), (far_a_ref, far_b_ref))
    attended = jnp.concatenate(
        [own_ref[pl.ds(start, HALF), :]]
        + [jnp.where(core == 0, first[:HALF, :], second[:HALF, :]) for first, second in pairs],
        axis=1,
    )
    far = jnp.concatenate([far_a_ref[HALF:, :], far_b_ref[HALF:, :]], axis=0)
    masked = jnp.concatenate(
        [own_ref[D:, :], left_b_ref[HALF:, :], right_b_ref[HALF:, :], far], axis=1
    )
    masked = jnp.concatenate([masked[:256]] + [masked[256:]] * 4, axis=0)
    terms_ref[...] = dot(attended, masked, NT).astype(terms_ref.dtype)


def merge_kernel(rows_ref, keep_ref, got_ref, place_ref, merged_ref):
    terms = keep_ref[...] + got_ref[...].astype(F32)
    row = row_index(SLOTS * OUT_ROWS) % OUT_ROWS
    last = jnp.where(row % 4 == lane_index(128) // 32, terms[:, 256:], 0.0)
    blocks = [block.astype(BF) for block in (terms[:, :128], terms[:, 128:256], last)]
    for group in range(4):
        rows = slice(group * 8 * OUT_ROWS, (group + 1) * 8 * OUT_ROWS)
        stacked = jnp.concatenate([block[rows] for block in blocks], axis=0)
        out = slice(group * 8 * CHUNK, (group + 1) * 8 * CHUNK)
        merged_ref[out, :] = (
            dot(place_ref[...], stacked) + rows_ref[out, :].astype(F32)
        ).astype(BF)


def unpack_kernel(merged_ref, d_tokens_ref, d_w_ref, total_ref):
    piece = row_index(288)
    row = piece % 32
    source = row // PATCHES * CHUNK + piece // 32 * PATCHES + row % PATCHES
    chooser = pick((288, 8 * CHUNK), source, 1)
    for group in range(4):
        rows = dot(chooser, merged_ref[group * 8 * CHUNK : (group + 1) * 8 * CHUNK, :]).astype(BF)
        for block in range(9):
            d_tokens_ref[group * 32 : (group + 1) * 32, block * 128 : (block + 1) * 128] = rows[
                block * 32 : (block + 1) * 32
            ]
    merged = merged_ref[...].astype(F32).reshape(SLOTS, CHUNK, 128)
    total_ref[...] = jnp.sum(merged[:, 32:], axis=0)
    first = TOKEN_ROWS - 32
    d_w_ref[:, :128] = total_ref[first : first + OUT_ROWS, :]
    d_w_ref[:, 128:256] = total_ref[first + OUT_ROWS : first + 2 * OUT_ROWS, :]
    for row in range(OUT_ROWS):
        at = first + 2 * OUT_ROWS + row // 4
        lanes = slice(row % 4 * 32, row % 4 * 32 + 32)
        d_w_ref[row : row + 1, 256:] = total_ref[at : at + 1, lanes]


def body(tokens, d_out, frames, frame_order, w_qkv, w_out):
    place = lax.axis_index("dp")
    core = lax.axis_index("core")
    shape = jax.ShapeDtypeStruct
    live = (frame_order[0] < frames[0]).astype(F32)
    packed = call(
        pack_kernel,
        shape((256, D), BF),
        (tokens[0], d_out[0]),
        scratch=(pltpu.VMEM((256, D), BF), pltpu.SemaphoreType.DMA((2,))),
        limit=60,
        far=(0, 1),
    )
    arrived = lax.all_to_all(
        packed.reshape(SLOTS, 8, D), ("y", "z"), split_axis=0, concat_axis=0, tiled=True
    ).reshape(256, D)
    firsts = tuple(w_qkv[:, kind * D : kind * D + WIDE] for kind in range(3))
    kept, masked, joined, probs, own, right_far, left_far, right, left = call(
        forward_kernel,
        (
            shape((ROWS, D), BF),
            shape((ROWS, D), BF),
            shape((ROWS, 3 * D), BF),
            shape((H, SLOTS, ROWS), F32),
            shape((PAYLOAD, ROWS), BF),
        )
        + (shape((HALF + COLS // 2, ROWS), BF),) * 2
        + (shape((HALF + COLS, ROWS), BF),) * 2,
        (place.reshape(1), core.reshape(1), arrived, live[:, None]) + firsts + (w_qkv,),
        scratch=(
            pltpu.VMEM((D, ROWS), BF),
            pltpu.VMEM((D, ROWS), F32),
            pltpu.VMEM((D, ROWS), F32),
            pltpu.VMEM((D, 3 * D), BF),
            pltpu.SemaphoreType.DMA((6,)),
        ),
        smem=(0, 1),
        far=(7,),
        limit=47,
        flops=int(2e9),
        data=int(14e6),
    )
    up = [(i, (i + 1) % 4) for i in range(4)]
    down = [(i, (i + 3) % 4) for i in range(4)]
    left_a = lax.ppermute(right_far, "dp", up)
    right_a = lax.ppermute(left_far, "dp", down)
    left_b = lax.ppermute(right, "dp", up)
    right_b = lax.ppermute(left, "dp", down)
    grads = call(
        attention_grad_kernel,
        shape((ROWS, 3 * D), BF),
        (masked, joined, probs, w_out),
        scratch=(pltpu.VMEM((ROWS, D), BF),),
        limit=24,
        flops=int(3e9),
        data=int(16e6),
    )
    far_a = lax.ppermute(left_a, "dp", up)
    far_b = lax.ppermute(right_a, "dp", down)
    rows, places = call(
        token_grad_kernel,
        (shape((SLOTS * CHUNK, 128), BF), shape((8 * CHUNK, 3 * 8 * OUT_ROWS), BF)),
        (kept, masked, grads, w_qkv, left_a, right_a),
        far=(4, 5),
        limit=24,
        flops=int(3e9),
        data=int(16e6),
    )
    payloads = (own, left_a, left_b, right_a, right_b, far_a, far_b)
    send = call(
        functools.partial(weight_kernel, True),
        shape((SLOTS * OUT_ROWS, WIDE), BF),
        (core.reshape(1),) + payloads + (rows,),
        smem=(0,),
        far=(8,),
        flops=int(1e9),
        data=int(4e6),
    )
    got = lax.ppermute(send, "core", [(0, 1), (1, 0)])
    keep = call(
        functools.partial(weight_kernel, False),
        shape((SLOTS * OUT_ROWS, WIDE), F32),
        (core.reshape(1),) + payloads + (send,),
        smem=(0,),
        far=(8,),
        flops=int(1e9),
        data=int(4e6),
    )
    merged = call(
        merge_kernel, shape((SLOTS * CHUNK, 128), BF), (rows, keep, got, places), limit=16
    )
    returned = lax.all_to_all(
        merged.reshape(SLOTS, CHUNK, 128), ("y", "z"), split_axis=0, concat_axis=0, tiled=True
    ).reshape(SLOTS * CHUNK, 128)
    d_tokens, d_w = call(
        unpack_kernel,
        (shape((ROWS, D), BF), shape((OUT_ROWS, COLS), F32)),
        (returned,),
        scratch=(pltpu.VMEM((CHUNK - 32, 128), F32),),
        limit=16,
    )
    return d_tokens[None], d_w


def solution(mesh):
    fine = Mesh(mesh.devices.reshape(4, 4, 8, 2), ("dp", "y", "z", "core"))
    seq = ("y", "z", "core")
    placed = (P("dp", seq, None), P("dp", seq, None), P("dp"), P("dp", None), P(), P())
    return jax.shard_map(
        body,
        mesh=fine,
        in_specs=placed,
        out_specs=(P("dp", seq, None), P(seq, "dp")),
        check_vma=False,
    )
```

```python
import functools
import math

import jax
import jax.numpy as jnp
from jax import lax
from jax.experimental import pallas as pl
from jax.experimental.pallas import tpu as pltpu
from jax.sharding import Mesh, PartitionSpec as P

H = 16
D = 1152
E = D // H
SLOTS = 32
PATCHES = 4
ROWS = SLOTS * PATCHES
SCALE = 1.0 / math.sqrt(E)
BF = jnp.bfloat16
F32 = jnp.float32
MIB = 1024 * 1024
COLS = 288
WIDE = 384
OUT_ROWS = 18
CHUNK = 80
TOKEN_ROWS = 36
PAYLOAD = D + COLS
HALF = D // 2
EXP_SCALE = SCALE * math.log2(math.e)

NN = (((1,), (0,)), ((), ()))
NT = (((1,), (1,)), ((), ()))
TN = (((0,), (0,)), ((), ()))


def dot(a, b, dims=NN):
    return lax.dot_general(a, b, dims, preferred_element_type=F32)


def call(
    kernel, out_shape, inputs, scratch=(), limit=32, flops=0, data=0, smem=(), far=(), far_out=()
):
    spaces = {i: pltpu.SMEM for i in smem} | {i: pl.ANY for i in far}
    single = isinstance(out_shape, jax.ShapeDtypeStruct)
    shapes = (out_shape,) if single else tuple(out_shape)
    outs = pl.pallas_call(
        kernel,
        out_shape=shapes,
        in_specs=[
            pl.BlockSpec(memory_space=spaces.get(i, pltpu.VMEM)) for i in range(len(inputs))
        ],
        out_specs=tuple(
            pl.BlockSpec(memory_space=pl.ANY if i in far_out else pltpu.VMEM)
            for i in range(len(shapes))
        ),
        scratch_shapes=list(scratch),
        compiler_params=pltpu.CompilerParams(vmem_limit_bytes=limit * MIB),
        cost_estimate=pl.CostEstimate(flops=flops, bytes_accessed=data, transcendentals=0),
    )(*inputs)
    return outs[0] if single else outs


def pick(shape, target, along):
    return (lax.broadcasted_iota(jnp.int32, shape, along) == target).astype(F32).astype(BF)


def row_index(rows):
    return lax.broadcasted_iota(jnp.int32, (rows, 1), 0)


def lane_index(lanes):
    return lax.broadcasted_iota(jnp.int32, (1, lanes), 1)


def source_row(packed):
    inner = packed % 8
    return packed // 8 * PATCHES + inner % PATCHES + jnp.where(inner >= PATCHES, ROWS // 2, 0)


def patch_row(packed):
    inner = packed % 8
    return packed // 8 + inner % PATCHES * SLOTS + jnp.where(inner >= PATCHES, ROWS, 0)


def pack_kernel(tokens_ref, d_out_ref, packed_ref, both_ref, out_ref, sems, out_sems):
    part = ROWS // 2
    copies = [
        pltpu.make_async_copy(
            ref.at[pl.ds(half * part, part)],
            both_ref.at[pl.ds(half * ROWS + i * part, part)],
            sems.at[half * 2 + i],
        )
        for half in range(2)
        for i, ref in enumerate((tokens_ref, d_out_ref))
    ]
    for copy in copies:
        copy.start()
    chooser = pick((ROWS, ROWS), source_row(row_index(ROWS)), 1)
    outs = []
    for half in range(2):
        for copy in copies[half * 2 : half * 2 + 2]:
            copy.wait()
        rows = slice(half * ROWS, (half + 1) * ROWS)
        out_ref[rows, :] = dot(chooser, both_ref[rows, :]).astype(BF)
        span = pl.ds(half * ROWS, ROWS)
        out = pltpu.make_async_copy(out_ref.at[span], packed_ref.at[span], out_sems.at[half])
        out.start()
        outs.append(out)
    for out in outs:
        out.wait()


def row_stats(tokens):
    values = tokens.astype(F32)
    center = values - jnp.mean(values, axis=-1, keepdims=True)
    spread = jnp.mean(center * center, axis=-1, keepdims=True)
    inverse = lax.rsqrt(spread + 1e-06)
    return center * inverse, inverse


def window(head):
    low = head * E
    base = low // 128 * 128
    width = 128 if low + E <= base + 128 else 256
    lane = lax.broadcasted_iota(jnp.int32, (ROWS, width), 1)
    inside = (lane >= low - base) & (lane < low - base + E)
    return base, width, inside


def only(inside, array):
    return jnp.where(inside, array, jnp.zeros_like(array))


def lane_patch():
    return lax.broadcasted_iota(jnp.int32, (SLOTS, ROWS), 1) // SLOTS


def diagonal(full, patch):
    packed = full[:SLOTS]
    for p in range(1, PATCHES):
        packed = jnp.where(patch == p, full[p * SLOTS : (p + 1) * SLOTS], packed)
    return packed


def spread(packed, patch):
    blocks = [jnp.where(patch == p, packed, 0.0) for p in range(PATCHES)]
    return jnp.concatenate(blocks, axis=0).astype(BF)


def forward_kernel(
    place_ref, core_ref, packed_ref, live_ref, first_q_ref, first_k_ref, first_v_ref, w_qkv_ref,
    tokens_ref, masked_ref, joined_ref, probs_ref,
    own_ref, right_far_ref, left_far_ref, right_ref, left_ref,
    turned_ref, values_ref, attended_ref, weight_ref, sems,
):
    spans = [pl.ds(kind * D + chunk * WIDE, WIDE) for chunk in (1, 2) for kind in range(3)]
    copies = [
        pltpu.make_async_copy(w_qkv_ref.at[:, span], weight_ref.at[:, span], sems.at[i])
        for i, span in enumerate(spans)
    ]
    for copy in copies:
        copy.start()
    plain = dot(pick((256, 256), patch_row(lane_index(256)), 0), packed_ref[...])
    tokens = plain[:ROWS].astype(BF)
    tokens_ref[...] = tokens
    normalized, _ = row_stats(tokens)
    normed = normalized.astype(BF)
    live = live_ref[...]
    masked = plain[ROWS:] * jnp.concatenate([live] * PATCHES, axis=0)
    masked_ref[...] = masked.astype(BF)
    for block in range(9):
        lanes = slice(block * 128, (block + 1) * 128)
        turned_ref[lanes, :] = masked[:, lanes].T.astype(BF)
    me = place_ref[0]

    def slice_for(step, first, size):
        start = pl.multiple_of((me + step) % 4 * COLS, 16) + first
        return turned_ref[pl.ds(pl.multiple_of(start, 16), size), :]

    own_ref[D:, :] = slice_for(0, 0, COLS)
    right_ref[HALF:, :] = slice_for(1, 0, COLS)
    left_ref[HALF:, :] = slice_for(3, 0, COLS)
    right_far_ref[HALF:, :] = slice_for(2, 0, COLS // 2)
    left_far_ref[HALF:, :] = slice_for(2, COLS // 2, COLS // 2)
    patch = lane_patch()
    done = 0
    for chunk in range(3):
        if chunk > 0:
            for copy in copies[chunk * 3 - 3 : chunk * 3]:
                copy.wait()
        for kind in range(3):
            columns = slice(kind * D + chunk * WIDE, kind * D + (chunk + 1) * WIDE)
            if chunk == 0:
                weight = (first_q_ref, first_k_ref, first_v_ref)[kind][...]
            else:
                weight = weight_ref[:, columns]
            product = dot(normed, weight)
            joined_ref[:, columns] = product.astype(BF)
            if kind == 2:
                for block in range(3):
                    at = chunk * WIDE + block * 128
                    values_ref[at : at + 128, :] = product[:, block * 128 : (block + 1) * 128].T
        while done < H and window(done)[0] + window(done)[1] <= (chunk + 1) * WIDE:
            head = done
            done += 1
            base, width, inside = window(head)
            queries = only(inside, joined_ref[:, base : base + width])
            keys_in = joined_ref[:, D + base : D + base + width]
            scores = diagonal(dot(keys_in, queries, NT), patch)
            scores = jnp.where(live > 0.5, scores, -1e30)
            top = jnp.max(scores, axis=0, keepdims=True)
            exponent = jnp.exp2((scores - top) * EXP_SCALE)
            probs = exponent / jnp.sum(exponent, axis=0, keepdims=True)
            probs_ref[head] = probs
            rows = slice(head * E, (head + 1) * E)
            attended = dot(values_ref[rows, :].astype(BF), spread(probs, patch))
            for group in range(4):
                at = group % 2 * HALF + head * 2 * OUT_ROWS + group // 2 * OUT_ROWS
                attended_ref[at : at + OUT_ROWS, :] = attended[group * OUT_ROWS : (group + 1) * OUT_ROWS]
    attended = attended_ref[...].astype(BF)
    own_ref[:D, :] = attended
    right_far_ref[:HALF, :] = attended[:HALF]
    left_far_ref[:HALF, :] = attended[HALF:]
    right_ref[:HALF, :] = attended[HALF:]
    left_ref[:HALF, :] = attended[:HALF]


def attention_grad_kernel(masked_ref, joined_ref, probs_ref, w_out_ref, grad_ref, head_ref):
    masked = masked_ref[...]
    for chunk in range(3):
        columns = slice(chunk * WIDE, (chunk + 1) * WIDE)
        head_ref[:, columns] = dot(masked, w_out_ref[columns, :], NT).astype(BF)
    patch = lane_patch()
    for head in range(H):
        base, width, inside = window(head)
        queries = only(inside, joined_ref[:, base : base + width])
        keys_in = joined_ref[:, D + base : D + base + width]
        values = joined_ref[:, 2 * D + base : 2 * D + base + width]
        head_grad = only(inside, head_ref[:, base : base + width])
        probs = probs_ref[head]
        prob_grad = diagonal(dot(values, head_grad, NT), patch)
        inner_sum = jnp.sum(probs * prob_grad, axis=0, keepdims=True)
        score_grad = spread(probs * (prob_grad - inner_sum) * SCALE, patch)
        parts = (
            dot(score_grad, keys_in, TN).astype(BF),
            dot(score_grad, queries).astype(BF),
            dot(spread(probs, patch), head_grad).astype(BF),
        )
        for index, part in enumerate(parts):
            at = index * D + base
            if head == 0:
                grad_ref[:, at : at + width] = part
            else:
                grad_ref[:, at : at + width] = jnp.where(inside, part, grad_ref[:, at : at + width])


def token_grad_kernel(
    tokens_ref, masked_ref, grad_ref, w_qkv_ref, after_ref, also_after_ref, d_tokens_ref
):
    masked = masked_ref[...]
    pieces = []
    for chunk in range(3):
        rows = slice(chunk * WIDE, (chunk + 1) * WIDE)
        pieces.append(dot(grad_ref[...], w_qkv_ref[rows, :], NT))
    normed_grad = jnp.concatenate(pieces, axis=1)
    normalized, inverse = row_stats(tokens_ref[...])
    mean_grad = jnp.mean(normed_grad, axis=-1, keepdims=True)
    mean_cross = jnp.mean(normed_grad * normalized, axis=-1, keepdims=True)
    d_tokens_ref[...] = (
        masked.astype(F32) + inverse * (normed_grad - mean_grad - normalized * mean_cross)
    ).astype(BF)


def weight_terms(core, payloads):
    own_ref, left_a_ref, right_a_ref, left_b_ref, right_b_ref, far_a_ref, far_b_ref = payloads
    start = pl.multiple_of(core * HALF, HALF)
    pairs = ((left_a_ref, left_b_ref), (right_b_ref, right_a_ref), (far_a_ref, far_b_ref))
    attended = jnp.concatenate(
        [own_ref[pl.ds(start, HALF), :]]
        + [jnp.where(core == 0, first[:HALF, :], second[:HALF, :]) for first, second in pairs],
        axis=1,
    )
    far = jnp.concatenate([far_a_ref[HALF:, :], far_b_ref[HALF:, :]], axis=0)
    masked = jnp.concatenate(
        [own_ref[D:, :], left_b_ref[HALF:, :], right_b_ref[HALF:, :], far], axis=1
    )
    masked = jnp.concatenate([masked[:256]] + [masked[256:]] * 4, axis=0)
    return dot(attended, masked, NT)


def send_kernel(core_ref, *refs):
    refs[-1][...] = weight_terms(1 - core_ref[0], refs[:7]).astype(BF)


def keep_kernel(core_ref, *refs):
    d_tokens_ref, _, terms_ref, packed_ref, place_ref = refs[7:]
    terms_ref[...] = weight_terms(core_ref[0], refs[:7])
    term = lane_index(3 * 8 * OUT_ROWS)
    kind, inner = term // (8 * OUT_ROWS), term % (8 * OUT_ROWS)
    row = inner % OUT_ROWS
    at = TOKEN_ROWS + kind * OUT_ROWS + jnp.where(kind == 2, row // 4, row)
    place_ref[...] = pick((8 * CHUNK, 3 * 8 * OUT_ROWS), inner // OUT_ROWS * CHUNK + at, 0)
    piece = lane_index(576)
    target = piece % 16 * CHUNK + piece // 64 * PATCHES + piece % 64 // 16
    chooser = pick((16 * CHUNK, 576), target, 0)
    for half in range(2):
        stacked = jnp.concatenate(
            [
                d_tokens_ref[
                    p * SLOTS + half * 16 : p * SLOTS + half * 16 + 16, c * 128 : (c + 1) * 128
                ]
                for c in range(9)
                for p in range(PATCHES)
            ],
            axis=0,
        )
        packed_ref[half * 16 * CHUNK : (half + 1) * 16 * CHUNK, :] = dot(chooser, stacked).astype(BF)


def merge_kernel(rows_ref, keep_ref, got_ref, place_ref, merged_ref):
    terms = keep_ref[...] + got_ref[...].astype(F32)
    row = row_index(SLOTS * OUT_ROWS) % OUT_ROWS
    last = jnp.where(row % 4 == lane_index(128) // 32, terms[:, 256:], 0.0)
    blocks = [block.astype(BF) for block in (terms[:, :128], terms[:, 128:256], last)]
    for group in range(4):
        rows = slice(group * 8 * OUT_ROWS, (group + 1) * 8 * OUT_ROWS)
        stacked = jnp.concatenate([block[rows] for block in blocks], axis=0)
        out = slice(group * 8 * CHUNK, (group + 1) * 8 * CHUNK)
        merged_ref[out, :] = (
            dot(place_ref[...], stacked) + rows_ref[out, :].astype(F32)
        ).astype(BF)


def unpack_kernel(merged_ref, d_tokens_ref, d_w_ref, rows_ref, total_ref, sems):
    piece = row_index(288)
    row = piece % 32
    source = row // PATCHES * CHUNK + piece // 32 * PATCHES + row % PATCHES
    chooser = pick((288, 8 * CHUNK), source, 1)
    copies = []
    for group in range(4):
        rows = dot(chooser, merged_ref[group * 8 * CHUNK : (group + 1) * 8 * CHUNK, :]).astype(BF)
        for block in range(9):
            rows_ref[group * 32 : (group + 1) * 32, block * 128 : (block + 1) * 128] = rows[
                block * 32 : (block + 1) * 32
            ]
        span = pl.ds(group * 32, 32)
        copy = pltpu.make_async_copy(rows_ref.at[span], d_tokens_ref.at[span], sems.at[group])
        copy.start()
        copies.append(copy)
    merged = merged_ref[...].astype(F32).reshape(SLOTS, CHUNK, 128)
    total_ref[...] = jnp.sum(merged[:, 32:], axis=0)
    first = TOKEN_ROWS - 32
    d_w_ref[:, :128] = total_ref[first : first + OUT_ROWS, :]
    d_w_ref[:, 128:256] = total_ref[first + OUT_ROWS : first + 2 * OUT_ROWS, :]
    for row in range(OUT_ROWS):
        at = first + 2 * OUT_ROWS + row // 4
        lanes = slice(row % 4 * 32, row % 4 * 32 + 32)
        d_w_ref[row : row + 1, 256:] = total_ref[at : at + 1, lanes]
    for copy in copies:
        copy.wait()


def body(tokens, d_out, frames, frame_order, w_qkv, w_out):
    place = lax.axis_index("dp")
    core = lax.axis_index("core")
    shape = jax.ShapeDtypeStruct
    live = (frame_order[0] < frames[0]).astype(F32)
    packed = call(
        pack_kernel,
        shape((256, D), BF),
        (tokens[0], d_out[0]),
        scratch=(
            pltpu.VMEM((256, D), BF),
            pltpu.VMEM((256, D), BF),
            pltpu.SemaphoreType.DMA((4,)),
            pltpu.SemaphoreType.DMA((2,)),
        ),
        limit=60,
        far=(0, 1),
        far_out=(0,),
    )
    arrived = lax.all_to_all(
        packed.reshape(SLOTS, 8, D), ("y", "z"), split_axis=0, concat_axis=0, tiled=True
    ).reshape(256, D)
    firsts = tuple(w_qkv[:, kind * D : kind * D + WIDE] for kind in range(3))
    kept, masked, joined, probs, own, right_far, left_far, right, left = call(
        forward_kernel,
        (
            shape((ROWS, D), BF),
            shape((ROWS, D), BF),
            shape((ROWS, 3 * D), BF),
            shape((H, SLOTS, ROWS), F32),
            shape((PAYLOAD, ROWS), BF),
        )
        + (shape((HALF + COLS // 2, ROWS), BF),) * 2
        + (shape((HALF + COLS, ROWS), BF),) * 2,
        (place.reshape(1), core.reshape(1), arrived, live[:, None]) + firsts + (w_qkv,),
        scratch=(
            pltpu.VMEM((D, ROWS), BF),
            pltpu.VMEM((D, ROWS), F32),
            pltpu.VMEM((D, ROWS), F32),
            pltpu.VMEM((D, 3 * D), BF),
            pltpu.SemaphoreType.DMA((6,)),
        ),
        smem=(0, 1),
        far=(7,),
        limit=47,
        flops=int(2e9),
        data=int(14e6),
    )
    up = [(i, (i + 1) % 4) for i in range(4)]
    down = [(i, (i + 3) % 4) for i in range(4)]
    left_a = lax.ppermute(right_far, "dp", up)
    right_a = lax.ppermute(left_far, "dp", down)
    left_b = lax.ppermute(right, "dp", up)
    right_b = lax.ppermute(left, "dp", down)
    grads = call(
        attention_grad_kernel,
        shape((ROWS, 3 * D), BF),
        (masked, joined, probs, w_out),
        scratch=(pltpu.VMEM((ROWS, D), BF),),
        limit=24,
        flops=int(3e9),
        data=int(16e6),
    )
    far_a = lax.ppermute(left_a, "dp", up)
    far_b = lax.ppermute(right_a, "dp", down)
    d_rows = call(
        token_grad_kernel,
        shape((ROWS, D), BF),
        (kept, masked, grads, w_qkv, left_a, right_a),
        far=(4, 5),
        limit=24,
        flops=int(3e9),
        data=int(16e6),
    )
    payloads = (core.reshape(1), own, left_a, right_a, left_b, right_b, far_a, far_b)
    send = call(
        send_kernel,
        shape((SLOTS * OUT_ROWS, WIDE), BF),
        payloads + (d_rows,),
        smem=(0,),
        far=(8,),
        flops=int(1e9),
        data=int(4e6),
    )
    got = lax.ppermute(send, "core", [(0, 1), (1, 0)])
    keep, rows, places = call(
        keep_kernel,
        (
            shape((SLOTS * OUT_ROWS, WIDE), F32),
            shape((SLOTS * CHUNK, 128), BF),
            shape((8 * CHUNK, 3 * 8 * OUT_ROWS), BF),
        ),
        payloads + (d_rows, send),
        smem=(0,),
        far=(9,),
        flops=int(1e9),
        data=int(4e6),
    )
    merged = call(
        merge_kernel, shape((SLOTS * CHUNK, 128), BF), (rows, keep, got, places), limit=16
    )
    returned = lax.all_to_all(
        merged.reshape(SLOTS, CHUNK, 128), ("y", "z"), split_axis=0, concat_axis=0, tiled=True
    ).reshape(SLOTS * CHUNK, 128)
    d_tokens, d_w = call(
        unpack_kernel,
        (shape((ROWS, D), BF), shape((OUT_ROWS, COLS), F32)),
        (returned,),
        scratch=(
            pltpu.VMEM((ROWS, D), BF),
            pltpu.VMEM((CHUNK - 32, 128), F32),
            pltpu.SemaphoreType.DMA((4,)),
        ),
        limit=16,
        far_out=(0,),
    )
    return d_tokens[None], d_w


def solution(mesh):
    fine = Mesh(mesh.devices.reshape(4, 4, 8, 2), ("dp", "y", "z", "core"))
    seq = ("y", "z", "core")
    placed = (P("dp", seq, None), P("dp", seq, None), P("dp"), P("dp", None), P(), P())
    return jax.shard_map(
        body,
        mesh=fine,
        in_specs=placed,
        out_specs=(P("dp", seq, None), P(seq, "dp")),
        check_vma=False,
    )
```

```python
import functools
import math

import jax
import jax.numpy as jnp
from jax import lax
from jax.experimental import pallas as pl
from jax.experimental.pallas import tpu as pltpu
from jax.sharding import Mesh, PartitionSpec as P

H = 16
D = 1152
E = D // H
SLOTS = 32
PATCHES = 4
ROWS = SLOTS * PATCHES
SCALE = 1.0 / math.sqrt(E)
BF = jnp.bfloat16
F32 = jnp.float32
MIB = 1024 * 1024
COLS = 288
WIDE = 384
OUT_ROWS = 18
CHUNK = 80
TOKEN_ROWS = 36
PAYLOAD = D + COLS
HALF = D // 2
EXP_SCALE = SCALE * math.log2(math.e)

NN = (((1,), (0,)), ((), ()))
NT = (((1,), (1,)), ((), ()))
TN = (((0,), (0,)), ((), ()))


def dot(a, b, dims=NN):
    return lax.dot_general(a, b, dims, preferred_element_type=F32)


def call(
    kernel, out_shape, inputs, scratch=(), limit=32, flops=0, data=0, smem=(), far=(), far_out=()
):
    spaces = {i: pltpu.SMEM for i in smem} | {i: pl.ANY for i in far}
    single = isinstance(out_shape, jax.ShapeDtypeStruct)
    shapes = (out_shape,) if single else tuple(out_shape)
    outs = pl.pallas_call(
        kernel,
        out_shape=shapes,
        in_specs=[
            pl.BlockSpec(memory_space=spaces.get(i, pltpu.VMEM)) for i in range(len(inputs))
        ],
        out_specs=tuple(
            pl.BlockSpec(memory_space=pl.ANY if i in far_out else pltpu.VMEM)
            for i in range(len(shapes))
        ),
        scratch_shapes=list(scratch),
        compiler_params=pltpu.CompilerParams(vmem_limit_bytes=limit * MIB),
        cost_estimate=pl.CostEstimate(flops=flops, bytes_accessed=data, transcendentals=0),
    )(*inputs)
    return outs[0] if single else outs


def pick(shape, target, along):
    return (lax.broadcasted_iota(jnp.int32, shape, along) == target).astype(F32).astype(BF)


def row_index(rows):
    return lax.broadcasted_iota(jnp.int32, (rows, 1), 0)


def lane_index(lanes):
    return lax.broadcasted_iota(jnp.int32, (1, lanes), 1)


def source_row(packed):
    inner = packed % 8
    return packed // 8 * PATCHES + inner % PATCHES + jnp.where(inner >= PATCHES, ROWS // 2, 0)


def patch_row(packed):
    inner = packed % 8
    return packed // 8 + inner % PATCHES * SLOTS + jnp.where(inner >= PATCHES, ROWS, 0)


def pack_kernel(tokens_ref, d_out_ref, packed_ref, both_ref, out_ref, sems, out_sems):
    part = ROWS // 2
    copies = [
        pltpu.make_async_copy(
            ref.at[pl.ds(half * part, part)],
            both_ref.at[pl.ds(half * ROWS + i * part, part)],
            sems.at[half * 2 + i],
        )
        for half in range(2)
        for i, ref in enumerate((tokens_ref, d_out_ref))
    ]
    for copy in copies:
        copy.start()
    chooser = pick((ROWS, ROWS), source_row(row_index(ROWS)), 1)
    outs = []
    for half in range(2):
        for copy in copies[half * 2 : half * 2 + 2]:
            copy.wait()
        rows = slice(half * ROWS, (half + 1) * ROWS)
        out_ref[rows, :] = dot(chooser, both_ref[rows, :]).astype(BF)
        span = pl.ds(half * ROWS, ROWS)
        out = pltpu.make_async_copy(out_ref.at[span], packed_ref.at[span], out_sems.at[half])
        out.start()
        outs.append(out)
    for out in outs:
        out.wait()


def row_stats(tokens):
    values = tokens.astype(F32)
    center = values - jnp.mean(values, axis=-1, keepdims=True)
    spread = jnp.mean(center * center, axis=-1, keepdims=True)
    inverse = lax.rsqrt(spread + 1e-06)
    return center * inverse, inverse


def window(head):
    low = head * E
    base = low // 128 * 128
    width = 128 if low + E <= base + 128 else 256
    lane = lax.broadcasted_iota(jnp.int32, (ROWS, width), 1)
    inside = (lane >= low - base) & (lane < low - base + E)
    return base, width, inside


def only(inside, array):
    return jnp.where(inside, array, jnp.zeros_like(array))


def lane_patch():
    return lax.broadcasted_iota(jnp.int32, (SLOTS, ROWS), 1) // SLOTS


def diagonal(full, patch):
    packed = full[:SLOTS]
    for p in range(1, PATCHES):
        packed = jnp.where(patch == p, full[p * SLOTS : (p + 1) * SLOTS], packed)
    return packed


def spread(packed, patch):
    blocks = [jnp.where(patch == p, packed, 0.0) for p in range(PATCHES)]
    return jnp.concatenate(blocks, axis=0).astype(BF)


def forward_kernel(
    place_ref, core_ref, packed_ref, live_ref, first_q_ref, first_k_ref, first_v_ref, w_qkv_ref,
    tokens_ref, masked_ref, joined_ref, probs_ref,
    own_ref, right_far_ref, left_far_ref, right_ref, left_ref,
    turned_ref, values_ref, attended_ref, weight_ref, sems,
):
    spans = [pl.ds(kind * D + chunk * WIDE, WIDE) for chunk in (1, 2) for kind in range(3)]
    copies = [
        pltpu.make_async_copy(w_qkv_ref.at[:, span], weight_ref.at[:, span], sems.at[i])
        for i, span in enumerate(spans)
    ]
    for copy in copies:
        copy.start()
    plain = dot(pick((256, 256), patch_row(lane_index(256)), 0), packed_ref[...])
    tokens = plain[:ROWS].astype(BF)
    tokens_ref[...] = tokens
    normalized, _ = row_stats(tokens)
    normed = normalized.astype(BF)
    live = live_ref[...]
    masked = plain[ROWS:] * jnp.concatenate([live] * PATCHES, axis=0)
    masked_ref[...] = masked.astype(BF)
    for block in range(9):
        lanes = slice(block * 128, (block + 1) * 128)
        turned_ref[lanes, :] = masked[:, lanes].T.astype(BF)
    me = place_ref[0]

    def slice_for(step, first, size):
        start = pl.multiple_of((me + step) % 4 * COLS, 16) + first
        return turned_ref[pl.ds(pl.multiple_of(start, 16), size), :]

    own_ref[D:, :] = slice_for(0, 0, COLS)
    right_ref[HALF:, :] = slice_for(1, 0, COLS)
    left_ref[HALF:, :] = slice_for(3, 0, COLS)
    right_far_ref[HALF:, :] = slice_for(2, 0, COLS // 2)
    left_far_ref[HALF:, :] = slice_for(2, COLS // 2, COLS // 2)
    patch = lane_patch()
    done = 0
    for chunk in range(3):
        if chunk > 0:
            for copy in copies[chunk * 3 - 3 : chunk * 3]:
                copy.wait()
        for kind in range(3):
            columns = slice(kind * D + chunk * WIDE, kind * D + (chunk + 1) * WIDE)
            if chunk == 0:
                weight = (first_q_ref, first_k_ref, first_v_ref)[kind][...]
            else:
                weight = weight_ref[:, columns]
            product = dot(normed, weight)
            joined_ref[:, columns] = product.astype(BF)
            if kind == 2:
                for block in range(3):
                    at = chunk * WIDE + block * 128
                    values_ref[at : at + 128, :] = product[:, block * 128 : (block + 1) * 128].T
        while done < H and window(done)[0] + window(done)[1] <= (chunk + 1) * WIDE:
            head = done
            done += 1
            base, width, inside = window(head)
            queries = only(inside, joined_ref[:, base : base + width])
            keys_in = joined_ref[:, D + base : D + base + width]
            scores = diagonal(dot(keys_in, queries, NT), patch)
            scores = jnp.where(live > 0.5, scores, -1e30)
            top = jnp.max(scores, axis=0, keepdims=True)
            exponent = jnp.exp2((scores - top) * EXP_SCALE)
            probs = exponent / jnp.sum(exponent, axis=0, keepdims=True)
            probs_ref[head] = probs
            rows = slice(head * E, (head + 1) * E)
            attended = dot(values_ref[rows, :].astype(BF), spread(probs, patch))
            for group in range(4):
                at = group % 2 * HALF + head * 2 * OUT_ROWS + group // 2 * OUT_ROWS
                attended_ref[at : at + OUT_ROWS, :] = attended[group * OUT_ROWS : (group + 1) * OUT_ROWS]
    attended = attended_ref[...].astype(BF)
    own_ref[:D, :] = attended
    right_far_ref[:HALF, :] = attended[:HALF]
    left_far_ref[:HALF, :] = attended[HALF:]
    right_ref[:HALF, :] = attended[HALF:]
    left_ref[:HALF, :] = attended[:HALF]


def attention_grad_kernel(masked_ref, joined_ref, probs_ref, w_out_ref, grad_ref, head_ref):
    masked = masked_ref[...]
    for chunk in range(3):
        columns = slice(chunk * WIDE, (chunk + 1) * WIDE)
        head_ref[:, columns] = dot(masked, w_out_ref[columns, :], NT).astype(BF)
    patch = lane_patch()
    for head in range(H):
        base, width, inside = window(head)
        queries = only(inside, joined_ref[:, base : base + width])
        keys_in = joined_ref[:, D + base : D + base + width]
        values = joined_ref[:, 2 * D + base : 2 * D + base + width]
        head_grad = only(inside, head_ref[:, base : base + width])
        probs = probs_ref[head]
        prob_grad = diagonal(dot(values, head_grad, NT), patch)
        inner_sum = jnp.sum(probs * prob_grad, axis=0, keepdims=True)
        score_grad = spread(probs * (prob_grad - inner_sum) * SCALE, patch)
        parts = (
            dot(score_grad, keys_in, TN).astype(BF),
            dot(score_grad, queries).astype(BF),
            dot(spread(probs, patch), head_grad).astype(BF),
        )
        for index, part in enumerate(parts):
            at = index * D + base
            if head == 0:
                grad_ref[:, at : at + width] = part
            else:
                grad_ref[:, at : at + width] = jnp.where(inside, part, grad_ref[:, at : at + width])


def token_grad_kernel(
    tokens_ref, masked_ref, grad_ref, w_qkv_ref, after_ref, also_after_ref, d_tokens_ref
):
    masked = masked_ref[...]
    pieces = []
    for chunk in range(3):
        rows = slice(chunk * WIDE, (chunk + 1) * WIDE)
        pieces.append(dot(grad_ref[...], w_qkv_ref[rows, :], NT))
    normed_grad = jnp.concatenate(pieces, axis=1)
    normalized, inverse = row_stats(tokens_ref[...])
    mean_grad = jnp.mean(normed_grad, axis=-1, keepdims=True)
    mean_cross = jnp.mean(normed_grad * normalized, axis=-1, keepdims=True)
    d_tokens_ref[...] = (
        masked.astype(F32) + inverse * (normed_grad - mean_grad - normalized * mean_cross)
    ).astype(BF)


def weight_terms(core, payloads):
    own_ref, left_a_ref, right_a_ref, left_b_ref, right_b_ref, far_a_ref, far_b_ref = payloads
    start = pl.multiple_of(core * HALF, HALF)
    pairs = ((left_a_ref, left_b_ref), (right_b_ref, right_a_ref), (far_a_ref, far_b_ref))
    attended = jnp.concatenate(
        [own_ref[pl.ds(start, HALF), :]]
        + [jnp.where(core == 0, first[:HALF, :], second[:HALF, :]) for first, second in pairs],
        axis=1,
    )
    far = jnp.concatenate([far_a_ref[HALF:, :], far_b_ref[HALF:, :]], axis=0)
    masked = jnp.concatenate(
        [own_ref[D:, :], left_b_ref[HALF:, :], right_b_ref[HALF:, :], far], axis=1
    )
    masked = jnp.concatenate([masked[:256]] + [masked[256:]] * 4, axis=0)
    return dot(attended, masked, NT)


def send_kernel(core_ref, *refs):
    refs[-1][...] = weight_terms(1 - core_ref[0], refs[:7]).astype(BF)


def keep_kernel(core_ref, *refs):
    d_tokens_ref, _, terms_ref, packed_ref, place_ref = refs[7:]
    terms_ref[...] = weight_terms(core_ref[0], refs[:7])
    term = lane_index(3 * 8 * OUT_ROWS)
    kind, inner = term // (8 * OUT_ROWS), term % (8 * OUT_ROWS)
    row = inner % OUT_ROWS
    at = TOKEN_ROWS + kind * OUT_ROWS + jnp.where(kind == 2, row // 4, row)
    place_ref[...] = pick((8 * CHUNK, 3 * 8 * OUT_ROWS), inner // OUT_ROWS * CHUNK + at, 0)
    piece = lane_index(576)
    target = piece % 16 * CHUNK + piece // 64 * PATCHES + piece % 64 // 16
    chooser = pick((16 * CHUNK, 576), target, 0)
    for half in range(2):
        stacked = jnp.concatenate(
            [
                d_tokens_ref[
                    p * SLOTS + half * 16 : p * SLOTS + half * 16 + 16, c * 128 : (c + 1) * 128
                ]
                for c in range(9)
                for p in range(PATCHES)
            ],
            axis=0,
        )
        packed_ref[half * 16 * CHUNK : (half + 1) * 16 * CHUNK, :] = dot(chooser, stacked).astype(BF)


def merge_kernel(rows_ref, keep_ref, got_ref, place_ref, merged_ref):
    terms = keep_ref[...] + got_ref[...].astype(F32)
    row = row_index(SLOTS * OUT_ROWS) % OUT_ROWS
    last = jnp.where(row % 4 == lane_index(128) // 32, terms[:, 256:], 0.0)
    blocks = [block.astype(BF) for block in (terms[:, :128], terms[:, 128:256], last)]
    for group in range(4):
        rows = slice(group * 8 * OUT_ROWS, (group + 1) * 8 * OUT_ROWS)
        stacked = jnp.concatenate([block[rows] for block in blocks], axis=0)
        out = slice(group * 8 * CHUNK, (group + 1) * 8 * CHUNK)
        merged_ref[out, :] = (
            dot(place_ref[...], stacked) + rows_ref[out, :].astype(F32)
        ).astype(BF)


def unpack_kernel(merged_ref, d_tokens_ref, d_w_ref, total_ref):
    piece = row_index(288)
    row = piece % 32
    source = row // PATCHES * CHUNK + piece // 32 * PATCHES + row % PATCHES
    chooser = pick((288, 8 * CHUNK), source, 1)
    for group in range(4):
        rows = dot(chooser, merged_ref[group * 8 * CHUNK : (group + 1) * 8 * CHUNK, :]).astype(BF)
        for block in range(9):
            d_tokens_ref[group * 32 : (group + 1) * 32, block * 128 : (block + 1) * 128] = rows[
                block * 32 : (block + 1) * 32
            ]
    merged = merged_ref[...].astype(F32).reshape(SLOTS, CHUNK, 128)
    total_ref[...] = jnp.sum(merged[:, 32:], axis=0)
    first = TOKEN_ROWS - 32
    d_w_ref[:, :128] = total_ref[first : first + OUT_ROWS, :]
    d_w_ref[:, 128:256] = total_ref[first + OUT_ROWS : first + 2 * OUT_ROWS, :]
    for row in range(OUT_ROWS):
        at = first + 2 * OUT_ROWS + row // 4
        lanes = slice(row % 4 * 32, row % 4 * 32 + 32)
        d_w_ref[row : row + 1, 256:] = total_ref[at : at + 1, lanes]


def body(tokens, d_out, frames, frame_order, w_qkv, w_out):
    place = lax.axis_index("dp")
    core = lax.axis_index("core")
    shape = jax.ShapeDtypeStruct
    live = (frame_order[0] < frames[0]).astype(F32)
    packed = call(
        pack_kernel,
        shape((256, D), BF),
        (tokens[0], d_out[0]),
        scratch=(
            pltpu.VMEM((256, D), BF),
            pltpu.VMEM((256, D), BF),
            pltpu.SemaphoreType.DMA((4,)),
            pltpu.SemaphoreType.DMA((2,)),
        ),
        limit=60,
        far=(0, 1),
        far_out=(0,),
    )
    arrived = lax.all_to_all(
        packed.reshape(SLOTS, 8, D), ("y", "z"), split_axis=0, concat_axis=0, tiled=True
    ).reshape(256, D)
    firsts = tuple(w_qkv[:, kind * D : kind * D + WIDE] for kind in range(3))
    kept, masked, joined, probs, own, right_far, left_far, right, left = call(
        forward_kernel,
        (
            shape((ROWS, D), BF),
            shape((ROWS, D), BF),
            shape((ROWS, 3 * D), BF),
            shape((H, SLOTS, ROWS), F32),
            shape((PAYLOAD, ROWS), BF),
        )
        + (shape((HALF + COLS // 2, ROWS), BF),) * 2
        + (shape((HALF + COLS, ROWS), BF),) * 2,
        (place.reshape(1), core.reshape(1), arrived, live[:, None]) + firsts + (w_qkv,),
        scratch=(
            pltpu.VMEM((D, ROWS), BF),
            pltpu.VMEM((D, ROWS), F32),
            pltpu.VMEM((D, ROWS), F32),
            pltpu.VMEM((D, 3 * D), BF),
            pltpu.SemaphoreType.DMA((6,)),
        ),
        smem=(0, 1),
        far=(7,),
        limit=47,
        flops=int(2e9),
        data=int(14e6),
    )
    up = [(i, (i + 1) % 4) for i in range(4)]
    down = [(i, (i + 3) % 4) for i in range(4)]
    left_a = lax.ppermute(right_far, "dp", up)
    right_a = lax.ppermute(left_far, "dp", down)
    left_b = lax.ppermute(right, "dp", up)
    right_b = lax.ppermute(left, "dp", down)
    grads = call(
        attention_grad_kernel,
        shape((ROWS, 3 * D), BF),
        (masked, joined, probs, w_out),
        scratch=(pltpu.VMEM((ROWS, D), BF),),
        limit=24,
        flops=int(3e9),
        data=int(16e6),
    )
    far_a = lax.ppermute(left_a, "dp", up)
    far_b = lax.ppermute(right_a, "dp", down)
    d_rows = call(
        token_grad_kernel,
        shape((ROWS, D), BF),
        (kept, masked, grads, w_qkv, left_a, right_a),
        far=(4, 5),
        limit=24,
        flops=int(3e9),
        data=int(16e6),
    )
    payloads = (core.reshape(1), own, left_a, right_a, left_b, right_b, far_a, far_b)
    send = call(
        send_kernel,
        shape((SLOTS * OUT_ROWS, WIDE), BF),
        payloads + (d_rows,),
        smem=(0,),
        far=(8,),
        flops=int(1e9),
        data=int(4e6),
    )
    got = lax.ppermute(send, "core", [(0, 1), (1, 0)])
    keep, rows, places = call(
        keep_kernel,
        (
            shape((SLOTS * OUT_ROWS, WIDE), F32),
            shape((SLOTS * CHUNK, 128), BF),
            shape((8 * CHUNK, 3 * 8 * OUT_ROWS), BF),
        ),
        payloads + (d_rows, send),
        smem=(0,),
        far=(9,),
        flops=int(1e9),
        data=int(4e6),
    )
    merged = call(
        merge_kernel, shape((SLOTS * CHUNK, 128), BF), (rows, keep, got, places), limit=16
    )
    returned = lax.all_to_all(
        merged.reshape(SLOTS, CHUNK, 128), ("y", "z"), split_axis=0, concat_axis=0, tiled=True
    ).reshape(SLOTS * CHUNK, 128)
    d_tokens, d_w = call(
        unpack_kernel,
        (shape((ROWS, D), BF), shape((OUT_ROWS, COLS), F32)),
        (returned,),
        scratch=(pltpu.VMEM((CHUNK - 32, 128), F32),),
        limit=16,
    )
    return d_tokens[None], d_w


def solution(mesh):
    fine = Mesh(mesh.devices.reshape(4, 4, 8, 2), ("dp", "y", "z", "core"))
    seq = ("y", "z", "core")
    placed = (P("dp", seq, None), P("dp", seq, None), P("dp"), P("dp", None), P(), P())
    return jax.shard_map(
        body,
        mesh=fine,
        in_specs=placed,
        out_specs=(P("dp", seq, None), P(seq, "dp")),
        check_vma=False,
    )
```

```python
import functools
import math

import jax
import jax.numpy as jnp
from jax import lax
from jax.experimental import pallas as pl
from jax.experimental.pallas import tpu as pltpu
from jax.sharding import Mesh, PartitionSpec as P

H = 16
D = 1152
E = D // H
SLOTS = 32
PATCHES = 4
ROWS = SLOTS * PATCHES
SCALE = 1.0 / math.sqrt(E)
BF = jnp.bfloat16
F32 = jnp.float32
MIB = 1024 * 1024
COLS = 288
WIDE = 384
OUT_ROWS = 18
CHUNK = 80
TOKEN_ROWS = 36
PAYLOAD = D + COLS
HALF = D // 2
EXP_SCALE = SCALE * math.log2(math.e)

NN = (((1,), (0,)), ((), ()))
NT = (((1,), (1,)), ((), ()))
TN = (((0,), (0,)), ((), ()))


def dot(a, b, dims=NN):
    return lax.dot_general(a, b, dims, preferred_element_type=F32)


def call(
    kernel, out_shape, inputs, scratch=(), limit=32, flops=0, data=0, smem=(), far=(), far_out=()
):
    spaces = {i: pltpu.SMEM for i in smem} | {i: pl.ANY for i in far}
    single = isinstance(out_shape, jax.ShapeDtypeStruct)
    shapes = (out_shape,) if single else tuple(out_shape)
    outs = pl.pallas_call(
        kernel,
        out_shape=shapes,
        in_specs=[
            pl.BlockSpec(memory_space=spaces.get(i, pltpu.VMEM)) for i in range(len(inputs))
        ],
        out_specs=tuple(
            pl.BlockSpec(memory_space=pl.ANY if i in far_out else pltpu.VMEM)
            for i in range(len(shapes))
        ),
        scratch_shapes=list(scratch),
        compiler_params=pltpu.CompilerParams(vmem_limit_bytes=limit * MIB),
        cost_estimate=pl.CostEstimate(flops=flops, bytes_accessed=data, transcendentals=0),
    )(*inputs)
    return outs[0] if single else outs


def pick(shape, target, along):
    return (lax.broadcasted_iota(jnp.int32, shape, along) == target).astype(F32).astype(BF)


def row_index(rows):
    return lax.broadcasted_iota(jnp.int32, (rows, 1), 0)


def lane_index(lanes):
    return lax.broadcasted_iota(jnp.int32, (1, lanes), 1)


def source_row(packed):
    inner = packed % 8
    return packed // 8 * PATCHES + inner % PATCHES + jnp.where(inner >= PATCHES, ROWS // 2, 0)


def patch_row(packed):
    inner = packed % 8
    return packed // 8 + inner % PATCHES * SLOTS + jnp.where(inner >= PATCHES, ROWS, 0)


def pack_kernel(tokens_ref, d_out_ref, packed_ref, both_ref, out_ref, sems, out_sems):
    part = ROWS // 2
    copies = [
        pltpu.make_async_copy(
            ref.at[pl.ds(half * part, part)],
            both_ref.at[pl.ds(half * ROWS + i * part, part)],
            sems.at[half * 2 + i],
        )
        for half in range(2)
        for i, ref in enumerate((tokens_ref, d_out_ref))
    ]
    for copy in copies:
        copy.start()
    chooser = pick((ROWS, ROWS), source_row(row_index(ROWS)), 1)
    outs = []
    for half in range(2):
        for copy in copies[half * 2 : half * 2 + 2]:
            copy.wait()
        rows = slice(half * ROWS, (half + 1) * ROWS)
        out_ref[rows, :] = dot(chooser, both_ref[rows, :]).astype(BF)
        span = pl.ds(half * ROWS, ROWS)
        out = pltpu.make_async_copy(out_ref.at[span], packed_ref.at[span], out_sems.at[half])
        out.start()
        outs.append(out)
    for out in outs:
        out.wait()


def row_stats(tokens):
    values = tokens.astype(F32)
    center = values - jnp.mean(values, axis=-1, keepdims=True)
    spread = jnp.mean(center * center, axis=-1, keepdims=True)
    inverse = lax.rsqrt(spread + 1e-06)
    return center * inverse, inverse


def window(head):
    low = head * E
    base = low // 128 * 128
    width = 128 if low + E <= base + 128 else 256
    lane = lax.broadcasted_iota(jnp.int32, (ROWS, width), 1)
    inside = (lane >= low - base) & (lane < low - base + E)
    return base, width, inside


def only(inside, array):
    return jnp.where(inside, array, jnp.zeros_like(array))


def lane_patch():
    return lax.broadcasted_iota(jnp.int32, (SLOTS, ROWS), 1) // SLOTS


def diagonal(full, patch):
    packed = full[:SLOTS]
    for p in range(1, PATCHES):
        packed = jnp.where(patch == p, full[p * SLOTS : (p + 1) * SLOTS], packed)
    return packed


def spread(packed, patch):
    blocks = [jnp.where(patch == p, packed, 0.0) for p in range(PATCHES)]
    return jnp.concatenate(blocks, axis=0).astype(BF)


def forward_kernel(
    place_ref, core_ref, packed_ref, live_ref, first_q_ref, first_k_ref, first_v_ref, w_qkv_ref,
    tokens_ref, masked_ref, joined_ref, probs_ref,
    own_ref, right_far_ref, left_far_ref, right_ref, left_ref,
    turned_ref, values_ref, attended_ref, weight_ref, sems,
):
    spans = [pl.ds(kind * D + chunk * WIDE, WIDE) for chunk in (1, 2) for kind in range(3)]
    copies = [
        pltpu.make_async_copy(w_qkv_ref.at[:, span], weight_ref.at[:, span], sems.at[i])
        for i, span in enumerate(spans)
    ]
    for copy in copies:
        copy.start()
    plain = dot(pick((256, 256), patch_row(lane_index(256)), 0), packed_ref[...])
    tokens = plain[:ROWS].astype(BF)
    tokens_ref[...] = tokens
    normalized, _ = row_stats(tokens)
    normed = normalized.astype(BF)
    live = live_ref[...]
    masked = plain[ROWS:] * jnp.concatenate([live] * PATCHES, axis=0)
    masked_ref[...] = masked.astype(BF)
    for block in range(9):
        lanes = slice(block * 128, (block + 1) * 128)
        turned_ref[lanes, :] = masked[:, lanes].T.astype(BF)
    me = place_ref[0]

    def slice_for(step, first, size):
        start = pl.multiple_of((me + step) % 4 * COLS, 16) + first
        return turned_ref[pl.ds(pl.multiple_of(start, 16), size), :]

    own_ref[D:, :] = slice_for(0, 0, COLS)
    right_ref[HALF:, :] = slice_for(1, 0, COLS)
    left_ref[HALF:, :] = slice_for(3, 0, COLS)
    right_far_ref[HALF:, :] = slice_for(2, 0, COLS // 2)
    left_far_ref[HALF:, :] = slice_for(2, COLS // 2, COLS // 2)
    patch = lane_patch()
    done = 0
    for chunk in range(3):
        if chunk > 0:
            for copy in copies[chunk * 3 - 3 : chunk * 3]:
                copy.wait()
        for kind in range(3):
            columns = slice(kind * D + chunk * WIDE, kind * D + (chunk + 1) * WIDE)
            if chunk == 0:
                weight = (first_q_ref, first_k_ref, first_v_ref)[kind][...]
            else:
                weight = weight_ref[:, columns]
            product = dot(normed, weight)
            joined_ref[:, columns] = product.astype(BF)
            if kind == 2:
                for block in range(3):
                    at = chunk * WIDE + block * 128
                    values_ref[at : at + 128, :] = product[:, block * 128 : (block + 1) * 128].T
        while done < H and window(done)[0] + window(done)[1] <= (chunk + 1) * WIDE:
            head = done
            done += 1
            base, width, inside = window(head)
            queries = only(inside, joined_ref[:, base : base + width])
            keys_in = joined_ref[:, D + base : D + base + width]
            scores = diagonal(dot(keys_in, queries, NT), patch)
            scores = jnp.where(live > 0.5, scores, -1e30)
            top = jnp.max(scores, axis=0, keepdims=True)
            exponent = jnp.exp2((scores - top) * EXP_SCALE)
            probs = exponent / jnp.sum(exponent, axis=0, keepdims=True)
            probs_ref[head] = probs
            rows = slice(head * E, (head + 1) * E)
            attended = dot(values_ref[rows, :].astype(BF), spread(probs, patch))
            for group in range(4):
                at = group % 2 * HALF + head * 2 * OUT_ROWS + group // 2 * OUT_ROWS
                attended_ref[at : at + OUT_ROWS, :] = attended[group * OUT_ROWS : (group + 1) * OUT_ROWS]
    attended = attended_ref[...].astype(BF)
    own_ref[:D, :] = attended
    right_far_ref[:HALF, :] = attended[:HALF]
    left_far_ref[:HALF, :] = attended[HALF:]
    right_ref[:HALF, :] = attended[HALF:]
    left_ref[:HALF, :] = attended[:HALF]


def head_grad_kernel(masked_ref, w_out_ref, head_ref):
    masked = masked_ref[...]
    for chunk in range(3):
        columns = slice(chunk * WIDE, (chunk + 1) * WIDE)
        head_ref[:, columns] = dot(masked, w_out_ref[columns, :], NT).astype(BF)


def attention_grad_kernel(joined_ref, probs_ref, head_ref, after_ref, also_after_ref, grad_ref):
    patch = lane_patch()
    for head in range(H):
        base, width, inside = window(head)
        queries = only(inside, joined_ref[:, base : base + width])
        keys_in = joined_ref[:, D + base : D + base + width]
        values = joined_ref[:, 2 * D + base : 2 * D + base + width]
        head_grad = only(inside, head_ref[:, base : base + width])
        probs = probs_ref[head]
        prob_grad = diagonal(dot(values, head_grad, NT), patch)
        inner_sum = jnp.sum(probs * prob_grad, axis=0, keepdims=True)
        score_grad = spread(probs * (prob_grad - inner_sum) * SCALE, patch)
        parts = (
            dot(score_grad, keys_in, TN).astype(BF),
            dot(score_grad, queries).astype(BF),
            dot(spread(probs, patch), head_grad).astype(BF),
        )
        for index, part in enumerate(parts):
            at = index * D + base
            if head == 0:
                grad_ref[:, at : at + width] = part
            else:
                grad_ref[:, at : at + width] = jnp.where(inside, part, grad_ref[:, at : at + width])


def token_grad_kernel(tokens_ref, masked_ref, grad_ref, w_qkv_ref, d_tokens_ref):
    masked = masked_ref[...]
    pieces = []
    for chunk in range(3):
        rows = slice(chunk * WIDE, (chunk + 1) * WIDE)
        pieces.append(dot(grad_ref[...], w_qkv_ref[rows, :], NT))
    normed_grad = jnp.concatenate(pieces, axis=1)
    normalized, inverse = row_stats(tokens_ref[...])
    mean_grad = jnp.mean(normed_grad, axis=-1, keepdims=True)
    mean_cross = jnp.mean(normed_grad * normalized, axis=-1, keepdims=True)
    d_tokens_ref[...] = (
        masked.astype(F32) + inverse * (normed_grad - mean_grad - normalized * mean_cross)
    ).astype(BF)


def weight_terms(core, payloads):
    own_ref, left_a_ref, right_a_ref, left_b_ref, right_b_ref, far_a_ref, far_b_ref = payloads
    start = pl.multiple_of(core * HALF, HALF)
    pairs = ((left_a_ref, left_b_ref), (right_b_ref, right_a_ref), (far_a_ref, far_b_ref))
    attended = jnp.concatenate(
        [own_ref[pl.ds(start, HALF), :]]
        + [jnp.where(core == 0, first[:HALF, :], second[:HALF, :]) for first, second in pairs],
        axis=1,
    )
    far = jnp.concatenate([far_a_ref[HALF:, :], far_b_ref[HALF:, :]], axis=0)
    masked = jnp.concatenate(
        [own_ref[D:, :], left_b_ref[HALF:, :], right_b_ref[HALF:, :], far], axis=1
    )
    masked = jnp.concatenate([masked[:256]] + [masked[256:]] * 4, axis=0)
    return dot(attended, masked, NT)


def send_kernel(core_ref, *refs):
    refs[-1][...] = weight_terms(1 - core_ref[0], refs[:7]).astype(BF)


def keep_kernel(core_ref, *refs):
    d_tokens_ref, _, terms_ref, packed_ref, place_ref = refs[7:]
    terms_ref[...] = weight_terms(core_ref[0], refs[:7])
    term = lane_index(3 * 8 * OUT_ROWS)
    kind, inner = term // (8 * OUT_ROWS), term % (8 * OUT_ROWS)
    row = inner % OUT_ROWS
    at = TOKEN_ROWS + kind * OUT_ROWS + jnp.where(kind == 2, row // 4, row)
    place_ref[...] = pick((8 * CHUNK, 3 * 8 * OUT_ROWS), inner // OUT_ROWS * CHUNK + at, 0)
    piece = lane_index(576)
    target = piece % 16 * CHUNK + piece // 64 * PATCHES + piece % 64 // 16
    chooser = pick((16 * CHUNK, 576), target, 0)
    for half in range(2):
        stacked = jnp.concatenate(
            [
                d_tokens_ref[
                    p * SLOTS + half * 16 : p * SLOTS + half * 16 + 16, c * 128 : (c + 1) * 128
                ]
                for c in range(9)
                for p in range(PATCHES)
            ],
            axis=0,
        )
        packed_ref[half * 16 * CHUNK : (half + 1) * 16 * CHUNK, :] = dot(chooser, stacked).astype(BF)


def merge_kernel(rows_ref, keep_ref, got_ref, place_ref, merged_ref):
    terms = keep_ref[...] + got_ref[...].astype(F32)
    row = row_index(SLOTS * OUT_ROWS) % OUT_ROWS
    last = jnp.where(row % 4 == lane_index(128) // 32, terms[:, 256:], 0.0)
    blocks = [block.astype(BF) for block in (terms[:, :128], terms[:, 128:256], last)]
    for group in range(4):
        rows = slice(group * 8 * OUT_ROWS, (group + 1) * 8 * OUT_ROWS)
        stacked = jnp.concatenate([block[rows] for block in blocks], axis=0)
        out = slice(group * 8 * CHUNK, (group + 1) * 8 * CHUNK)
        merged_ref[out, :] = (
            dot(place_ref[...], stacked) + rows_ref[out, :].astype(F32)
        ).astype(BF)


def unpack_kernel(merged_ref, d_tokens_ref, d_w_ref, total_ref):
    piece = row_index(288)
    row = piece % 32
    source = row // PATCHES * CHUNK + piece // 32 * PATCHES + row % PATCHES
    chooser = pick((288, 8 * CHUNK), source, 1)
    for group in range(4):
        rows = dot(chooser, merged_ref[group * 8 * CHUNK : (group + 1) * 8 * CHUNK, :]).astype(BF)
        for block in range(9):
            d_tokens_ref[group * 32 : (group + 1) * 32, block * 128 : (block + 1) * 128] = rows[
                block * 32 : (block + 1) * 32
            ]
    merged = merged_ref[...].astype(F32).reshape(SLOTS, CHUNK, 128)
    total_ref[...] = jnp.sum(merged[:, 32:], axis=0)
    first = TOKEN_ROWS - 32
    d_w_ref[:, :128] = total_ref[first : first + OUT_ROWS, :]
    d_w_ref[:, 128:256] = total_ref[first + OUT_ROWS : first + 2 * OUT_ROWS, :]
    for row in range(OUT_ROWS):
        at = first + 2 * OUT_ROWS + row // 4
        lanes = slice(row % 4 * 32, row % 4 * 32 + 32)
        d_w_ref[row : row + 1, 256:] = total_ref[at : at + 1, lanes]


def body(tokens, d_out, frames, frame_order, w_qkv, w_out):
    place = lax.axis_index("dp")
    core = lax.axis_index("core")
    shape = jax.ShapeDtypeStruct
    live = (frame_order[0] < frames[0]).astype(F32)
    packed = call(
        pack_kernel,
        shape((256, D), BF),
        (tokens[0], d_out[0]),
        scratch=(
            pltpu.VMEM((256, D), BF),
            pltpu.VMEM((256, D), BF),
            pltpu.SemaphoreType.DMA((4,)),
            pltpu.SemaphoreType.DMA((2,)),
        ),
        limit=60,
        far=(0, 1),
        far_out=(0,),
    )
    arrived = lax.all_to_all(
        packed.reshape(SLOTS, 8, D), ("y", "z"), split_axis=0, concat_axis=0, tiled=True
    ).reshape(256, D)
    firsts = tuple(w_qkv[:, kind * D : kind * D + WIDE] for kind in range(3))
    kept, masked, joined, probs, own, right_far, left_far, right, left = call(
        forward_kernel,
        (
            shape((ROWS, D), BF),
            shape((ROWS, D), BF),
            shape((ROWS, 3 * D), BF),
            shape((H, SLOTS, ROWS), F32),
            shape((PAYLOAD, ROWS), BF),
        )
        + (shape((HALF + COLS // 2, ROWS), BF),) * 2
        + (shape((HALF + COLS, ROWS), BF),) * 2,
        (place.reshape(1), core.reshape(1), arrived, live[:, None]) + firsts + (w_qkv,),
        scratch=(
            pltpu.VMEM((D, ROWS), BF),
            pltpu.VMEM((D, ROWS), F32),
            pltpu.VMEM((D, ROWS), F32),
            pltpu.VMEM((D, 3 * D), BF),
            pltpu.SemaphoreType.DMA((6,)),
        ),
        smem=(0, 1),
        far=(7,),
        limit=47,
        flops=int(2e9),
        data=int(14e6),
    )
    up = [(i, (i + 1) % 4) for i in range(4)]
    down = [(i, (i + 3) % 4) for i in range(4)]
    left_a = lax.ppermute(right_far, "dp", up)
    right_a = lax.ppermute(left_far, "dp", down)
    left_b = lax.ppermute(right, "dp", up)
    right_b = lax.ppermute(left, "dp", down)
    head_grads = call(
        head_grad_kernel,
        shape((ROWS, D), BF),
        (masked, w_out),
        limit=16,
        flops=int(1e9),
        data=int(4e6),
    )
    far_a = lax.ppermute(left_a, "dp", up)
    far_b = lax.ppermute(right_a, "dp", down)
    grads = call(
        attention_grad_kernel,
        shape((ROWS, 3 * D), BF),
        (joined, probs, head_grads, left_a, right_a),
        far=(3, 4),
        limit=16,
        flops=int(3e9),
        data=int(16e6),
    )
    d_rows = call(
        token_grad_kernel,
        shape((ROWS, D), BF),
        (kept, masked, grads, w_qkv),
        limit=24,
        flops=int(3e9),
        data=int(16e6),
    )
    payloads = (core.reshape(1), own, left_a, right_a, left_b, right_b, far_a, far_b)
    send = call(
        send_kernel,
        shape((SLOTS * OUT_ROWS, WIDE), BF),
        payloads + (d_rows,),
        smem=(0,),
        far=(8,),
        flops=int(1e9),
        data=int(4e6),
    )
    got = lax.ppermute(send, "core", [(0, 1), (1, 0)])
    keep, rows, places = call(
        keep_kernel,
        (
            shape((SLOTS * OUT_ROWS, WIDE), F32),
            shape((SLOTS * CHUNK, 128), BF),
            shape((8 * CHUNK, 3 * 8 * OUT_ROWS), BF),
        ),
        payloads + (d_rows, send),
        smem=(0,),
        far=(9,),
        flops=int(1e9),
        data=int(4e6),
    )
    merged = call(
        merge_kernel, shape((SLOTS * CHUNK, 128), BF), (rows, keep, got, places), limit=16
    )
    returned = lax.all_to_all(
        merged.reshape(SLOTS, CHUNK, 128), ("y", "z"), split_axis=0, concat_axis=0, tiled=True
    ).reshape(SLOTS * CHUNK, 128)
    d_tokens, d_w = call(
        unpack_kernel,
        (shape((ROWS, D), BF), shape((OUT_ROWS, COLS), F32)),
        (returned,),
        scratch=(pltpu.VMEM((CHUNK - 32, 128), F32),),
        limit=16,
    )
    return d_tokens[None], d_w


def solution(mesh):
    fine = Mesh(mesh.devices.reshape(4, 4, 8, 2), ("dp", "y", "z", "core"))
    seq = ("y", "z", "core")
    placed = (P("dp", seq, None), P("dp", seq, None), P("dp"), P("dp", None), P(), P())
    return jax.shard_map(
        body,
        mesh=fine,
        in_specs=placed,
        out_specs=(P("dp", seq, None), P(seq, "dp")),
        check_vma=False,
    )
```

```python
import functools
import math

import jax
import jax.numpy as jnp
from jax import lax
from jax.experimental import pallas as pl
from jax.experimental.pallas import tpu as pltpu
from jax.sharding import Mesh, PartitionSpec as P

H = 16
D = 1152
E = D // H
SLOTS = 32
PATCHES = 4
ROWS = SLOTS * PATCHES
SCALE = 1.0 / math.sqrt(E)
BF = jnp.bfloat16
F32 = jnp.float32
MIB = 1024 * 1024
COLS = 288
WIDE = 384
OUT_ROWS = 18
CHUNK = 80
TOKEN_ROWS = 36
PAYLOAD = D + COLS
HALF = D // 2
EARLY_HEADS = 5
EXP_SCALE = SCALE * math.log2(math.e)

NN = (((1,), (0,)), ((), ()))
NT = (((1,), (1,)), ((), ()))
TN = (((0,), (0,)), ((), ()))


def dot(a, b, dims=NN):
    return lax.dot_general(a, b, dims, preferred_element_type=F32)


def call(
    kernel, out_shape, inputs, scratch=(), limit=32, flops=0, data=0, smem=(), far=(), far_out=()
):
    spaces = {i: pltpu.SMEM for i in smem} | {i: pl.ANY for i in far}
    single = isinstance(out_shape, jax.ShapeDtypeStruct)
    shapes = (out_shape,) if single else tuple(out_shape)
    outs = pl.pallas_call(
        kernel,
        out_shape=shapes,
        in_specs=[
            pl.BlockSpec(memory_space=spaces.get(i, pltpu.VMEM)) for i in range(len(inputs))
        ],
        out_specs=tuple(
            pl.BlockSpec(memory_space=pl.ANY if i in far_out else pltpu.VMEM)
            for i in range(len(shapes))
        ),
        scratch_shapes=list(scratch),
        compiler_params=pltpu.CompilerParams(vmem_limit_bytes=limit * MIB),
        cost_estimate=pl.CostEstimate(flops=flops, bytes_accessed=data, transcendentals=0),
    )(*inputs)
    return outs[0] if single else outs


def pick(shape, target, along):
    return (lax.broadcasted_iota(jnp.int32, shape, along) == target).astype(F32).astype(BF)


def row_index(rows):
    return lax.broadcasted_iota(jnp.int32, (rows, 1), 0)


def lane_index(lanes):
    return lax.broadcasted_iota(jnp.int32, (1, lanes), 1)


def source_row(packed):
    inner = packed % 8
    return packed // 8 * PATCHES + inner % PATCHES + jnp.where(inner >= PATCHES, ROWS // 2, 0)


def patch_row(packed):
    inner = packed % 8
    return packed // 8 + inner % PATCHES * SLOTS + jnp.where(inner >= PATCHES, ROWS, 0)


def pack_kernel(tokens_ref, d_out_ref, packed_ref, both_ref, out_ref, sems, out_sems):
    part = ROWS // 2
    copies = [
        pltpu.make_async_copy(
            ref.at[pl.ds(half * part, part)],
            both_ref.at[pl.ds(half * ROWS + i * part, part)],
            sems.at[half * 2 + i],
        )
        for half in range(2)
        for i, ref in enumerate((tokens_ref, d_out_ref))
    ]
    for copy in copies:
        copy.start()
    chooser = pick((ROWS, ROWS), source_row(row_index(ROWS)), 1)
    outs = []
    for half in range(2):
        for copy in copies[half * 2 : half * 2 + 2]:
            copy.wait()
        rows = slice(half * ROWS, (half + 1) * ROWS)
        out_ref[rows, :] = dot(chooser, both_ref[rows, :]).astype(BF)
        span = pl.ds(half * ROWS, ROWS)
        out = pltpu.make_async_copy(out_ref.at[span], packed_ref.at[span], out_sems.at[half])
        out.start()
        outs.append(out)
    for out in outs:
        out.wait()


def row_stats(tokens):
    values = tokens.astype(F32)
    center = values - jnp.mean(values, axis=-1, keepdims=True)
    spread = jnp.mean(center * center, axis=-1, keepdims=True)
    inverse = lax.rsqrt(spread + 1e-06)
    return center * inverse, inverse


def window(head):
    low = head * E
    base = low // 128 * 128
    width = 128 if low + E <= base + 128 else 256
    lane = lax.broadcasted_iota(jnp.int32, (ROWS, width), 1)
    inside = (lane >= low - base) & (lane < low - base + E)
    return base, width, inside


def only(inside, array):
    return jnp.where(inside, array, jnp.zeros_like(array))


def lane_patch():
    return lax.broadcasted_iota(jnp.int32, (SLOTS, ROWS), 1) // SLOTS


def diagonal(full, patch):
    packed = full[:SLOTS]
    for p in range(1, PATCHES):
        packed = jnp.where(patch == p, full[p * SLOTS : (p + 1) * SLOTS], packed)
    return packed


def spread(packed, patch):
    blocks = [jnp.where(patch == p, packed, 0.0) for p in range(PATCHES)]
    return jnp.concatenate(blocks, axis=0).astype(BF)


def forward_kernel(
    place_ref, core_ref, packed_ref, live_ref, first_q_ref, first_k_ref, first_v_ref, w_qkv_ref,
    tokens_ref, masked_ref, joined_ref, probs_ref,
    own_ref, right_far_ref, left_far_ref, right_ref, left_ref,
    turned_ref, values_ref, attended_ref, weight_ref, sems,
):
    spans = [pl.ds(kind * D + chunk * WIDE, WIDE) for chunk in (1, 2) for kind in range(3)]
    copies = [
        pltpu.make_async_copy(w_qkv_ref.at[:, span], weight_ref.at[:, span], sems.at[i])
        for i, span in enumerate(spans)
    ]
    for copy in copies:
        copy.start()
    plain = dot(pick((256, 256), patch_row(lane_index(256)), 0), packed_ref[...])
    tokens = plain[:ROWS].astype(BF)
    tokens_ref[...] = tokens
    normalized, _ = row_stats(tokens)
    normed = normalized.astype(BF)
    live = live_ref[...]
    masked = plain[ROWS:] * jnp.concatenate([live] * PATCHES, axis=0)
    masked_ref[...] = masked.astype(BF)
    for block in range(9):
        lanes = slice(block * 128, (block + 1) * 128)
        turned_ref[lanes, :] = masked[:, lanes].T.astype(BF)
    me = place_ref[0]

    def slice_for(step, first, size):
        start = pl.multiple_of((me + step) % 4 * COLS, 16) + first
        return turned_ref[pl.ds(pl.multiple_of(start, 16), size), :]

    own_ref[D:, :] = slice_for(0, 0, COLS)
    right_ref[HALF:, :] = slice_for(1, 0, COLS)
    left_ref[HALF:, :] = slice_for(3, 0, COLS)
    right_far_ref[HALF:, :] = slice_for(2, 0, COLS // 2)
    left_far_ref[HALF:, :] = slice_for(2, COLS // 2, COLS // 2)
    patch = lane_patch()
    done = 0
    for chunk in range(3):
        if chunk > 0:
            for copy in copies[chunk * 3 - 3 : chunk * 3]:
                copy.wait()
        for kind in range(3):
            columns = slice(kind * D + chunk * WIDE, kind * D + (chunk + 1) * WIDE)
            if chunk == 0:
                weight = (first_q_ref, first_k_ref, first_v_ref)[kind][...]
            else:
                weight = weight_ref[:, columns]
            product = dot(normed, weight)
            joined_ref[:, columns] = product.astype(BF)
            if kind == 2:
                for block in range(3):
                    at = chunk * WIDE + block * 128
                    values_ref[at : at + 128, :] = product[:, block * 128 : (block + 1) * 128].T
        while done < H and window(done)[0] + window(done)[1] <= (chunk + 1) * WIDE:
            head = done
            done += 1
            base, width, inside = window(head)
            queries = only(inside, joined_ref[:, base : base + width])
            keys_in = joined_ref[:, D + base : D + base + width]
            scores = diagonal(dot(keys_in, queries, NT), patch)
            scores = jnp.where(live > 0.5, scores, -1e30)
            top = jnp.max(scores, axis=0, keepdims=True)
            exponent = jnp.exp2((scores - top) * EXP_SCALE)
            probs = exponent / jnp.sum(exponent, axis=0, keepdims=True)
            probs_ref[head] = probs
            rows = slice(head * E, (head + 1) * E)
            attended = dot(values_ref[rows, :].astype(BF), spread(probs, patch))
            for group in range(4):
                at = group % 2 * HALF + head * 2 * OUT_ROWS + group // 2 * OUT_ROWS
                attended_ref[at : at + OUT_ROWS, :] = attended[group * OUT_ROWS : (group + 1) * OUT_ROWS]
    attended = attended_ref[...].astype(BF)
    own_ref[:D, :] = attended
    right_far_ref[:HALF, :] = attended[:HALF]
    left_far_ref[:HALF, :] = attended[HALF:]
    right_ref[:HALF, :] = attended[HALF:]
    left_ref[:HALF, :] = attended[:HALF]


def attention_grads(heads, joined_ref, probs_ref, head_ref, grad_ref, stride, fresh):
    patch = lane_patch()
    for head in heads:
        base, width, inside = window(head)
        queries = only(inside, joined_ref[:, base : base + width])
        keys_in = joined_ref[:, D + base : D + base + width]
        values = joined_ref[:, 2 * D + base : 2 * D + base + width]
        head_grad = only(inside, head_ref[:, base : base + width])
        probs = probs_ref[head]
        prob_grad = diagonal(dot(values, head_grad, NT), patch)
        inner_sum = jnp.sum(probs * prob_grad, axis=0, keepdims=True)
        score_grad = spread(probs * (prob_grad - inner_sum) * SCALE, patch)
        parts = (
            dot(score_grad, keys_in, TN).astype(BF),
            dot(score_grad, queries).astype(BF),
            dot(spread(probs, patch), head_grad).astype(BF),
        )
        for index, part in enumerate(parts):
            at = index * stride + base
            if fresh and head == heads[0]:
                grad_ref[:, at : at + width] = part
            else:
                grad_ref[:, at : at + width] = jnp.where(inside, part, grad_ref[:, at : at + width])


def early_grad_kernel(masked_ref, joined_ref, probs_ref, w_out_ref, head_ref, early_ref):
    masked = masked_ref[...]
    for chunk in range(3):
        columns = slice(chunk * WIDE, (chunk + 1) * WIDE)
        head_ref[:, columns] = dot(masked, w_out_ref[columns, :], NT).astype(BF)
    attention_grads(range(EARLY_HEADS), joined_ref, probs_ref, head_ref, early_ref, WIDE, True)


def late_grad_kernel(
    tokens_ref, masked_ref, joined_ref, probs_ref, head_ref, early_ref, w_qkv_ref,
    after_ref, also_after_ref, d_tokens_ref, grad_ref, weight_ref, sem,
):
    weights = pltpu.make_async_copy(w_qkv_ref, weight_ref, sem)
    weights.start()
    for kind in range(3):
        grad_ref[:, kind * D : kind * D + WIDE] = early_ref[:, kind * WIDE : (kind + 1) * WIDE]
    attention_grads(range(EARLY_HEADS, H), joined_ref, probs_ref, head_ref, grad_ref, D, False)
    masked = masked_ref[...]
    weights.wait()
    pieces = []
    for chunk in range(3):
        rows = slice(chunk * WIDE, (chunk + 1) * WIDE)
        pieces.append(dot(grad_ref[...], weight_ref[rows, :], NT))
    normed_grad = jnp.concatenate(pieces, axis=1)
    normalized, inverse = row_stats(tokens_ref[...])
    mean_grad = jnp.mean(normed_grad, axis=-1, keepdims=True)
    mean_cross = jnp.mean(normed_grad * normalized, axis=-1, keepdims=True)
    d_tokens_ref[...] = (
        masked.astype(F32) + inverse * (normed_grad - mean_grad - normalized * mean_cross)
    ).astype(BF)


def weight_terms(core, payloads):
    own_ref, left_a_ref, right_a_ref, left_b_ref, right_b_ref, far_a_ref, far_b_ref = payloads
    start = pl.multiple_of(core * HALF, HALF)
    pairs = ((left_a_ref, left_b_ref), (right_b_ref, right_a_ref), (far_a_ref, far_b_ref))
    attended = jnp.concatenate(
        [own_ref[pl.ds(start, HALF), :]]
        + [jnp.where(core == 0, first[:HALF, :], second[:HALF, :]) for first, second in pairs],
        axis=1,
    )
    far = jnp.concatenate([far_a_ref[HALF:, :], far_b_ref[HALF:, :]], axis=0)
    masked = jnp.concatenate(
        [own_ref[D:, :], left_b_ref[HALF:, :], right_b_ref[HALF:, :], far], axis=1
    )
    masked = jnp.concatenate([masked[:256]] + [masked[256:]] * 4, axis=0)
    return dot(attended, masked, NT)


def send_kernel(core_ref, *refs):
    refs[-1][...] = weight_terms(1 - core_ref[0], refs[:7]).astype(BF)


def keep_kernel(core_ref, *refs):
    d_tokens_ref, _, terms_ref, packed_ref, place_ref = refs[7:]
    terms_ref[...] = weight_terms(core_ref[0], refs[:7])
    term = lane_index(3 * 8 * OUT_ROWS)
    kind, inner = term // (8 * OUT_ROWS), term % (8 * OUT_ROWS)
    row = inner % OUT_ROWS
    at = TOKEN_ROWS + kind * OUT_ROWS + jnp.where(kind == 2, row // 4, row)
    place_ref[...] = pick((8 * CHUNK, 3 * 8 * OUT_ROWS), inner // OUT_ROWS * CHUNK + at, 0)
    piece = lane_index(576)
    target = piece % 16 * CHUNK + piece // 64 * PATCHES + piece % 64 // 16
    chooser = pick((16 * CHUNK, 576), target, 0)
    for half in range(2):
        stacked = jnp.concatenate(
            [
                d_tokens_ref[
                    p * SLOTS + half * 16 : p * SLOTS + half * 16 + 16, c * 128 : (c + 1) * 128
                ]
                for c in range(9)
                for p in range(PATCHES)
            ],
            axis=0,
        )
        packed_ref[half * 16 * CHUNK : (half + 1) * 16 * CHUNK, :] = dot(chooser, stacked).astype(BF)


def merge_kernel(rows_ref, keep_ref, got_ref, place_ref, merged_ref):
    terms = keep_ref[...] + got_ref[...].astype(F32)
    row = row_index(SLOTS * OUT_ROWS) % OUT_ROWS
    last = jnp.where(row % 4 == lane_index(128) // 32, terms[:, 256:], 0.0)
    blocks = [block.astype(BF) for block in (terms[:, :128], terms[:, 128:256], last)]
    for group in range(4):
        rows = slice(group * 8 * OUT_ROWS, (group + 1) * 8 * OUT_ROWS)
        stacked = jnp.concatenate([block[rows] for block in blocks], axis=0)
        out = slice(group * 8 * CHUNK, (group + 1) * 8 * CHUNK)
        merged_ref[out, :] = (
            dot(place_ref[...], stacked) + rows_ref[out, :].astype(F32)
        ).astype(BF)


def unpack_kernel(merged_ref, d_tokens_ref, d_w_ref, total_ref):
    piece = row_index(288)
    row = piece % 32
    source = row // PATCHES * CHUNK + piece // 32 * PATCHES + row % PATCHES
    chooser = pick((288, 8 * CHUNK), source, 1)
    for group in range(4):
        rows = dot(chooser, merged_ref[group * 8 * CHUNK : (group + 1) * 8 * CHUNK, :]).astype(BF)
        for block in range(9):
            d_tokens_ref[group * 32 : (group + 1) * 32, block * 128 : (block + 1) * 128] = rows[
                block * 32 : (block + 1) * 32
            ]
    merged = merged_ref[...].astype(F32).reshape(SLOTS, CHUNK, 128)
    total_ref[...] = jnp.sum(merged[:, 32:], axis=0)
    first = TOKEN_ROWS - 32
    d_w_ref[:, :128] = total_ref[first : first + OUT_ROWS, :]
    d_w_ref[:, 128:256] = total_ref[first + OUT_ROWS : first + 2 * OUT_ROWS, :]
    for row in range(OUT_ROWS):
        at = first + 2 * OUT_ROWS + row // 4
        lanes = slice(row % 4 * 32, row % 4 * 32 + 32)
        d_w_ref[row : row + 1, 256:] = total_ref[at : at + 1, lanes]


def body(tokens, d_out, frames, frame_order, w_qkv, w_out):
    place = lax.axis_index("dp")
    core = lax.axis_index("core")
    shape = jax.ShapeDtypeStruct
    live = (frame_order[0] < frames[0]).astype(F32)
    packed = call(
        pack_kernel,
        shape((256, D), BF),
        (tokens[0], d_out[0]),
        scratch=(
            pltpu.VMEM((256, D), BF),
            pltpu.VMEM((256, D), BF),
            pltpu.SemaphoreType.DMA((4,)),
            pltpu.SemaphoreType.DMA((2,)),
        ),
        limit=60,
        far=(0, 1),
        far_out=(0,),
    )
    arrived = lax.all_to_all(
        packed.reshape(SLOTS, 8, D), ("y", "z"), split_axis=0, concat_axis=0, tiled=True
    ).reshape(256, D)
    firsts = tuple(w_qkv[:, kind * D : kind * D + WIDE] for kind in range(3))
    kept, masked, joined, probs, own, right_far, left_far, right, left = call(
        forward_kernel,
        (
            shape((ROWS, D), BF),
            shape((ROWS, D), BF),
            shape((ROWS, 3 * D), BF),
            shape((H, SLOTS, ROWS), F32),
            shape((PAYLOAD, ROWS), BF),
        )
        + (shape((HALF + COLS // 2, ROWS), BF),) * 2
        + (shape((HALF + COLS, ROWS), BF),) * 2,
        (place.reshape(1), core.reshape(1), arrived, live[:, None]) + firsts + (w_qkv,),
        scratch=(
            pltpu.VMEM((D, ROWS), BF),
            pltpu.VMEM((D, ROWS), F32),
            pltpu.VMEM((D, ROWS), F32),
            pltpu.VMEM((D, 3 * D), BF),
            pltpu.SemaphoreType.DMA((6,)),
        ),
        smem=(0, 1),
        far=(7,),
        limit=47,
        flops=int(2e9),
        data=int(14e6),
    )
    up = [(i, (i + 1) % 4) for i in range(4)]
    down = [(i, (i + 3) % 4) for i in range(4)]
    left_a = lax.ppermute(right_far, "dp", up)
    right_a = lax.ppermute(left_far, "dp", down)
    left_b = lax.ppermute(right, "dp", up)
    right_b = lax.ppermute(left, "dp", down)
    head_grads, early = call(
        early_grad_kernel,
        (shape((ROWS, D), BF), shape((ROWS, 3 * WIDE), BF)),
        (masked, joined, probs, w_out),
        limit=16,
        flops=int(2e9),
        data=int(8e6),
    )
    far_a = lax.ppermute(left_a, "dp", up)
    far_b = lax.ppermute(right_a, "dp", down)
    d_rows = call(
        late_grad_kernel,
        shape((ROWS, D), BF),
        (kept, masked, joined, probs, head_grads, early, w_qkv, left_a, right_a),
        scratch=(
            pltpu.VMEM((ROWS, 3 * D), BF),
            pltpu.VMEM((D, 3 * D), BF),
            pltpu.SemaphoreType.DMA,
        ),
        far=(6, 7, 8),
        limit=48,
        flops=int(6e9),
        data=int(32e6),
    )
    payloads = (core.reshape(1), own, left_a, right_a, left_b, right_b, far_a, far_b)
    send = call(
        send_kernel,
        shape((SLOTS * OUT_ROWS, WIDE), BF),
        payloads + (d_rows,),
        smem=(0,),
        far=(8,),
        flops=int(1e9),
        data=int(4e6),
    )
    got = lax.ppermute(send, "core", [(0, 1), (1, 0)])
    keep, rows, places = call(
        keep_kernel,
        (
            shape((SLOTS * OUT_ROWS, WIDE), F32),
            shape((SLOTS * CHUNK, 128), BF),
            shape((8 * CHUNK, 3 * 8 * OUT_ROWS), BF),
        ),
        payloads + (d_rows, send),
        smem=(0,),
        far=(9,),
        flops=int(1e9),
        data=int(4e6),
    )
    merged = call(
        merge_kernel, shape((SLOTS * CHUNK, 128), BF), (rows, keep, got, places), limit=16
    )
    returned = lax.all_to_all(
        merged.reshape(SLOTS, CHUNK, 128), ("y", "z"), split_axis=0, concat_axis=0, tiled=True
    ).reshape(SLOTS * CHUNK, 128)
    d_tokens, d_w = call(
        unpack_kernel,
        (shape((ROWS, D), BF), shape((OUT_ROWS, COLS), F32)),
        (returned,),
        scratch=(pltpu.VMEM((CHUNK - 32, 128), F32),),
        limit=16,
    )
    return d_tokens[None], d_w


def solution(mesh):
    fine = Mesh(mesh.devices.reshape(4, 4, 8, 2), ("dp", "y", "z", "core"))
    seq = ("y", "z", "core")
    placed = (P("dp", seq, None), P("dp", seq, None), P("dp"), P("dp", None), P(), P())
    return jax.shard_map(
        body,
        mesh=fine,
        in_specs=placed,
        out_specs=(P("dp", seq, None), P(seq, "dp")),
        check_vma=False,
    )
```

```python
import functools
import math

import jax
import jax.numpy as jnp
from jax import lax
from jax.experimental import pallas as pl
from jax.experimental.pallas import tpu as pltpu
from jax.sharding import Mesh, PartitionSpec as P

H = 16
D = 1152
E = D // H
SLOTS = 32
PATCHES = 4
ROWS = SLOTS * PATCHES
SCALE = 1.0 / math.sqrt(E)
BF = jnp.bfloat16
F32 = jnp.float32
MIB = 1024 * 1024
COLS = 288
WIDE = 384
OUT_ROWS = 18
CHUNK = 80
TOKEN_ROWS = 36
PAYLOAD = D + COLS
HALF = D // 2
EARLY_HEADS = 5
EXP_SCALE = SCALE * math.log2(math.e)

NN = (((1,), (0,)), ((), ()))
NT = (((1,), (1,)), ((), ()))
TN = (((0,), (0,)), ((), ()))


def dot(a, b, dims=NN):
    return lax.dot_general(a, b, dims, preferred_element_type=F32)


def call(
    kernel, out_shape, inputs, scratch=(), limit=32, flops=0, data=0, smem=(), far=(), far_out=()
):
    spaces = {i: pltpu.SMEM for i in smem} | {i: pl.ANY for i in far}
    single = isinstance(out_shape, jax.ShapeDtypeStruct)
    shapes = (out_shape,) if single else tuple(out_shape)
    outs = pl.pallas_call(
        kernel,
        out_shape=shapes,
        in_specs=[
            pl.BlockSpec(memory_space=spaces.get(i, pltpu.VMEM)) for i in range(len(inputs))
        ],
        out_specs=tuple(
            pl.BlockSpec(memory_space=pl.ANY if i in far_out else pltpu.VMEM)
            for i in range(len(shapes))
        ),
        scratch_shapes=list(scratch),
        compiler_params=pltpu.CompilerParams(vmem_limit_bytes=limit * MIB),
        cost_estimate=pl.CostEstimate(flops=flops, bytes_accessed=data, transcendentals=0),
    )(*inputs)
    return outs[0] if single else outs


def pick(shape, target, along):
    return (lax.broadcasted_iota(jnp.int32, shape, along) == target).astype(F32).astype(BF)


def row_index(rows):
    return lax.broadcasted_iota(jnp.int32, (rows, 1), 0)


def lane_index(lanes):
    return lax.broadcasted_iota(jnp.int32, (1, lanes), 1)


def source_row(packed):
    inner = packed % 8
    return packed // 8 * PATCHES + inner % PATCHES + jnp.where(inner >= PATCHES, ROWS // 2, 0)


def patch_row(packed):
    inner = packed % 8
    return packed // 8 + inner % PATCHES * SLOTS + jnp.where(inner >= PATCHES, ROWS, 0)


def pack_kernel(tokens_ref, d_out_ref, packed_ref, both_ref, out_ref, sems, out_sems):
    part = ROWS // 2
    copies = [
        pltpu.make_async_copy(
            ref.at[pl.ds(half * part, part)],
            both_ref.at[pl.ds(half * ROWS + i * part, part)],
            sems.at[half * 2 + i],
        )
        for half in range(2)
        for i, ref in enumerate((tokens_ref, d_out_ref))
    ]
    for copy in copies:
        copy.start()
    chooser = pick((ROWS, ROWS), source_row(row_index(ROWS)), 1)
    outs = []
    for half in range(2):
        for copy in copies[half * 2 : half * 2 + 2]:
            copy.wait()
        rows = slice(half * ROWS, (half + 1) * ROWS)
        out_ref[rows, :] = dot(chooser, both_ref[rows, :]).astype(BF)
        span = pl.ds(half * ROWS, ROWS)
        out = pltpu.make_async_copy(out_ref.at[span], packed_ref.at[span], out_sems.at[half])
        out.start()
        outs.append(out)
    for out in outs:
        out.wait()


def row_stats(tokens):
    values = tokens.astype(F32)
    center = values - jnp.mean(values, axis=-1, keepdims=True)
    spread = jnp.mean(center * center, axis=-1, keepdims=True)
    inverse = lax.rsqrt(spread + 1e-06)
    return center * inverse, inverse


def window(head):
    low = head * E
    base = low // 128 * 128
    width = 128 if low + E <= base + 128 else 256
    lane = lax.broadcasted_iota(jnp.int32, (ROWS, width), 1)
    inside = (lane >= low - base) & (lane < low - base + E)
    return base, width, inside


def only(inside, array):
    return jnp.where(inside, array, jnp.zeros_like(array))


def lane_patch():
    return lax.broadcasted_iota(jnp.int32, (SLOTS, ROWS), 1) // SLOTS


def diagonal(full, patch):
    packed = full[:SLOTS]
    for p in range(1, PATCHES):
        packed = jnp.where(patch == p, full[p * SLOTS : (p + 1) * SLOTS], packed)
    return packed


def spread(packed, patch):
    blocks = [jnp.where(patch == p, packed, 0.0) for p in range(PATCHES)]
    return jnp.concatenate(blocks, axis=0).astype(BF)


def forward_kernel(
    place_ref, core_ref, packed_ref, live_ref, first_q_ref, first_k_ref, first_v_ref, w_qkv_ref,
    tokens_ref, masked_ref, joined_ref, probs_ref,
    own_ref, right_far_ref, left_far_ref, right_ref, left_ref,
    turned_ref, values_ref, attended_ref, weight_ref, sems,
):
    spans = [pl.ds(kind * D + chunk * WIDE, WIDE) for chunk in (1, 2) for kind in range(3)]
    copies = [
        pltpu.make_async_copy(w_qkv_ref.at[:, span], weight_ref.at[:, span], sems.at[i])
        for i, span in enumerate(spans)
    ]
    for copy in copies:
        copy.start()
    plain = dot(pick((256, 256), patch_row(lane_index(256)), 0), packed_ref[...])
    tokens = plain[:ROWS].astype(BF)
    tokens_ref[...] = tokens
    normalized, _ = row_stats(tokens)
    normed = normalized.astype(BF)
    live = live_ref[...]
    masked = plain[ROWS:] * jnp.concatenate([live] * PATCHES, axis=0)
    masked_ref[...] = masked.astype(BF)
    for block in range(9):
        lanes = slice(block * 128, (block + 1) * 128)
        turned_ref[lanes, :] = masked[:, lanes].T.astype(BF)
    me = place_ref[0]

    def slice_for(step, first, size):
        start = pl.multiple_of((me + step) % 4 * COLS, 16) + first
        return turned_ref[pl.ds(pl.multiple_of(start, 16), size), :]

    own_ref[D:, :] = slice_for(0, 0, COLS)
    right_ref[HALF:, :] = slice_for(1, 0, COLS)
    left_ref[HALF:, :] = slice_for(3, 0, COLS)
    right_far_ref[HALF:, :] = slice_for(2, 0, COLS // 2)
    left_far_ref[HALF:, :] = slice_for(2, COLS // 2, COLS // 2)
    patch = lane_patch()
    done = 0
    for chunk in range(3):
        if chunk > 0:
            for copy in copies[chunk * 3 - 3 : chunk * 3]:
                copy.wait()
        for kind in range(3):
            columns = slice(kind * D + chunk * WIDE, kind * D + (chunk + 1) * WIDE)
            if chunk == 0:
                weight = (first_q_ref, first_k_ref, first_v_ref)[kind][...]
            else:
                weight = weight_ref[:, columns]
            product = dot(normed, weight)
            joined_ref[:, columns] = product.astype(BF)
            if kind == 2:
                for block in range(3):
                    at = chunk * WIDE + block * 128
                    values_ref[at : at + 128, :] = product[:, block * 128 : (block + 1) * 128].T
        while done < H and window(done)[0] + window(done)[1] <= (chunk + 1) * WIDE:
            head = done
            done += 1
            base, width, inside = window(head)
            queries = only(inside, joined_ref[:, base : base + width])
            keys_in = joined_ref[:, D + base : D + base + width]
            scores = diagonal(dot(keys_in, queries, NT), patch)
            scores = jnp.where(live > 0.5, scores, -1e30)
            top = jnp.max(scores, axis=0, keepdims=True)
            exponent = jnp.exp2((scores - top) * EXP_SCALE)
            probs = exponent / jnp.sum(exponent, axis=0, keepdims=True)
            probs_ref[head] = probs
            rows = slice(head * E, (head + 1) * E)
            attended = dot(values_ref[rows, :].astype(BF), spread(probs, patch))
            for group in range(4):
                at = group % 2 * HALF + head * 2 * OUT_ROWS + group // 2 * OUT_ROWS
                attended_ref[at : at + OUT_ROWS, :] = attended[group * OUT_ROWS : (group + 1) * OUT_ROWS]
    attended = attended_ref[...].astype(BF)
    own_ref[:D, :] = attended
    right_far_ref[:HALF, :] = attended[:HALF]
    left_far_ref[:HALF, :] = attended[HALF:]
    right_ref[:HALF, :] = attended[HALF:]
    left_ref[:HALF, :] = attended[:HALF]


def attention_grads(heads, joined_ref, probs_ref, head_ref, grad_ref, stride, fresh):
    patch = lane_patch()
    for head in heads:
        base, width, inside = window(head)
        queries = only(inside, joined_ref[:, base : base + width])
        keys_in = joined_ref[:, D + base : D + base + width]
        values = joined_ref[:, 2 * D + base : 2 * D + base + width]
        head_grad = only(inside, head_ref[:, base : base + width])
        probs = probs_ref[head]
        prob_grad = diagonal(dot(values, head_grad, NT), patch)
        inner_sum = jnp.sum(probs * prob_grad, axis=0, keepdims=True)
        score_grad = spread(probs * (prob_grad - inner_sum) * SCALE, patch)
        parts = (
            dot(score_grad, keys_in, TN).astype(BF),
            dot(score_grad, queries).astype(BF),
            dot(spread(probs, patch), head_grad).astype(BF),
        )
        for index, part in enumerate(parts):
            at = index * stride + base
            if fresh and head == heads[0]:
                grad_ref[:, at : at + width] = part
            else:
                grad_ref[:, at : at + width] = jnp.where(inside, part, grad_ref[:, at : at + width])


def early_grad_kernel(masked_ref, joined_ref, probs_ref, w_out_ref, head_ref, early_ref):
    masked = masked_ref[...]
    for chunk in range(3):
        columns = slice(chunk * WIDE, (chunk + 1) * WIDE)
        head_ref[:, columns] = dot(masked, w_out_ref[columns, :], NT).astype(BF)
    attention_grads(range(EARLY_HEADS), joined_ref, probs_ref, head_ref, early_ref, WIDE, True)


def late_grad_kernel(
    joined_ref, probs_ref, head_ref, early_ref, after_ref, also_after_ref, grad_ref
):
    for kind in range(3):
        grad_ref[:, kind * D : kind * D + WIDE] = early_ref[:, kind * WIDE : (kind + 1) * WIDE]
    attention_grads(range(EARLY_HEADS, H), joined_ref, probs_ref, head_ref, grad_ref, D, False)


def token_grad_kernel(tokens_ref, masked_ref, grad_ref, w_qkv_ref, d_tokens_ref):
    masked = masked_ref[...]
    pieces = []
    for chunk in range(3):
        rows = slice(chunk * WIDE, (chunk + 1) * WIDE)
        pieces.append(dot(grad_ref[...], w_qkv_ref[rows, :], NT))
    normed_grad = jnp.concatenate(pieces, axis=1)
    normalized, inverse = row_stats(tokens_ref[...])
    mean_grad = jnp.mean(normed_grad, axis=-1, keepdims=True)
    mean_cross = jnp.mean(normed_grad * normalized, axis=-1, keepdims=True)
    d_tokens_ref[...] = (
        masked.astype(F32) + inverse * (normed_grad - mean_grad - normalized * mean_cross)
    ).astype(BF)


def weight_terms(core, payloads):
    own_ref, left_a_ref, right_a_ref, left_b_ref, right_b_ref, far_a_ref, far_b_ref = payloads
    start = pl.multiple_of(core * HALF, HALF)
    pairs = ((left_a_ref, left_b_ref), (right_b_ref, right_a_ref), (far_a_ref, far_b_ref))
    attended = jnp.concatenate(
        [own_ref[pl.ds(start, HALF), :]]
        + [jnp.where(core == 0, first[:HALF, :], second[:HALF, :]) for first, second in pairs],
        axis=1,
    )
    far = jnp.concatenate([far_a_ref[HALF:, :], far_b_ref[HALF:, :]], axis=0)
    masked = jnp.concatenate(
        [own_ref[D:, :], left_b_ref[HALF:, :], right_b_ref[HALF:, :], far], axis=1
    )
    masked = jnp.concatenate([masked[:256]] + [masked[256:]] * 4, axis=0)
    return dot(attended, masked, NT)


def send_kernel(core_ref, *refs):
    refs[-1][...] = weight_terms(1 - core_ref[0], refs[:7]).astype(BF)


def keep_kernel(core_ref, *refs):
    d_tokens_ref, _, terms_ref, packed_ref, place_ref = refs[7:]
    terms_ref[...] = weight_terms(core_ref[0], refs[:7])
    term = lane_index(3 * 8 * OUT_ROWS)
    kind, inner = term // (8 * OUT_ROWS), term % (8 * OUT_ROWS)
    row = inner % OUT_ROWS
    at = TOKEN_ROWS + kind * OUT_ROWS + jnp.where(kind == 2, row // 4, row)
    place_ref[...] = pick((8 * CHUNK, 3 * 8 * OUT_ROWS), inner // OUT_ROWS * CHUNK + at, 0)
    piece = lane_index(576)
    target = piece % 16 * CHUNK + piece // 64 * PATCHES + piece % 64 // 16
    chooser = pick((16 * CHUNK, 576), target, 0)
    for half in range(2):
        stacked = jnp.concatenate(
            [
                d_tokens_ref[
                    p * SLOTS + half * 16 : p * SLOTS + half * 16 + 16, c * 128 : (c + 1) * 128
                ]
                for c in range(9)
                for p in range(PATCHES)
            ],
            axis=0,
        )
        packed_ref[half * 16 * CHUNK : (half + 1) * 16 * CHUNK, :] = dot(chooser, stacked).astype(BF)


def merge_kernel(rows_ref, keep_ref, got_ref, place_ref, merged_ref):
    terms = keep_ref[...] + got_ref[...].astype(F32)
    row = row_index(SLOTS * OUT_ROWS) % OUT_ROWS
    last = jnp.where(row % 4 == lane_index(128) // 32, terms[:, 256:], 0.0)
    blocks = [block.astype(BF) for block in (terms[:, :128], terms[:, 128:256], last)]
    for group in range(4):
        rows = slice(group * 8 * OUT_ROWS, (group + 1) * 8 * OUT_ROWS)
        stacked = jnp.concatenate([block[rows] for block in blocks], axis=0)
        out = slice(group * 8 * CHUNK, (group + 1) * 8 * CHUNK)
        merged_ref[out, :] = (
            dot(place_ref[...], stacked) + rows_ref[out, :].astype(F32)
        ).astype(BF)


def unpack_kernel(merged_ref, d_tokens_ref, d_w_ref, total_ref):
    piece = row_index(288)
    row = piece % 32
    source = row // PATCHES * CHUNK + piece // 32 * PATCHES + row % PATCHES
    chooser = pick((288, 8 * CHUNK), source, 1)
    for group in range(4):
        rows = dot(chooser, merged_ref[group * 8 * CHUNK : (group + 1) * 8 * CHUNK, :]).astype(BF)
        for block in range(9):
            d_tokens_ref[group * 32 : (group + 1) * 32, block * 128 : (block + 1) * 128] = rows[
                block * 32 : (block + 1) * 32
            ]
    merged = merged_ref[...].astype(F32).reshape(SLOTS, CHUNK, 128)
    total_ref[...] = jnp.sum(merged[:, 32:], axis=0)
    first = TOKEN_ROWS - 32
    d_w_ref[:, :128] = total_ref[first : first + OUT_ROWS, :]
    d_w_ref[:, 128:256] = total_ref[first + OUT_ROWS : first + 2 * OUT_ROWS, :]
    for row in range(OUT_ROWS):
        at = first + 2 * OUT_ROWS + row // 4
        lanes = slice(row % 4 * 32, row % 4 * 32 + 32)
        d_w_ref[row : row + 1, 256:] = total_ref[at : at + 1, lanes]


def body(tokens, d_out, frames, frame_order, w_qkv, w_out):
    place = lax.axis_index("dp")
    core = lax.axis_index("core")
    shape = jax.ShapeDtypeStruct
    live = (frame_order[0] < frames[0]).astype(F32)
    packed = call(
        pack_kernel,
        shape((256, D), BF),
        (tokens[0], d_out[0]),
        scratch=(
            pltpu.VMEM((256, D), BF),
            pltpu.VMEM((256, D), BF),
            pltpu.SemaphoreType.DMA((4,)),
            pltpu.SemaphoreType.DMA((2,)),
        ),
        limit=60,
        far=(0, 1),
        far_out=(0,),
    )
    arrived = lax.all_to_all(
        packed.reshape(SLOTS, 8, D), ("y", "z"), split_axis=0, concat_axis=0, tiled=True
    ).reshape(256, D)
    firsts = tuple(w_qkv[:, kind * D : kind * D + WIDE] for kind in range(3))
    kept, masked, joined, probs, own, right_far, left_far, right, left = call(
        forward_kernel,
        (
            shape((ROWS, D), BF),
            shape((ROWS, D), BF),
            shape((ROWS, 3 * D), BF),
            shape((H, SLOTS, ROWS), F32),
            shape((PAYLOAD, ROWS), BF),
        )
        + (shape((HALF + COLS // 2, ROWS), BF),) * 2
        + (shape((HALF + COLS, ROWS), BF),) * 2,
        (place.reshape(1), core.reshape(1), arrived, live[:, None]) + firsts + (w_qkv,),
        scratch=(
            pltpu.VMEM((D, ROWS), BF),
            pltpu.VMEM((D, ROWS), F32),
            pltpu.VMEM((D, ROWS), F32),
            pltpu.VMEM((D, 3 * D), BF),
            pltpu.SemaphoreType.DMA((6,)),
        ),
        smem=(0, 1),
        far=(7,),
        limit=47,
        flops=int(2e9),
        data=int(14e6),
    )
    up = [(i, (i + 1) % 4) for i in range(4)]
    down = [(i, (i + 3) % 4) for i in range(4)]
    left_a = lax.ppermute(right_far, "dp", up)
    right_a = lax.ppermute(left_far, "dp", down)
    left_b = lax.ppermute(right, "dp", up)
    right_b = lax.ppermute(left, "dp", down)
    head_grads, early = call(
        early_grad_kernel,
        (shape((ROWS, D), BF), shape((ROWS, 3 * WIDE), BF)),
        (masked, joined, probs, w_out),
        limit=16,
        flops=int(2e9),
        data=int(8e6),
    )
    far_a = lax.ppermute(left_a, "dp", up)
    far_b = lax.ppermute(right_a, "dp", down)
    grads = call(
        late_grad_kernel,
        shape((ROWS, 3 * D), BF),
        (joined, probs, head_grads, early, left_a, right_a),
        far=(4, 5),
        limit=16,
        flops=int(3e9),
        data=int(16e6),
    )
    d_rows = call(
        token_grad_kernel,
        shape((ROWS, D), BF),
        (kept, masked, grads, w_qkv),
        limit=24,
        flops=int(3e9),
        data=int(16e6),
    )
    payloads = (core.reshape(1), own, left_a, right_a, left_b, right_b, far_a, far_b)
    send = call(
        send_kernel,
        shape((SLOTS * OUT_ROWS, WIDE), BF),
        payloads + (d_rows,),
        smem=(0,),
        far=(8,),
        flops=int(1e9),
        data=int(4e6),
    )
    got = lax.ppermute(send, "core", [(0, 1), (1, 0)])
    keep, rows, places = call(
        keep_kernel,
        (
            shape((SLOTS * OUT_ROWS, WIDE), F32),
            shape((SLOTS * CHUNK, 128), BF),
            shape((8 * CHUNK, 3 * 8 * OUT_ROWS), BF),
        ),
        payloads + (d_rows, send),
        smem=(0,),
        far=(9,),
        flops=int(1e9),
        data=int(4e6),
    )
    merged = call(
        merge_kernel, shape((SLOTS * CHUNK, 128), BF), (rows, keep, got, places), limit=16
    )
    returned = lax.all_to_all(
        merged.reshape(SLOTS, CHUNK, 128), ("y", "z"), split_axis=0, concat_axis=0, tiled=True
    ).reshape(SLOTS * CHUNK, 128)
    d_tokens, d_w = call(
        unpack_kernel,
        (shape((ROWS, D), BF), shape((OUT_ROWS, COLS), F32)),
        (returned,),
        scratch=(pltpu.VMEM((CHUNK - 32, 128), F32),),
        limit=16,
    )
    return d_tokens[None], d_w


def solution(mesh):
    fine = Mesh(mesh.devices.reshape(4, 4, 8, 2), ("dp", "y", "z", "core"))
    seq = ("y", "z", "core")
    placed = (P("dp", seq, None), P("dp", seq, None), P("dp"), P("dp", None), P(), P())
    return jax.shard_map(
        body,
        mesh=fine,
        in_specs=placed,
        out_specs=(P("dp", seq, None), P(seq, "dp")),
        check_vma=False,
    )
```

```python
import functools
import math

import jax
import jax.numpy as jnp
from jax import lax
from jax.experimental import pallas as pl
from jax.experimental.pallas import tpu as pltpu
from jax.sharding import Mesh, PartitionSpec as P

H = 16
D = 1152
E = D // H
SLOTS = 32
PATCHES = 4
ROWS = SLOTS * PATCHES
SCALE = 1.0 / math.sqrt(E)
BF = jnp.bfloat16
F32 = jnp.float32
MIB = 1024 * 1024
COLS = 288
WIDE = 384
OUT_ROWS = 18
CHUNK = 80
TOKEN_ROWS = 36
PAYLOAD = D + COLS
HALF = D // 2
EARLY_HEADS = 5
PART = ROWS // 4
EXP_SCALE = SCALE * math.log2(math.e)

NN = (((1,), (0,)), ((), ()))
NT = (((1,), (1,)), ((), ()))
TN = (((0,), (0,)), ((), ()))


def dot(a, b, dims=NN):
    return lax.dot_general(a, b, dims, preferred_element_type=F32)


def call(
    kernel, out_shape, inputs, scratch=(), limit=32, flops=0, data=0, smem=(), far=(), far_out=()
):
    spaces = {i: pltpu.SMEM for i in smem} | {i: pl.ANY for i in far}
    single = isinstance(out_shape, jax.ShapeDtypeStruct)
    shapes = (out_shape,) if single else tuple(out_shape)
    outs = pl.pallas_call(
        kernel,
        out_shape=shapes,
        in_specs=[
            pl.BlockSpec(memory_space=spaces.get(i, pltpu.VMEM)) for i in range(len(inputs))
        ],
        out_specs=tuple(
            pl.BlockSpec(memory_space=pl.ANY if i in far_out else pltpu.VMEM)
            for i in range(len(shapes))
        ),
        scratch_shapes=list(scratch),
        compiler_params=pltpu.CompilerParams(vmem_limit_bytes=limit * MIB),
        cost_estimate=pl.CostEstimate(flops=flops, bytes_accessed=data, transcendentals=0),
    )(*inputs)
    return outs[0] if single else outs


def pick(shape, target, along):
    return (lax.broadcasted_iota(jnp.int32, shape, along) == target).astype(F32).astype(BF)


def row_index(rows):
    return lax.broadcasted_iota(jnp.int32, (rows, 1), 0)


def lane_index(lanes):
    return lax.broadcasted_iota(jnp.int32, (1, lanes), 1)


def source_row(packed):
    inner = packed % 8
    return packed // 8 * PATCHES + inner % PATCHES + jnp.where(inner >= PATCHES, PART, 0)


def patch_row(packed):
    inner = packed % 8
    return packed // 8 + inner % PATCHES * SLOTS + jnp.where(inner >= PATCHES, ROWS, 0)


def pack_kernel(tokens_ref, d_out_ref, packed_ref, both_ref, out_ref, sems, out_sems):
    copies = [
        pltpu.make_async_copy(
            ref.at[pl.ds(quarter * PART, PART)],
            both_ref.at[pl.ds(quarter * 2 * PART + i * PART, PART)],
            sems.at[quarter * 2 + i],
        )
        for quarter in range(4)
        for i, ref in enumerate((tokens_ref, d_out_ref))
    ]
    for copy in copies:
        copy.start()
    chooser = pick((2 * PART, 2 * PART), source_row(row_index(2 * PART)), 1)
    outs = []
    for quarter in range(4):
        for copy in copies[quarter * 2 : quarter * 2 + 2]:
            copy.wait()
        rows = slice(quarter * 2 * PART, (quarter + 1) * 2 * PART)
        out_ref[rows, :] = dot(chooser, both_ref[rows, :]).astype(BF)
        span = pl.ds(quarter * 2 * PART, 2 * PART)
        out = pltpu.make_async_copy(out_ref.at[span], packed_ref.at[span], out_sems.at[quarter])
        out.start()
        outs.append(out)
    for out in outs:
        out.wait()


def row_stats(tokens):
    values = tokens.astype(F32)
    center = values - jnp.mean(values, axis=-1, keepdims=True)
    spread = jnp.mean(center * center, axis=-1, keepdims=True)
    inverse = lax.rsqrt(spread + 1e-06)
    return center * inverse, inverse


def window(head):
    low = head * E
    base = low // 128 * 128
    width = 128 if low + E <= base + 128 else 256
    lane = lax.broadcasted_iota(jnp.int32, (ROWS, width), 1)
    inside = (lane >= low - base) & (lane < low - base + E)
    return base, width, inside


def only(inside, array):
    return jnp.where(inside, array, jnp.zeros_like(array))


def lane_patch():
    return lax.broadcasted_iota(jnp.int32, (SLOTS, ROWS), 1) // SLOTS


def diagonal(full, patch):
    packed = full[:SLOTS]
    for p in range(1, PATCHES):
        packed = jnp.where(patch == p, full[p * SLOTS : (p + 1) * SLOTS], packed)
    return packed


def spread(packed, patch):
    blocks = [jnp.where(patch == p, packed, 0.0) for p in range(PATCHES)]
    return jnp.concatenate(blocks, axis=0).astype(BF)


def forward_kernel(
    place_ref, core_ref, packed_ref, live_ref, first_q_ref, first_k_ref, first_v_ref, w_qkv_ref,
    tokens_ref, masked_ref, joined_ref, probs_ref,
    own_ref, right_far_ref, left_far_ref, right_ref, left_ref,
    turned_ref, values_ref, attended_ref, weight_ref, sems,
):
    spans = [pl.ds(kind * D + chunk * WIDE, WIDE) for chunk in (1, 2) for kind in range(3)]
    copies = [
        pltpu.make_async_copy(w_qkv_ref.at[:, span], weight_ref.at[:, span], sems.at[i])
        for i, span in enumerate(spans)
    ]
    for copy in copies:
        copy.start()
    plain = dot(pick((256, 256), patch_row(lane_index(256)), 0), packed_ref[...])
    tokens = plain[:ROWS].astype(BF)
    tokens_ref[...] = tokens
    normalized, _ = row_stats(tokens)
    normed = normalized.astype(BF)
    live = live_ref[...]
    masked = plain[ROWS:] * jnp.concatenate([live] * PATCHES, axis=0)
    masked_ref[...] = masked.astype(BF)
    for block in range(9):
        lanes = slice(block * 128, (block + 1) * 128)
        turned_ref[lanes, :] = masked[:, lanes].T.astype(BF)
    me = place_ref[0]

    def slice_for(step, first, size):
        start = pl.multiple_of((me + step) % 4 * COLS, 16) + first
        return turned_ref[pl.ds(pl.multiple_of(start, 16), size), :]

    own_ref[D:, :] = slice_for(0, 0, COLS)
    right_ref[HALF:, :] = slice_for(1, 0, COLS)
    left_ref[HALF:, :] = slice_for(3, 0, COLS)
    right_far_ref[HALF:, :] = slice_for(2, 0, COLS // 2)
    left_far_ref[HALF:, :] = slice_for(2, COLS // 2, COLS // 2)
    patch = lane_patch()
    done = 0
    for chunk in range(3):
        if chunk > 0:
            for copy in copies[chunk * 3 - 3 : chunk * 3]:
                copy.wait()
        for kind in range(3):
            columns = slice(kind * D + chunk * WIDE, kind * D + (chunk + 1) * WIDE)
            if chunk == 0:
                weight = (first_q_ref, first_k_ref, first_v_ref)[kind][...]
            else:
                weight = weight_ref[:, columns]
            product = dot(normed, weight)
            joined_ref[:, columns] = product.astype(BF)
            if kind == 2:
                for block in range(3):
                    at = chunk * WIDE + block * 128
                    values_ref[at : at + 128, :] = product[:, block * 128 : (block + 1) * 128].T
        while done < H and window(done)[0] + window(done)[1] <= (chunk + 1) * WIDE:
            head = done
            done += 1
            base, width, inside = window(head)
            queries = only(inside, joined_ref[:, base : base + width])
            keys_in = joined_ref[:, D + base : D + base + width]
            scores = diagonal(dot(keys_in, queries, NT), patch)
            scores = jnp.where(live > 0.5, scores, -1e30)
            top = jnp.max(scores, axis=0, keepdims=True)
            exponent = jnp.exp2((scores - top) * EXP_SCALE)
            probs = exponent / jnp.sum(exponent, axis=0, keepdims=True)
            probs_ref[head] = probs
            rows = slice(head * E, (head + 1) * E)
            attended = dot(values_ref[rows, :].astype(BF), spread(probs, patch))
            for group in range(4):
                at = group % 2 * HALF + head * 2 * OUT_ROWS + group // 2 * OUT_ROWS
                attended_ref[at : at + OUT_ROWS, :] = attended[group * OUT_ROWS : (group + 1) * OUT_ROWS]
    attended = attended_ref[...].astype(BF)
    own_ref[:D, :] = attended
    right_far_ref[:HALF, :] = attended[:HALF]
    left_far_ref[:HALF, :] = attended[HALF:]
    right_ref[:HALF, :] = attended[HALF:]
    left_ref[:HALF, :] = attended[:HALF]


def attention_grads(heads, joined_ref, probs_ref, head_ref, grad_ref, stride, fresh):
    patch = lane_patch()
    for head in heads:
        base, width, inside = window(head)
        queries = only(inside, joined_ref[:, base : base + width])
        keys_in = joined_ref[:, D + base : D + base + width]
        values = joined_ref[:, 2 * D + base : 2 * D + base + width]
        head_grad = only(inside, head_ref[:, base : base + width])
        probs = probs_ref[head]
        prob_grad = diagonal(dot(values, head_grad, NT), patch)
        inner_sum = jnp.sum(probs * prob_grad, axis=0, keepdims=True)
        score_grad = spread(probs * (prob_grad - inner_sum) * SCALE, patch)
        parts = (
            dot(score_grad, keys_in, TN).astype(BF),
            dot(score_grad, queries).astype(BF),
            dot(spread(probs, patch), head_grad).astype(BF),
        )
        for index, part in enumerate(parts):
            at = index * stride + base
            if fresh and head == heads[0]:
                grad_ref[:, at : at + width] = part
            else:
                grad_ref[:, at : at + width] = jnp.where(inside, part, grad_ref[:, at : at + width])


def early_grad_kernel(masked_ref, joined_ref, probs_ref, w_out_ref, head_ref, early_ref):
    masked = masked_ref[...]
    for chunk in range(3):
        columns = slice(chunk * WIDE, (chunk + 1) * WIDE)
        head_ref[:, columns] = dot(masked, w_out_ref[columns, :], NT).astype(BF)
    attention_grads(range(EARLY_HEADS), joined_ref, probs_ref, head_ref, early_ref, WIDE, True)


def late_grad_kernel(
    joined_ref, probs_ref, head_ref, early_ref, after_ref, also_after_ref, grad_ref
):
    for kind in range(3):
        grad_ref[:, kind * D : kind * D + WIDE] = early_ref[:, kind * WIDE : (kind + 1) * WIDE]
    attention_grads(range(EARLY_HEADS, H), joined_ref, probs_ref, head_ref, grad_ref, D, False)


def token_grad_kernel(tokens_ref, masked_ref, grad_ref, w_qkv_ref, d_tokens_ref):
    masked = masked_ref[...]
    pieces = []
    for chunk in range(3):
        rows = slice(chunk * WIDE, (chunk + 1) * WIDE)
        pieces.append(dot(grad_ref[...], w_qkv_ref[rows, :], NT))
    normed_grad = jnp.concatenate(pieces, axis=1)
    normalized, inverse = row_stats(tokens_ref[...])
    mean_grad = jnp.mean(normed_grad, axis=-1, keepdims=True)
    mean_cross = jnp.mean(normed_grad * normalized, axis=-1, keepdims=True)
    d_tokens_ref[...] = (
        masked.astype(F32) + inverse * (normed_grad - mean_grad - normalized * mean_cross)
    ).astype(BF)


def weight_terms(core, payloads):
    own_ref, left_a_ref, right_a_ref, left_b_ref, right_b_ref, far_a_ref, far_b_ref = payloads
    start = pl.multiple_of(core * HALF, HALF)
    pairs = ((left_a_ref, left_b_ref), (right_b_ref, right_a_ref), (far_a_ref, far_b_ref))
    attended = jnp.concatenate(
        [own_ref[pl.ds(start, HALF), :]]
        + [jnp.where(core == 0, first[:HALF, :], second[:HALF, :]) for first, second in pairs],
        axis=1,
    )
    far = jnp.concatenate([far_a_ref[HALF:, :], far_b_ref[HALF:, :]], axis=0)
    masked = jnp.concatenate(
        [own_ref[D:, :], left_b_ref[HALF:, :], right_b_ref[HALF:, :], far], axis=1
    )
    masked = jnp.concatenate([masked[:256]] + [masked[256:]] * 4, axis=0)
    return dot(attended, masked, NT)


def send_kernel(core_ref, *refs):
    refs[-1][...] = weight_terms(1 - core_ref[0], refs[:7]).astype(BF)


def keep_kernel(core_ref, *refs):
    d_tokens_ref, _, terms_ref, packed_ref, place_ref = refs[7:]
    terms_ref[...] = weight_terms(core_ref[0], refs[:7])
    term = lane_index(3 * 8 * OUT_ROWS)
    kind, inner = term // (8 * OUT_ROWS), term % (8 * OUT_ROWS)
    row = inner % OUT_ROWS
    at = TOKEN_ROWS + kind * OUT_ROWS + jnp.where(kind == 2, row // 4, row)
    place_ref[...] = pick((8 * CHUNK, 3 * 8 * OUT_ROWS), inner // OUT_ROWS * CHUNK + at, 0)
    piece = lane_index(576)
    target = piece % 16 * CHUNK + piece // 64 * PATCHES + piece % 64 // 16
    chooser = pick((16 * CHUNK, 576), target, 0)
    for half in range(2):
        stacked = jnp.concatenate(
            [
                d_tokens_ref[
                    p * SLOTS + half * 16 : p * SLOTS + half * 16 + 16, c * 128 : (c + 1) * 128
                ]
                for c in range(9)
                for p in range(PATCHES)
            ],
            axis=0,
        )
        packed_ref[half * 16 * CHUNK : (half + 1) * 16 * CHUNK, :] = dot(chooser, stacked).astype(BF)


def merge_kernel(rows_ref, keep_ref, got_ref, place_ref, merged_ref):
    terms = keep_ref[...] + got_ref[...].astype(F32)
    row = row_index(SLOTS * OUT_ROWS) % OUT_ROWS
    last = jnp.where(row % 4 == lane_index(128) // 32, terms[:, 256:], 0.0)
    blocks = [block.astype(BF) for block in (terms[:, :128], terms[:, 128:256], last)]
    for group in range(4):
        rows = slice(group * 8 * OUT_ROWS, (group + 1) * 8 * OUT_ROWS)
        stacked = jnp.concatenate([block[rows] for block in blocks], axis=0)
        out = slice(group * 8 * CHUNK, (group + 1) * 8 * CHUNK)
        merged_ref[out, :] = (
            dot(place_ref[...], stacked) + rows_ref[out, :].astype(F32)
        ).astype(BF)


def unpack_kernel(merged_ref, d_tokens_ref, d_w_ref, total_ref):
    piece = row_index(288)
    row = piece % 32
    source = row // PATCHES * CHUNK + piece // 32 * PATCHES + row % PATCHES
    chooser = pick((288, 8 * CHUNK), source, 1)
    for group in range(4):
        rows = dot(chooser, merged_ref[group * 8 * CHUNK : (group + 1) * 8 * CHUNK, :]).astype(BF)
        for block in range(9):
            d_tokens_ref[group * 32 : (group + 1) * 32, block * 128 : (block + 1) * 128] = rows[
                block * 32 : (block + 1) * 32
            ]
    merged = merged_ref[...].astype(F32).reshape(SLOTS, CHUNK, 128)
    total_ref[...] = jnp.sum(merged[:, 32:], axis=0)
    first = TOKEN_ROWS - 32
    d_w_ref[:, :128] = total_ref[first : first + OUT_ROWS, :]
    d_w_ref[:, 128:256] = total_ref[first + OUT_ROWS : first + 2 * OUT_ROWS, :]
    for row in range(OUT_ROWS):
        at = first + 2 * OUT_ROWS + row // 4
        lanes = slice(row % 4 * 32, row % 4 * 32 + 32)
        d_w_ref[row : row + 1, 256:] = total_ref[at : at + 1, lanes]


def body(tokens, d_out, frames, frame_order, w_qkv, w_out):
    place = lax.axis_index("dp")
    core = lax.axis_index("core")
    shape = jax.ShapeDtypeStruct
    live = (frame_order[0] < frames[0]).astype(F32)
    packed = call(
        pack_kernel,
        shape((256, D), BF),
        (tokens[0], d_out[0]),
        scratch=(
            pltpu.VMEM((256, D), BF),
            pltpu.VMEM((256, D), BF),
            pltpu.SemaphoreType.DMA((8,)),
            pltpu.SemaphoreType.DMA((4,)),
        ),
        limit=60,
        far=(0, 1),
        far_out=(0,),
    )
    arrived = lax.all_to_all(
        packed.reshape(SLOTS, 8, D), ("y", "z"), split_axis=0, concat_axis=0, tiled=True
    ).reshape(256, D)
    firsts = tuple(w_qkv[:, kind * D : kind * D + WIDE] for kind in range(3))
    kept, masked, joined, probs, own, right_far, left_far, right, left = call(
        forward_kernel,
        (
            shape((ROWS, D), BF),
            shape((ROWS, D), BF),
            shape((ROWS, 3 * D), BF),
            shape((H, SLOTS, ROWS), F32),
            shape((PAYLOAD, ROWS), BF),
        )
        + (shape((HALF + COLS // 2, ROWS), BF),) * 2
        + (shape((HALF + COLS, ROWS), BF),) * 2,
        (place.reshape(1), core.reshape(1), arrived, live[:, None]) + firsts + (w_qkv,),
        scratch=(
            pltpu.VMEM((D, ROWS), BF),
            pltpu.VMEM((D, ROWS), F32),
            pltpu.VMEM((D, ROWS), F32),
            pltpu.VMEM((D, 3 * D), BF),
            pltpu.SemaphoreType.DMA((6,)),
        ),
        smem=(0, 1),
        far=(7,),
        limit=47,
        flops=int(2e9),
        data=int(14e6),
    )
    up = [(i, (i + 1) % 4) for i in range(4)]
    down = [(i, (i + 3) % 4) for i in range(4)]
    left_a = lax.ppermute(right_far, "dp", up)
    right_a = lax.ppermute(left_far, "dp", down)
    left_b = lax.ppermute(right, "dp", up)
    right_b = lax.ppermute(left, "dp", down)
    head_grads, early = call(
        early_grad_kernel,
        (shape((ROWS, D), BF), shape((ROWS, 3 * WIDE), BF)),
        (masked, joined, probs, w_out),
        limit=16,
        flops=int(2e9),
        data=int(8e6),
    )
    far_a = lax.ppermute(left_a, "dp", up)
    far_b = lax.ppermute(right_a, "dp", down)
    grads = call(
        late_grad_kernel,
        shape((ROWS, 3 * D), BF),
        (joined, probs, head_grads, early, left_a, right_a),
        far=(4, 5),
        limit=16,
        flops=int(3e9),
        data=int(16e6),
    )
    d_rows = call(
        token_grad_kernel,
        shape((ROWS, D), BF),
        (kept, masked, grads, w_qkv),
        limit=24,
        flops=int(3e9),
        data=int(16e6),
    )
    payloads = (core.reshape(1), own, left_a, right_a, left_b, right_b, far_a, far_b)
    send = call(
        send_kernel,
        shape((SLOTS * OUT_ROWS, WIDE), BF),
        payloads + (d_rows,),
        smem=(0,),
        far=(8,),
        flops=int(1e9),
        data=int(4e6),
    )
    got = lax.ppermute(send, "core", [(0, 1), (1, 0)])
    keep, rows, places = call(
        keep_kernel,
        (
            shape((SLOTS * OUT_ROWS, WIDE), F32),
            shape((SLOTS * CHUNK, 128), BF),
            shape((8 * CHUNK, 3 * 8 * OUT_ROWS), BF),
        ),
        payloads + (d_rows, send),
        smem=(0,),
        far=(9,),
        flops=int(1e9),
        data=int(4e6),
    )
    merged = call(
        merge_kernel, shape((SLOTS * CHUNK, 128), BF), (rows, keep, got, places), limit=16
    )
    returned = lax.all_to_all(
        merged.reshape(SLOTS, CHUNK, 128), ("y", "z"), split_axis=0, concat_axis=0, tiled=True
    ).reshape(SLOTS * CHUNK, 128)
    d_tokens, d_w = call(
        unpack_kernel,
        (shape((ROWS, D), BF), shape((OUT_ROWS, COLS), F32)),
        (returned,),
        scratch=(pltpu.VMEM((CHUNK - 32, 128), F32),),
        limit=16,
    )
    return d_tokens[None], d_w


def solution(mesh):
    fine = Mesh(mesh.devices.reshape(4, 4, 8, 2), ("dp", "y", "z", "core"))
    seq = ("y", "z", "core")
    placed = (P("dp", seq, None), P("dp", seq, None), P("dp"), P("dp", None), P(), P())
    return jax.shard_map(
        body,
        mesh=fine,
        in_specs=placed,
        out_specs=(P("dp", seq, None), P(seq, "dp")),
        check_vma=False,
    )
```
